32 devices in a mesh: groups: 2 (over y), space: 4 (over z), test: 4 (over x, core).
Axes of the slice: x: 2, y: 2, z: 4, core: 2. Of those that a mesh axis runs over, the one named last changes fastest.
Arguments:
- log_k: bfloat16 [384, 288, 128], P(('groups', 'space')), parts along dimension 0, may hold values from -1.5 to 1.5
- heads: bfloat16 [4, 384, 288, 128], P('test', ('groups', 'space')), parts along dimension 1, may hold values from -6 to 6
- warm_adjoint: bfloat16 [4, 384, 288, 128], P('test', ('groups', 'space')), parts along dimension 1, may hold values from -6 to 6
- obs_columns: int32 [4, 128], P('test', 'groups'), parts along dimension 1, may hold values from 0 to 55295
- obs_residuals: float32 [4, 128, 128], P('test', 'groups'), parts along dimension 1, may hold values from -18 to 18
- well_columns: int32 [8], P(('groups', 'test')), parts along dimension 0, may hold values from 0 to 55295
Outputs:
- prior_gradient: float32 [384, 288, 128], P(('groups', 'space'), 'test'), parts along dimension 0
The draws below stay inside these ranges and needn't reach their ends.
There are 2 independent parts, one for each index of `groups`. The reference program is written for one: setup_inputs(seed, part) draws one part's arguments, and reference() takes and returns one part's arrays. A program takes and returns all parts, laid end to end along the dimension named above; each array names one. Nothing has to cross between parts.
Inputs may be any that keep to these rules, and one draw needn't show every extreme that they name: `obs_columns`: x * 288 + y of the borehole's cell column. `well_columns`: x * 288 + y of the well's cell column.
All inputs are finite; a program needn't handle non-finite values.
Results may differ from the reference program's by a relative error of at most 0.0003.
Values may be sent and summed in bfloat16 or wider, within the bound.
A program may use at most 128 MiB of HBM per device.

```python
import jax
import jax.numpy as jnp

NX = 192
NY = 288
NZ = 128
OBS = 64
ITERS = 2
TESTS = 4


def plant(array, key, least, largest):
    index_at = [jax.random.randint(jax.random.fold_in(key, axis), (), 0, length) for axis, length in enumerate(array.shape)]
    widest = array.shape.index(max(array.shape))
    neighbour = index_at[:widest] + [(index_at[widest] + 1) % array.shape[widest]] + index_at[widest + 1:]
    return array.at[tuple(index_at)].set(least).at[tuple(neighbour)].set(largest)


def block_scale(key, shape, pieces, least, top_value):
    def one(position, shards_of):
        steps = jax.random.uniform(jax.random.fold_in(jax.random.fold_in(key, 6), position), (shards_of,), jnp.float32, least / len(pieces), top_value / len(pieces))
        return jnp.repeat(jnp.exp(steps), shape[position] // shards_of).reshape((-1,) + (1,) * (len(shape) - position - 1))

    level = one(*pieces[0])
    for cut in pieces[1:]:
        level = level * one(*cut)
    return level


def bell_draw(rng, shape, scale, bound, shards=(), held_as=jnp.bfloat16):
    entries = jax.random.normal(rng, shape, jnp.float32) * scale
    if len(shards) > 0:
        entries = block_scale(rng, shape, shards, -0.22, 0.18) * entries
    return jnp.clip(entries, min=-bound, max=bound).astype(held_as)


def setup_inputs(seed: int = 0, part: int = 0) -> dict:
    key_of = jax.random.split(jax.random.key(seed), 7)
    part_keys = jax.random.split(jax.random.fold_in(key_of[6], part), 7)
    return {
        "log_k": jnp.clip(jax.random.uniform(part_keys[0], (NX, NY, NZ), jnp.float32, -1.5, 1.5) * block_scale(part_keys[0], (NX, NY, NZ), ((0, 4),), -0.4, 0.0), -1.5, 1.5).astype(jnp.bfloat16),
        "heads": bell_draw(part_keys[1], (TESTS, NX, NY, NZ), 1.0, 6.0, ((0, 4), (1, 4))),
        "warm_adjoint": bell_draw(part_keys[2], (TESTS, NX, NY, NZ), 1.0, 6.0, ((0, 4), (1, 4))),
        "obs_columns": plant(jax.random.randint(part_keys[3], (TESTS, OBS), 0, NX * NY), jax.random.fold_in(part_keys[3], 1), 0, (NX * NY) - 1).astype(jnp.int32),
        "obs_residuals": bell_draw(part_keys[4], (TESTS, OBS, NZ), 3.0, 18.0, ((0, 4),), jnp.float32),
        "well_columns": plant(jax.random.randint(part_keys[5], (TESTS,), 0, NX * NY), jax.random.fold_in(part_keys[5], 1), 0, (NX * NY) - 1).astype(jnp.int32),
    }


prior_gain = 5.0
range_squared = 4.0


def neighbours(padded):
    return [padded[2:, 1:-1, 1:-1], padded[:-2, 1:-1, 1:-1], padded[1:-1, 2:, 1:-1],
            padded[1:-1, :-2, 1:-1], padded[1:-1, 1:-1, 2:], padded[1:-1, 1:-1, :-2]]


def operate(values, padded, conduct):
    summed = jnp.zeros_like(values)
    for face_k, beside in zip(conduct, neighbours(padded)):
        summed = summed + face_k * (values - beside)
    return summed


def kappa_of(indices, length):
    return 4.0 * jnp.sin(jnp.pi * indices / length) ** 2


def reference(log_k, heads, warm_adjoint, obs_columns, obs_residuals, well_columns):
    logk_val = log_k.astype(jnp.float32)
    conduct = [jnp.exp(0.5 * (logk_val + beside)) for beside in neighbours(jnp.pad(logk_val, 1))]
    summed = jnp.zeros((NX, NY, NZ), jnp.float32)
    column_ids = jnp.arange(NX * NY, dtype=jnp.int32).reshape(NX, NY)
    for test_id in range(TESTS):
        source = jnp.zeros((NX * NY, NZ), jnp.float32).at[obs_columns[test_id]].add(obs_residuals[test_id])
        source = source.reshape(NX, NY, NZ)
        adjoint = warm_adjoint[test_id].astype(jnp.float32)
        residual = source - operate(adjoint, jnp.pad(adjoint, 1), conduct)
        direction = residual
        norm_now = jnp.sum(residual * residual)
        for iteration in range(ITERS):
            applied = operate(direction, jnp.pad(direction, 1), conduct)
            step_length = norm_now / jnp.sum(direction * applied)
            adjoint = adjoint + step_length * direction
            if iteration + 1 < ITERS:
                residual = residual - step_length * applied
                norm_next = jnp.sum(residual * residual)
                direction = residual + (norm_next / norm_now) * direction
                norm_now = norm_next
        head_val = heads[test_id].astype(jnp.float32)
        misfit_term = jnp.zeros_like(adjoint)
        for face_k, lam_side, head_side in zip(conduct, neighbours(jnp.pad(adjoint, 1)), neighbours(jnp.pad(head_val, 1))):
            misfit_term = misfit_term + face_k * (adjoint - lam_side) * (head_val - head_side)
        keep_mask = (column_ids != well_columns[test_id]).astype(jnp.float32)
        summed = summed + (-0.5 * misfit_term * keep_mask[:, :, None])
    kappa_x = kappa_of(jnp.arange(NX).astype(jnp.float32), NX)
    kappa_y = kappa_of(jnp.arange(NY).astype(jnp.float32), NY)
    kappa_z = kappa_of(jnp.arange(NZ).astype(jnp.float32), NZ)
    spectrum = prior_gain / (1.0 + range_squared * (kappa_x[:, None, None] + kappa_y[None, :, None] + kappa_z[None, None, :])) ** 2
    result = jnp.real(jnp.fft.ifftn(jnp.fft.fftn(summed) * spectrum))
    return result.astype(jnp.float32)
```

```python
import jax
import jax.numpy as jnp
import numpy as np
from jax import lax
from jax.experimental import pallas as pl
from jax.experimental.pallas import tpu as pltpu
from jax.sharding import PartitionSpec as P

ITERS = 2


prior_gain = 5.0
range_squared = 4.0


def with_halo(cells, sides, width):
    for axis, dim in sides:
        count = lax.axis_size(axis)
        ends = count - 1
        head = lax.slice_in_dim(cells, 0, width, axis=dim)
        tail = lax.slice_in_dim(cells, cells.shape[dim] - width, cells.shape[dim], axis=dim)
        cells = jnp.concatenate(
            [
                lax.ppermute(tail, axis, [(i, (i + 1) % count) for i in range(ends)]),
                cells,
                lax.ppermute(head, axis, [((i + 1) % count, i) for i in range(ends)]),
            ],
            axis=dim,
        )
    return cells


def neighbours(padded):
    return [
        padded[2:, 1:-1, 1:-1],
        padded[:-2, 1:-1, 1:-1],
        padded[1:-1, 2:, 1:-1],
        padded[1:-1, :-2, 1:-1],
        padded[1:-1, 1:-1, 2:],
        padded[1:-1, 1:-1, :-2],
    ]


def operate(values, padded, conduct):
    summed = jnp.zeros_like(values)
    for face_k, beside in zip(conduct, neighbours(padded)):
        summed = summed + face_k * (values - beside)
    return summed


def kappa_of(indices, length):
    return 4.0 * jnp.sin(jnp.pi * indices / length) ** 2


def pad_sides(padded):
    return jnp.pad(padded, ((0, 0), (1, 1), (1, 1)))


def with_faces(values):
    return pad_sides(with_halo(values, (("space", 0),), 1))


def squares(residual):
    return lax.psum(jnp.sum(residual * residual), "space")


def hartley(length):
    indices = jnp.arange(length, dtype=jnp.int32)
    products = indices[:, None] * indices[None, :] % length
    angles = products.astype(jnp.float32) * (2.0 * jnp.pi / length)
    return jnp.cos(angles) + jnp.sin(angles)


def on_device(log_k, heads, warm_adjoint, obs_columns, obs_residuals, well_columns):
    slab_rows, width_cells, depth_cells = log_k.shape
    space_count = lax.axis_size("space")
    first_row = lax.axis_index("space") * slab_rows
    logk_pad, head_pad = (
        with_halo(log_k, (("space", 0),), 1),
        with_halo(heads[0], (("space", 0),), 1),
    )
    logk_val = log_k.astype(jnp.float32)
    conduct = [
        jnp.exp(0.5 * (logk_val + beside))
        for beside in neighbours(pad_sides(logk_pad.astype(jnp.float32)))
    ]
    columns = obs_columns[0]
    row_local = columns // width_cells - first_row
    inside = (row_local >= 0) & (row_local < slab_rows)
    row_local = jnp.where(inside, row_local, slab_rows)
    source = jnp.zeros((slab_rows, width_cells, depth_cells), jnp.float32)
    source = source.at[row_local, columns % width_cells].add(obs_residuals[0], mode="drop")
    adjoint = warm_adjoint[0].astype(jnp.float32)
    lam_padded = with_faces(adjoint)
    residual = source - operate(adjoint, lam_padded, conduct)
    direction = residual
    norm_now = squares(residual)
    for iteration in range(ITERS):
        dir_padded = with_faces(direction)
        applied = operate(direction, dir_padded, conduct)
        step_length = norm_now / lax.psum(jnp.sum(direction * applied), "space")
        adjoint = adjoint + step_length * direction
        lam_padded = lam_padded + step_length * dir_padded
        if iteration + 1 < ITERS:
            residual = residual - step_length * applied
            norm_next = squares(residual)
            direction = residual + norm_next / norm_now * direction
            norm_now = norm_next
    lam_full = pad_sides(with_halo(adjoint, (("space", 0),), 1))
    head_val = heads[0].astype(jnp.float32)
    misfit_term = jnp.zeros_like(adjoint)
    for face_k, lam_side, head_side in zip(
        conduct, neighbours(lam_full), neighbours(pad_sides(head_pad.astype(jnp.float32)))
    ):
        misfit_term = misfit_term + face_k * (adjoint - lam_side) * (head_val - head_side)
    column_ids = (first_row + jnp.arange(slab_rows, dtype=jnp.int32))[
        :, None
    ] * width_cells + jnp.arange(width_cells, dtype=jnp.int32)[None, :]
    keep_mask = (column_ids != well_columns[0]).astype(jnp.float32)
    partial_value = -0.5 * misfit_term * keep_mask[:, :, None]
    highest = lax.Precision.HIGHEST
    cas_depth = hartley(depth_cells)
    cas_across = hartley(width_cells)
    along_cells = slab_rows * space_count
    cas_along = hartley(along_cells)
    summed = lax.psum_scatter(partial_value, "test", scatter_dimension=1, tiled=True)
    depth_freq = jnp.einsum("xyz,zk->xky", summed, cas_depth, precision=highest)
    pencil = lax.all_to_all(depth_freq, "test", split_axis=1, concat_axis=2, tiled=True)
    across_freq = jnp.einsum("xzy,yk->kzx", pencil, cas_across, precision=highest)
    column_block = lax.all_to_all(across_freq, "space", split_axis=0, concat_axis=2, tiled=True)
    along_freq = jnp.einsum("yzx,xk->yzk", column_block, cas_along, precision=highest)
    across_rows = column_block.shape[0]
    depth_rows = column_block.shape[1]
    kappa_x = kappa_of(jnp.arange(along_cells).astype(jnp.float32), along_cells)
    kappa_y = kappa_of(
        (lax.axis_index("space") * across_rows + jnp.arange(across_rows)).astype(jnp.float32),
        width_cells,
    )
    kappa_z = kappa_of(
        (lax.axis_index("test") * depth_rows + jnp.arange(depth_rows)).astype(jnp.float32),
        depth_cells,
    )
    spectrum = (
        prior_gain
        / (
            1.0
            + range_squared
            * (kappa_y[:, None, None] + kappa_z[None, :, None] + kappa_x[None, None, :])
        )
        ** 2
    )
    along_back = jnp.einsum("yzk,kx->yzx", along_freq * spectrum, cas_along, precision=highest)
    slab_block = lax.all_to_all(along_back, "space", split_axis=2, concat_axis=0, tiled=True)
    across_back = jnp.einsum("yzx,yk->xzk", slab_block, cas_across, precision=highest)
    depth_block = lax.all_to_all(across_back, "test", split_axis=2, concat_axis=1, tiled=True)
    result = jnp.einsum("xky,kz->xyz", depth_block, cas_depth, precision=highest)
    scale_back = 1.0 / (along_cells * width_cells * depth_cells)
    return result * scale_back


GUARD = 8
STEP = 256.0
TOP = 32000.0
BF = jnp.bfloat16
F32 = jnp.float32
VM = pl.BlockSpec(memory_space=pltpu.VMEM)
SM = pl.BlockSpec(memory_space=pltpu.SMEM)
ANY = pl.BlockSpec(memory_space=pl.ANY)
MESH = pl.DeviceIdType.MESH


def shape(*dims, dtype=jnp.float32):
    return jax.ShapeDtypeStruct(dims, dtype)


def iota(plane, axis):
    return lax.broadcasted_iota(jnp.int32, plane, axis)


def halves(values):
    top = values.astype(BF)
    return top, (values - top.astype(F32)).astype(BF)


def matmul(a, b):
    return jnp.dot(a, b, preferred_element_type=F32)


def dot3(a, b):
    a_top, a_low = halves(a)
    b_top, b_low = halves(b)
    return matmul(a_top, b_top) + (matmul(a_top, b_low) + matmul(a_low, b_top))


def encode(values, spare):
    rows, lanes = values.shape
    peak = jnp.maximum(jnp.max(jnp.abs(values), axis=0, keepdims=True), 1e-30)
    level = jnp.ceil(jnp.log2(peak) * STEP)
    scaled = jnp.round(values * (jnp.exp2(level * (-1.0 / STEP)) * TOP))
    both = jnp.concatenate([scaled, jnp.broadcast_to(level, (spare, lanes))], axis=0)
    return both.astype(jnp.int32).astype(jnp.int16)


def decode(codes, spare):
    wide = codes.astype(jnp.int32).astype(F32)
    rows = wide.shape[0] - spare
    level = wide[rows : rows + 1]
    return wide[:rows] * (jnp.exp2(level * (1.0 / STEP)) * (1.0 / TOP))


def swap_blocks(planes):
    count = len(planes)
    lanes = planes[0].shape[1]
    block = lanes // count
    at_lane = iota(planes[0].shape, 1) // block
    swapped = []
    for to in range(count):
        joined = planes[to]
        for frm in range(count):
            if frm != to:
                shift = (block * (frm - to)) % lanes
                joined = jnp.where(at_lane == frm, pltpu.roll(planes[frm], shift, 1), joined)
        swapped.append(joined)
    return swapped


def greet(others):
    barrier = pltpu.get_barrier_semaphore()
    for other in others:
        pl.semaphore_signal(barrier, inc=1, device_id=other, device_id_type=MESH)
    pl.semaphore_wait(barrier, len(others))


def gradient_kernel(
    well,
    columns,
    observed,
    logk,
    warm,
    heads,
    turned,
    out,
    lk,
    wm,
    hd,
    soft,
    res,
    img,
    ring,
    sources,
    acc,
    shared,
    mine,
    from_mate,
    ship,
    got,
    load_sem,
    halo_send,
    halo_take,
    send_sum,
    take_sum,
    send_mate,
    take_mate,
    send_across,
    take_across,
):
    rows, width, depth = logk.shape
    parts = 4
    chunk = rows // parts
    piece = width // 3
    pieces = range(3)
    slabs = shared.shape[0]
    slab, here = lax.axis_index("space"), lax.axis_index("test")
    half, core = here // 2, lax.rem(here, 2)
    mate = {"test": 2 * half + 1 - core}
    across = {"test": 2 * (1 - half) + core}
    others = [{"space": lax.rem(slab + k, slabs)} for k in range(1, slabs)]
    first_row = slab * rows

    def loads(m):
        span = pl.ds(m * chunk, chunk)
        to = pl.ds(3 + m * chunk, chunk)
        return [
            pltpu.make_async_copy(frm.at[span], held.at[to], load_sem.at[n, m])
            for n, (frm, held) in enumerate(((logk, lk), (warm, wm), (heads, hd)))
        ]

    for m in range(parts):
        for copy in loads(m):
            copy.start()

    def halo(direction):
        up = direction == 1
        copies = []
        for n, (frm, held, deep) in enumerate(((logk, lk, 3), (warm, wm, 3), (heads, hd, 1))):
            at = rows - deep if up else 0
            to = 3 - deep if up else 3 + rows
            copies.append(
                pltpu.make_async_remote_copy(
                    src_ref=frm.at[pl.ds(at, deep)],
                    dst_ref=held.at[pl.ds(to, deep)],
                    send_sem=halo_send.at[direction, n],
                    recv_sem=halo_take.at[direction, n],
                    device_id={"space": slab + 1 if up else slab - 1},
                    device_id_type=MESH,
                )
            )
        return copies

    greet(others + [mate, across])

    @pl.when(slab > 0)
    def _():
        for copy in halo(0):
            copy.start()

    @pl.when(slab < slabs - 1)
    def _():
        for copy in halo(1):
            copy.start()

    blank = jnp.zeros((3, width, depth), BF)

    @pl.when(slab == 0)
    def _():
        lk[0:3] = blank
        wm[0:3] = blank
        hd[0:3] = blank

    @pl.when(slab == slabs - 1)
    def _():
        lk[rows + 3 : rows + 6] = blank
        wm[rows + 3 : rows + 6] = blank
        hd[rows + 3 : rows + 6] = blank

    top, low = halves(observed[...])
    sources[...] = jnp.concatenate([top, low], axis=0)
    acc[...] = jnp.zeros_like(acc)
    edge = jnp.zeros((GUARD, depth), F32)
    for i in range(ring.shape[0]):
        ring[i, 0:GUARD, :] = edge
        ring[i, width + GUARD : width + 2 * GUARD, :] = edge

    at_lane = iota((piece, depth), 1)
    at_row = iota((piece, depth), 0)
    is_first, is_last = at_lane == 0, at_lane == depth - 1
    spots = iota((piece, columns.shape[1]), 0)

    def at(c):
        return pl.ds(c * piece, piece)

    def near(ref, i, c, off=0):
        return ref[i, pl.ds(GUARD + c * piece + off, piece), :]

    def store(ref, i, c, value):
        ref[i, pl.ds(GUARD + c * piece, piece), :] = value

    def ahead(value):
        return pltpu.roll(value, depth - 1, 1)

    def behind(value):
        return pltpu.roll(value, 1, 1)

    def beside(ref, below, i, above, c, outer):
        held = near(ref, i, c)
        lanes = jnp.where(is_last, outer, ahead(held)) + jnp.where(is_first, outer, behind(held))
        ends = near(ref, i, c, -1) + near(ref, i, c, 1)
        return held, (lanes + ends) + (near(ref, below, c) + near(ref, above, c))

    def partial(value):
        return jnp.sum(value.reshape(piece // 8, 8, depth), axis=0)

    def slot(n, base):
        return base + lax.rem(n, 4)

    def outside(n):
        return jnp.logical_or(
            jnp.logical_and(slab == 0, n < 3), jnp.logical_and(slab == slabs - 1, n >= rows + 3)
        )

    def prepare(n):
        one = jnp.ones((GUARD, depth), F32)
        soft[n, 0:GUARD, :] = one
        soft[n, width + GUARD : width + 2 * GUARD, :] = one
        for c in pieces:
            value = jnp.exp(0.5 * lk[n, at(c), :].astype(F32))
            store(soft, n, c, value)
            store(ring, slot(n, 0), c, value * wm[n, at(c), :].astype(F32))

    def residual(n):
        spot = columns[...] - (first_row + n - 3) * width
        for c in pieces:
            s, around = beside(soft, n - 1, n, n + 1, c, 1.0)
            held, total = beside(ring, slot(n - 1, 0), slot(n, 0), slot(n + 1, 0), c, 0.0)
            hits = jnp.where(spots == spot - c * piece, 1.0, 0.0).astype(BF)
            value = (s * total - held * around) + matmul(hits, sources[...])
            res[n, at(c), :] = value
            store(ring, slot(n, 4), c, s * value)
            store(ring, slot(n, 12), c, around)

        @pl.when(outside(n))
        def _():
            for c in pieces:
                res[n, at(c), :] = jnp.zeros((piece, depth), F32)
                store(ring, slot(n, 4), c, jnp.zeros((piece, depth), F32))

    def image(n, own):
        for c in pieces:
            held, total = beside(ring, slot(n - 1, 4), slot(n, 4), slot(n + 1, 4), c, 0.0)
            s, value = near(soft, n, c), res[n, at(c), :]
            applied = held * near(ring, slot(n, 12), c) - s * total
            img[n, at(c), :] = applied
            store(ring, slot(n, 8), c, s * applied)
            acc[0] += own * partial(value * value)
            acc[1] += own * partial(value * applied)

        @pl.when(outside(n))
        def _():
            for c in pieces:
                img[n, at(c), :] = jnp.zeros((piece, depth), F32)
                store(ring, slot(n, 8), c, jnp.zeros((piece, depth), F32))

    def twice(n):
        for c in pieces:
            held, total = beside(ring, slot(n - 1, 8), slot(n, 8), slot(n + 1, 8), c, 0.0)
            value = img[n, at(c), :]
            acc[2] += partial(value * value)
            acc[3] += partial(held * (value * near(ring, slot(n, 12), c) - total))

    def sweep(first, last, least, most):
        def step(k, _):
            if first == 3:

                @pl.when(jnp.logical_and(lax.rem(k - 3, chunk) == 0, k < rows + 3))
                def _():
                    for copy in loads((k - 3) // chunk):
                        copy.wait()

                @pl.when(jnp.logical_and(k == rows + 3, slab < slabs - 1))
                def _():
                    for copy in halo(0):
                        copy.wait_recv()

            prepare(k)

            @pl.when(k >= first + 2)
            def _():
                residual(k - 1)

            @pl.when(k >= first + 4)
            def _():
                own = jnp.logical_and(k - 2 >= least, k - 2 <= most)
                image(k - 2, own.astype(F32))

            @pl.when(k >= first + 6)
            def _():
                twice(k - 3)

            return 0

        lax.fori_loop(first, last + 1, step, 0)

    sweep(3, rows + 5, 5, rows + 2)

    @pl.when(slab > 0)
    def _():
        for copy in halo(1):
            copy.wait_recv()

    sweep(0, 8, 3, 4)

    shared[slab] = acc[...]
    copies = [
        pltpu.make_async_remote_copy(
            src_ref=shared.at[slab],
            dst_ref=shared.at[slab],
            send_sem=send_sum.at[k],
            recv_sem=take_sum.at[k],
            device_id=other,
            device_id_type=MESH,
        )
        for k, other in enumerate(others)
    ]
    for copy in copies:
        copy.start()

    @pl.when(slab > 0)
    def _():
        for copy in halo(0):
            copy.wait_send()

    @pl.when(slab < slabs - 1)
    def _():
        for copy in halo(1):
            copy.wait_send()

    for copy in copies:
        copy.wait()

    def gathered(n):
        total = shared[0, n]
        for m in range(1, slabs):
            total = total + shared[m, n]
        return jnp.broadcast_to(jnp.sum(total, axis=(0, 1), keepdims=True), (1, depth))

    norm, curve, square, bend = [gathered(n) for n in range(4)]
    length = norm / curve
    norm_next = length * length * square - norm
    curve_next = curve - 2.0 * length * square + length * length * bend
    ratio = norm_next / norm
    length_next = norm_next / (curve_next - ratio * norm_next / length)
    with_start = length + length_next * (1.0 + ratio)
    with_image = length_next * length

    def eighth(n, base):
        return base + lax.rem(n, 8)

    def fill(n):
        for c in pieces:
            field = wm[n, at(c), :].astype(F32)
            field = field + (with_start * res[n, at(c), :] - with_image * img[n, at(c), :])
            store(ring, eighth(n, 0), c, field)
            store(ring, eighth(n, 8), c, hd[n, at(c), :].astype(F32))

    fill(2)
    fill(3)
    count = 4
    groups = rows // count
    at_block = at_lane // (depth // count)

    def group(g):
        start = 3 + count * g
        for p in range(count):
            fill(start + p + 1)
        for c in pieces:
            fields = [near(ring, eighth(start + p, 0), c) for p in range(-1, count + 1)]
            levels = [near(ring, eighth(start + p, 8), c) for p in range(-1, count + 1)]
            steps = [
                (fields[p] - fields[p + 1]) * (levels[p] - levels[p + 1]) for p in range(count + 1)
            ]
            turns = []
            for p in range(count):
                n = start + p
                f, h, s = fields[p + 1], levels[p + 1], near(soft, n, c)
                total = near(soft, n - 1, c) * steps[p] + near(soft, n + 1, c) * steps[p + 1]
                for off in (-1, 1):
                    field = near(ring, eighth(n, 0), c, off)
                    level = near(ring, eighth(n, 8), c, off)
                    total += near(soft, n, c, off) * ((f - field) * (h - level))
                both = f * h
                product = (f - ahead(f)) * (h - ahead(h))
                total += jnp.where(is_last, both, ahead(s) * product)
                total += jnp.where(is_first, both, behind(s * product))
                place = well[0] - (first_row + n - 3) * width - c * piece
                value = jnp.where(at_row != place, s * total, 0.0)
                double = matmul(jnp.concatenate(halves(value), axis=1), turned[p])
                turns.append(double[:, :depth] + double[:, depth:])
            for t in range(count):
                joined = turns[-t % count]
                for b in range(1, count):
                    joined = jnp.where(at_block == b, turns[(b - t) % count], joined)
                mine[t % 2, g, t // 2, at(c), :] = joined
        to_mate(g).start()

    def to_mate(g):
        return pltpu.make_async_remote_copy(
            src_ref=mine.at[1 - core, g],
            dst_ref=from_mate.at[g],
            send_sem=send_mate.at[g],
            recv_sem=take_mate.at[g],
            device_id=mate,
            device_id_type=MESH,
        )

    def to_across(g):
        return pltpu.make_async_remote_copy(
            src_ref=ship.at[g],
            dst_ref=got.at[g],
            send_sem=send_across.at[g],
            recv_sem=take_across.at[g],
            device_id=across,
            device_id_type=MESH,
        )

    def relay(g):
        to_mate(g).wait_recv()
        ship[g] = encode(mine[core, g, 1 - half] + from_mate[g, 1 - half], 16)
        to_across(g).start()

    group(0)

    def step(g, _):
        group(g)
        relay(g - 1)
        return 0

    lax.fori_loop(1, groups, step, 0)
    relay(groups - 1)

    def finish(g, _):
        to_across(g).wait_recv()
        out[g] = (mine[core, g, half] + from_mate[g, half]) + decode(got[g], 16)
        to_mate(g).wait_send()
        to_across(g).wait_send()
        return 0

    lax.fori_loop(0, groups, finish, 0)


def spectral_kernel(
    summed,
    listed,
    cas_across,
    cas_depth,
    out,
    tables,
    freq,
    moments,
    filtered,
    going,
    coming,
    load_sem,
    send_end,
    take_end,
    send_back,
    take_back,
):
    groups, width, lanes = summed.shape
    count, part = going.shape[0], width // going.shape[0]
    spare = going.shape[2] - part
    rows = groups * count
    slabs = moments.shape[0]
    slab, here = lax.axis_index("space"), lax.axis_index("test")
    others = [{"space": lax.rem(slab + k, slabs)} for k in range(1, slabs)]
    peers = [lax.rem(here + k, count) for k in range(1, count)]
    fetch = pltpu.make_async_copy(listed.at[here], tables, load_sem)
    fetch.start()
    greet(others + [{"test": peer} for peer in peers])
    turn = lax.rem((count - here) * (lanes // count), lanes)

    def mix(g, _):
        top, low = halves(pltpu.roll(summed[g], turn, 1))
        mixed = matmul(cas_across[...], jnp.concatenate([top, top, low], axis=0))
        blocks = [mixed[j * part : (j + 1) * part] for j in range(count)]
        for p, plane in enumerate(swap_blocks(blocks)):
            freq[g * count + p] = plane
        return 0

    lax.fori_loop(0, groups, mix, 0)
    fetch.wait()
    pole, level, slope, decay, wrap_one, wrap_two = (tables[n] for n in range(6))

    def walk(i, carry):
        one, two, back_one, back_two = carry
        value, back = freq[i], freq[rows - 1 - i]
        return (
            value + pole * one,
            pole * (two + one),
            back + pole * back_one,
            pole * (back_two + back_one),
        )

    zero = jnp.zeros((part, lanes), jnp.float32)
    ends = lax.fori_loop(0, rows, walk, (zero, zero, zero, zero))
    for n in range(4):
        moments[slab, n] = encode(ends[n], spare)
    copies = [
        pltpu.make_async_remote_copy(
            src_ref=moments.at[slab],
            dst_ref=moments.at[slab],
            send_sem=send_end.at[k],
            recv_sem=take_end.at[k],
            device_id=other,
            device_id_type=MESH,
        )
        for k, other in enumerate(others)
    ]
    for copy in copies:
        copy.start()
    for copy in copies:
        copy.wait()

    def carried(direction, n):
        one, two = zero, zero
        for m in range(slabs, 0, -1):
            other = lax.rem(slab + 2 * slabs - direction * m, slabs)
            one, two = (
                decay * one + decode(moments[other, n], spare),
                decay * (two + rows * one) + decode(moments[other, n + 1], spare),
            )
        return wrap_one * one, wrap_one * two + wrap_two * one

    def forward(i, carry):
        one, two = carry
        two = pole * (two + one)
        one = freq[i] + pole * one
        filtered[i] = level * one + slope * two
        return one, two

    lax.fori_loop(0, rows, forward, carried(1, 0))

    def backward(i, carry):
        one, two = carry
        at = rows - 1 - i
        two = pole * (two + one)
        one = pole * one
        filtered[at] += level * one + slope * two
        return one + freq[at], two

    lax.fori_loop(0, rows, backward, carried(-1, 2))

    def to_peer(k, g):
        return pltpu.make_async_remote_copy(
            src_ref=going.at[peers[k], g],
            dst_ref=coming.at[here, g],
            send_sem=send_back.at[k, g],
            recv_sem=take_back.at[k, g],
            device_id={"test": peers[k]},
            device_id_type=MESH,
        )

    def unmix(g, _):
        blocks = swap_blocks([filtered[g * count + p] for p in range(count)])
        top, low = halves(jnp.concatenate(blocks, axis=0))
        mixed = matmul(cas_across[...], jnp.concatenate([top, top, low], axis=0))
        for u in range(count):
            going[u, g] = encode(mixed[u * part : (u + 1) * part], spare)
        for k in range(count - 1):
            to_peer(k, g).start()
        coming[here, g] = going[here, g]
        return 0

    lax.fori_loop(0, groups, unmix, 0)

    def back(g, _):
        for k in range(count - 1):
            to_peer(k, g).wait()
        planes = [decode(coming[t, g], spare) for t in range(count)]
        for p, plane in enumerate(swap_blocks(planes)):
            out[g * count + p] = dot3(plane, cas_depth[...])
        return 0

    lax.fori_loop(0, groups, back, 0)


def table(length):
    indices = np.arange(length)
    angles = (indices[:, None] * indices[None, :] % length) * (2.0 * np.pi / length)
    return (np.cos(angles) + np.sin(angles)).astype(np.float32)


def split(values):
    top = values.astype(jnp.bfloat16)
    return top, (values - top.astype(np.float32)).astype(jnp.bfloat16)


def turned_tables(length, count):
    tables = []
    for p in range(count):
        top, low = split(-0.5 * np.roll(table(length), p * (length // count), axis=1))
        tables.append(np.block([[top, low], [top, np.zeros_like(low)]]))
    return np.stack(tables)


def filter_tables(rows, along, width, depth, count):
    def kappa(length):
        return 4.0 * np.sin(np.pi * np.arange(length) / length) ** 2

    part, block = width // count, depth // count
    lanes_at = np.arange(depth)
    across_at = (lanes_at // block)[None, :] * part + np.arange(part)[:, None]
    listed = []
    for here in range(count):
        depth_at = here * block + lanes_at % block
        shift = 1.0 + range_squared * (kappa(width)[across_at] + kappa(depth)[depth_at][None, :])
        centre = 1.0 + shift / (2.0 * range_squared)
        pole = 1.0 / (centre + np.sqrt(centre * centre - 1.0))
        square = pole * pole
        gain = prior_gain / (range_squared * range_squared) * square / (width * depth)
        slope = gain / (1.0 - square) ** 2
        level = slope * (1.0 + square) / (1.0 - square)
        turn = pole**along
        wrap_one = 1.0 / (1.0 - turn)
        wrap_two = along * turn * wrap_one * wrap_one
        listed.append(np.stack([pole, level, slope, pole**rows, wrap_one, wrap_two]))
    return np.stack(listed).astype(np.float32)


def fast(log_k, heads, warm_adjoint, obs_columns, obs_residuals, well_columns):
    rows, width, depth = log_k.shape
    slabs = lax.axis_size("space")
    count = lax.axis_size("test")
    part = width // count
    groups = rows // count
    observed = obs_columns.shape[1]
    planes = rows + 6
    padded = width + 2 * GUARD
    spare = 16 - part % 16
    summed = pl.pallas_call(
        gradient_kernel,
        out_shape=shape(groups, width, depth),
        in_specs=[SM, VM, VM, ANY, ANY, ANY, VM],
        out_specs=VM,
        scratch_shapes=[pltpu.VMEM((planes, width, depth), BF)] * 3
        + [
            pltpu.VMEM((planes, padded, depth), F32),
            pltpu.VMEM((planes, width, depth), F32),
            pltpu.VMEM((planes, width, depth), F32),
            pltpu.VMEM((16, padded, depth), F32),
            pltpu.VMEM((2 * observed, depth), BF),
            pltpu.VMEM((4, 8, depth), F32),
            pltpu.VMEM((slabs, 4, 8, depth), F32),
            pltpu.VMEM((2, groups, 2, width, depth), F32),
            pltpu.VMEM((groups, 2, width, depth), F32),
            pltpu.VMEM((groups, width + 16, depth), jnp.int16),
            pltpu.VMEM((groups, width + 16, depth), jnp.int16),
            pltpu.SemaphoreType.DMA((3, 4)),
        ]
        + [pltpu.SemaphoreType.DMA((2, 3))] * 2
        + [pltpu.SemaphoreType.DMA((slabs - 1,))] * 2
        + [pltpu.SemaphoreType.DMA((groups,))] * 4,
        compiler_params=pltpu.CompilerParams(
            vmem_limit_bytes=60 * 1024 * 1024, collective_id=1, has_side_effects=True
        ),
        name="gradient",
    )(
        well_columns,
        jnp.concatenate([obs_columns, obs_columns], axis=1),
        obs_residuals[0],
        log_k,
        warm_adjoint[0],
        heads[0],
        jnp.asarray(turned_tables(depth, count)),
    )
    top, low = split(table(width))
    return pl.pallas_call(
        spectral_kernel,
        out_shape=shape(rows, part, depth),
        in_specs=[VM, ANY, VM, VM],
        out_specs=VM,
        scratch_shapes=[
            pltpu.VMEM((6, part, depth), F32),
            pltpu.VMEM((rows, part, depth), F32),
            pltpu.VMEM((slabs, 4, part + spare, depth), jnp.int16),
            pltpu.VMEM((rows, part, depth), F32),
            pltpu.VMEM((count, groups, part + spare, depth), jnp.int16),
            pltpu.VMEM((count, groups, part + spare, depth), jnp.int16),
            pltpu.SemaphoreType.DMA,
            pltpu.SemaphoreType.DMA((slabs - 1,)),
            pltpu.SemaphoreType.DMA((slabs - 1,)),
            pltpu.SemaphoreType.DMA((count - 1, groups)),
            pltpu.SemaphoreType.DMA((count - 1, groups)),
        ],
        compiler_params=pltpu.CompilerParams(
            vmem_limit_bytes=40 * 1024 * 1024, collective_id=2, has_side_effects=True
        ),
        name="spectral",
    )(
        summed,
        jnp.asarray(filter_tables(rows, rows * slabs, width, depth, count)),
        jnp.asarray(np.concatenate([top, low, top], axis=1)),
        jnp.asarray(table(depth)),
    )


def pick(log_k, heads, warm_adjoint, obs_columns, *rest):
    rows, width, depth = log_k.shape
    count = lax.axis_size("test")
    fits = depth == 128 and count == 4 and rows % 4 == 0 and rows >= 12 and width % 96 == 0
    fits = fits and obs_columns.shape[1] % 64 == 0 and rows * width <= 48 * 288
    run = fast if fits and lax.axis_size("space") > 1 else on_device
    return run(log_k, heads, warm_adjoint, obs_columns, *rest)


def solution(mesh):
    placed = (
        P(("groups", "space"), None, None),
        P("test", ("groups", "space"), None, None),
        P("test", ("groups", "space"), None, None),
        P("test", "groups"),
        P("test", "groups", None),
        P(("groups", "test")),
    )
    return jax.shard_map(
        pick,
        mesh=mesh,
        in_specs=placed,
        out_specs=P(("groups", "space"), "test", None),
        check_vma=False,
    )
```

```python
import jax
import jax.numpy as jnp
import numpy as np
from jax import lax
from jax.experimental import pallas as pl
from jax.experimental.pallas import tpu as pltpu
from jax.sharding import PartitionSpec as P

ITERS = 2


prior_gain = 5.0
range_squared = 4.0


def with_halo(cells, sides, width):
    for axis, dim in sides:
        count = lax.axis_size(axis)
        ends = count - 1
        head = lax.slice_in_dim(cells, 0, width, axis=dim)
        tail = lax.slice_in_dim(cells, cells.shape[dim] - width, cells.shape[dim], axis=dim)
        cells = jnp.concatenate(
            [
                lax.ppermute(tail, axis, [(i, (i + 1) % count) for i in range(ends)]),
                cells,
                lax.ppermute(head, axis, [((i + 1) % count, i) for i in range(ends)]),
            ],
            axis=dim,
        )
    return cells


def neighbours(padded):
    return [
        padded[2:, 1:-1, 1:-1],
        padded[:-2, 1:-1, 1:-1],
        padded[1:-1, 2:, 1:-1],
        padded[1:-1, :-2, 1:-1],
        padded[1:-1, 1:-1, 2:],
        padded[1:-1, 1:-1, :-2],
    ]


def operate(values, padded, conduct):
    summed = jnp.zeros_like(values)
    for face_k, beside in zip(conduct, neighbours(padded)):
        summed = summed + face_k * (values - beside)
    return summed


def kappa_of(indices, length):
    return 4.0 * jnp.sin(jnp.pi * indices / length) ** 2


def pad_sides(padded):
    return jnp.pad(padded, ((0, 0), (1, 1), (1, 1)))


def with_faces(values):
    return pad_sides(with_halo(values, (("space", 0),), 1))


def squares(residual):
    return lax.psum(jnp.sum(residual * residual), "space")


def hartley(length):
    indices = jnp.arange(length, dtype=jnp.int32)
    products = indices[:, None] * indices[None, :] % length
    angles = products.astype(jnp.float32) * (2.0 * jnp.pi / length)
    return jnp.cos(angles) + jnp.sin(angles)


def on_device(log_k, heads, warm_adjoint, obs_columns, obs_residuals, well_columns):
    slab_rows, width_cells, depth_cells = log_k.shape
    space_count = lax.axis_size("space")
    first_row = lax.axis_index("space") * slab_rows
    logk_pad, head_pad = (
        with_halo(log_k, (("space", 0),), 1),
        with_halo(heads[0], (("space", 0),), 1),
    )
    logk_val = log_k.astype(jnp.float32)
    conduct = [
        jnp.exp(0.5 * (logk_val + beside))
        for beside in neighbours(pad_sides(logk_pad.astype(jnp.float32)))
    ]
    columns = obs_columns[0]
    row_local = columns // width_cells - first_row
    inside = (row_local >= 0) & (row_local < slab_rows)
    row_local = jnp.where(inside, row_local, slab_rows)
    source = jnp.zeros((slab_rows, width_cells, depth_cells), jnp.float32)
    source = source.at[row_local, columns % width_cells].add(obs_residuals[0], mode="drop")
    adjoint = warm_adjoint[0].astype(jnp.float32)
    lam_padded = with_faces(adjoint)
    residual = source - operate(adjoint, lam_padded, conduct)
    direction = residual
    norm_now = squares(residual)
    for iteration in range(ITERS):
        dir_padded = with_faces(direction)
        applied = operate(direction, dir_padded, conduct)
        step_length = norm_now / lax.psum(jnp.sum(direction * applied), "space")
        adjoint = adjoint + step_length * direction
        lam_padded = lam_padded + step_length * dir_padded
        if iteration + 1 < ITERS:
            residual = residual - step_length * applied
            norm_next = squares(residual)
            direction = residual + norm_next / norm_now * direction
            norm_now = norm_next
    lam_full = pad_sides(with_halo(adjoint, (("space", 0),), 1))
    head_val = heads[0].astype(jnp.float32)
    misfit_term = jnp.zeros_like(adjoint)
    for face_k, lam_side, head_side in zip(
        conduct, neighbours(lam_full), neighbours(pad_sides(head_pad.astype(jnp.float32)))
    ):
        misfit_term = misfit_term + face_k * (adjoint - lam_side) * (head_val - head_side)
    column_ids = (first_row + jnp.arange(slab_rows, dtype=jnp.int32))[
        :, None
    ] * width_cells + jnp.arange(width_cells, dtype=jnp.int32)[None, :]
    keep_mask = (column_ids != well_columns[0]).astype(jnp.float32)
    partial_value = -0.5 * misfit_term * keep_mask[:, :, None]
    highest = lax.Precision.HIGHEST
    cas_depth = hartley(depth_cells)
    cas_across = hartley(width_cells)
    along_cells = slab_rows * space_count
    cas_along = hartley(along_cells)
    summed = lax.psum_scatter(partial_value, "test", scatter_dimension=1, tiled=True)
    depth_freq = jnp.einsum("xyz,zk->xky", summed, cas_depth, precision=highest)
    pencil = lax.all_to_all(depth_freq, "test", split_axis=1, concat_axis=2, tiled=True)
    across_freq = jnp.einsum("xzy,yk->kzx", pencil, cas_across, precision=highest)
    column_block = lax.all_to_all(across_freq, "space", split_axis=0, concat_axis=2, tiled=True)
    along_freq = jnp.einsum("yzx,xk->yzk", column_block, cas_along, precision=highest)
    across_rows = column_block.shape[0]
    depth_rows = column_block.shape[1]
    kappa_x = kappa_of(jnp.arange(along_cells).astype(jnp.float32), along_cells)
    kappa_y = kappa_of(
        (lax.axis_index("space") * across_rows + jnp.arange(across_rows)).astype(jnp.float32),
        width_cells,
    )
    kappa_z = kappa_of(
        (lax.axis_index("test") * depth_rows + jnp.arange(depth_rows)).astype(jnp.float32),
        depth_cells,
    )
    spectrum = (
        prior_gain
        / (
            1.0
            + range_squared
            * (kappa_y[:, None, None] + kappa_z[None, :, None] + kappa_x[None, None, :])
        )
        ** 2
    )
    along_back = jnp.einsum("yzk,kx->yzx", along_freq * spectrum, cas_along, precision=highest)
    slab_block = lax.all_to_all(along_back, "space", split_axis=2, concat_axis=0, tiled=True)
    across_back = jnp.einsum("yzx,yk->xzk", slab_block, cas_across, precision=highest)
    depth_block = lax.all_to_all(across_back, "test", split_axis=2, concat_axis=1, tiled=True)
    result = jnp.einsum("xky,kz->xyz", depth_block, cas_depth, precision=highest)
    scale_back = 1.0 / (along_cells * width_cells * depth_cells)
    return result * scale_back


GUARD = 8
STEP = 256.0
TOP = 32000.0
BF = jnp.bfloat16
F32 = jnp.float32
VM = pl.BlockSpec(memory_space=pltpu.VMEM)
SM = pl.BlockSpec(memory_space=pltpu.SMEM)
ANY = pl.BlockSpec(memory_space=pl.ANY)
MESH = pl.DeviceIdType.MESH


def shape(*dims, dtype=jnp.float32):
    return jax.ShapeDtypeStruct(dims, dtype)


def iota(plane, axis):
    return lax.broadcasted_iota(jnp.int32, plane, axis)


def halves(values):
    top = values.astype(BF)
    return top, (values - top.astype(F32)).astype(BF)


def matmul(a, b):
    return jnp.dot(a, b, preferred_element_type=F32)


def dot3(a, b):
    a_top, a_low = halves(a)
    b_top, b_low = halves(b)
    return matmul(a_top, b_top) + (matmul(a_top, b_low) + matmul(a_low, b_top))


def encode(values, spare):
    rows, lanes = values.shape
    peak = jnp.maximum(jnp.max(jnp.abs(values), axis=0, keepdims=True), 1e-30)
    level = jnp.ceil(jnp.log2(peak) * STEP)
    scaled = jnp.round(values * (jnp.exp2(level * (-1.0 / STEP)) * TOP))
    both = jnp.concatenate([scaled, jnp.broadcast_to(level, (spare, lanes))], axis=0)
    return both.astype(jnp.int32).astype(jnp.int16)


def decode(codes, spare):
    wide = codes.astype(jnp.int32).astype(F32)
    rows = wide.shape[0] - spare
    level = wide[rows : rows + 1]
    return wide[:rows] * (jnp.exp2(level * (1.0 / STEP)) * (1.0 / TOP))


def swap_blocks(planes):
    count = len(planes)
    lanes = planes[0].shape[1]
    block = lanes // count
    at_lane = iota(planes[0].shape, 1) // block
    swapped = []
    for to in range(count):
        joined = planes[to]
        for frm in range(count):
            if frm != to:
                shift = (block * (frm - to)) % lanes
                joined = jnp.where(at_lane == frm, pltpu.roll(planes[frm], shift, 1), joined)
        swapped.append(joined)
    return swapped


def greet(others):
    barrier = pltpu.get_barrier_semaphore()
    for other in others:
        pl.semaphore_signal(barrier, inc=1, device_id=other, device_id_type=MESH)
    pl.semaphore_wait(barrier, len(others))


def gradient_kernel(
    well,
    columns,
    observed,
    logk,
    warm,
    heads,
    turned,
    out,
    lk,
    wm,
    hd,
    soft,
    res,
    img,
    ring,
    sources,
    acc,
    shared,
    mine,
    from_mate,
    ship,
    got,
    load_sem,
    halo_send,
    halo_take,
    send_sum,
    take_sum,
    send_mate,
    take_mate,
    send_across,
    take_across,
):
    rows, width, depth = logk.shape
    parts = 4
    chunk = rows // parts
    piece = width // 3
    pieces = range(3)
    slabs = shared.shape[0]
    slab, here = lax.axis_index("space"), lax.axis_index("test")
    half, core = here // 2, lax.rem(here, 2)
    mate = {"test": 2 * half + 1 - core}
    across = {"test": 2 * (1 - half) + core}
    others = [{"space": lax.rem(slab + k, slabs)} for k in range(1, slabs)]
    first_row = slab * rows

    def loads(m):
        span = pl.ds(m * chunk, chunk)
        to = pl.ds(3 + m * chunk, chunk)
        return [
            pltpu.make_async_copy(frm.at[span], held.at[to], load_sem.at[n, m])
            for n, (frm, held) in enumerate(((logk, lk), (warm, wm), (heads, hd)))
        ]

    for m in range(parts):
        for copy in loads(m):
            copy.start()

    def halo(direction):
        up = direction == 1
        copies = []
        for n, (frm, held, deep) in enumerate(((logk, lk, 3), (warm, wm, 3), (heads, hd, 1))):
            at = rows - deep if up else 0
            to = 3 - deep if up else 3 + rows
            copies.append(
                pltpu.make_async_remote_copy(
                    src_ref=frm.at[pl.ds(at, deep)],
                    dst_ref=held.at[pl.ds(to, deep)],
                    send_sem=halo_send.at[direction, n],
                    recv_sem=halo_take.at[direction, n],
                    device_id={"space": slab + 1 if up else slab - 1},
                    device_id_type=MESH,
                )
            )
        return copies

    greet(others + [mate, across])

    @pl.when(slab > 0)
    def _():
        for copy in halo(0):
            copy.start()

    @pl.when(slab < slabs - 1)
    def _():
        for copy in halo(1):
            copy.start()

    blank = jnp.zeros((3, width, depth), BF)

    @pl.when(slab == 0)
    def _():
        lk[0:3] = blank
        wm[0:3] = blank
        hd[0:3] = blank

    @pl.when(slab == slabs - 1)
    def _():
        lk[rows + 3 : rows + 6] = blank
        wm[rows + 3 : rows + 6] = blank
        hd[rows + 3 : rows + 6] = blank

    top, low = halves(observed[...])
    sources[...] = jnp.concatenate([top, low], axis=0)
    acc[...] = jnp.zeros_like(acc)
    edge = jnp.zeros((GUARD, depth), F32)
    for i in range(ring.shape[0]):
        ring[i, 0:GUARD, :] = edge
        ring[i, width + GUARD : width + 2 * GUARD, :] = edge

    at_lane = iota((piece, depth), 1)
    at_row = iota((piece, depth), 0)
    is_first, is_last = at_lane == 0, at_lane == depth - 1
    spots = iota((width, 2 * columns.shape[1]), 0)

    def at(c):
        return pl.ds(c * piece, piece)

    def near(ref, i, c, off=0):
        return ref[i, pl.ds(GUARD + c * piece + off, piece), :]

    def store(ref, i, c, value):
        ref[i, pl.ds(GUARD + c * piece, piece), :] = value

    def ahead(value):
        return pltpu.roll(value, depth - 1, 1)

    def behind(value):
        return pltpu.roll(value, 1, 1)

    def ring_sum(held, ends, sides, outer):
        lanes = jnp.where(is_last, outer, ahead(held)) + jnp.where(is_first, outer, behind(held))
        return (lanes + ends) + sides

    def beside(ref, below, i, above, c, outer):
        held = near(ref, i, c)
        ends = near(ref, i, c, -1) + near(ref, i, c, 1)
        return held, ring_sum(held, ends, near(ref, below, c) + near(ref, above, c), outer)

    def around_slot(n, base, c):
        return beside(ring, base + (n - 1) % 4, base + n % 4, base + (n + 1) % 4, c, 0.0)

    def partial(value):
        return jnp.sum(value.reshape(piece // 8, 8, depth), axis=0)

    def clear(n, store_zero):
        if n < 3:
            pl.when(slab == 0)(store_zero)
        if n >= rows + 3:
            pl.when(slab == slabs - 1)(store_zero)

    blank_piece = jnp.zeros((piece, depth), F32)

    def prepare(at_row_base, views, n, static):
        soft_v, _, _, lk_v, wm_v = views
        one = jnp.ones((GUARD, depth), F32)
        soft_v[n, 0:GUARD, :] = one
        soft_v[n, width + GUARD : width + 2 * GUARD, :] = one
        for c in pieces:
            value = jnp.exp(0.5 * lk_v[n, at(c), :].astype(F32))
            store(soft_v, n, c, value)
            store(ring, n % 4, c, value * wm_v[n, at(c), :].astype(F32))

    def residual(at_row_base, views, n, static):
        soft_v, res_v = views[:2]
        spot = spots_at - (first_row + at_row_base + n - 3) * width
        hits = jnp.where(spots == spot, 1.0, 0.0).astype(BF)
        source = matmul(hits, sources[...])
        for c in pieces:
            s, around = beside(soft_v, n - 1, n, n + 1, c, 1.0)
            held, total = around_slot(n, 0, c)
            value = (s * total - held * around) + source[c * piece : (c + 1) * piece]
            res_v[n, at(c), :] = value
            store(ring, 4 + n % 4, c, s * value)
            store(ring, 12 + n % 4, c, around)

        def store_zero():
            for c in pieces:
                res_v[n, at(c), :] = blank_piece
                store(ring, 4 + n % 4, c, blank_piece)

        if static:
            clear(n, store_zero)

    def image(at_row_base, views, n, static, sums):
        soft_v, res_v, img_v = views[:3]
        for c in pieces:
            held, total = around_slot(n, 4, c)
            s, value = near(soft_v, n, c), res_v[n, at(c), :]
            applied = held * near(ring, 12 + n % 4, c) - s * total
            img_v[n, at(c), :] = applied
            store(ring, 8 + n % 4, c, s * applied)
            if sums is not None:
                sums[0].append(partial(value * value))
                sums[1].append(partial(value * applied))

        def store_zero():
            for c in pieces:
                img_v[n, at(c), :] = blank_piece
                store(ring, 8 + n % 4, c, blank_piece)

        if static:
            clear(n, store_zero)

    def twice(at_row_base, views, n, sums):
        img_v = views[2]
        for c in pieces:
            held, total = around_slot(n, 8, c)
            value = img_v[n, at(c), :]
            sums[2].append(partial(value * value))
            sums[3].append(partial(held * (value * near(ring, 12 + n % 4, c) - total)))

    def keep(sums):
        for n, terms in enumerate(sums):
            if terms:
                acc[n] += sum(terms[1:], terms[0])

    whole = (soft, res, img, lk, wm)

    def walk(first, last, r_rows, q_rows, q_own, t_rows):
        sums = [[], [], [], []]
        for k in range(first, last + 1):
            if k < rows + 6 and k <= r_rows[1] + 1:
                prepare(0, whole, k, True)
            if r_rows[0] <= k - 2 <= r_rows[1]:
                residual(0, whole, k - 2, True)
            if q_rows[0] <= k - 4 <= q_rows[1]:
                own = q_own[0] <= k - 4 <= q_own[1]
                image(0, whole, k - 4, True, sums if own else None)
            if t_rows[0] <= k - 5 <= t_rows[1]:
                twice(0, whole, k - 5, sums)
        keep(sums)

    def steady(j, _):
        base = 4 + 4 * j
        views = [ref.at[pl.ds(base, 11)] for ref in whole]
        sums = [[], [], [], []]
        for u in range(4):
            prepare(base, views, 7 + u, False)
            residual(base, views, 5 + u, False)
            image(base, views, 3 + u, False, sums)
            twice(base, views, 2 + u, sums)
        keep(sums)
        return 0

    spots_at = jnp.concatenate([columns[...], columns[...]], axis=1)
    for copy in loads(0):
        copy.wait()
    last = rows + 2
    walk(3, 10, (4, last + 2), (5, last + 1), (5, last), (6, last))
    for m in range(1, parts):
        for copy in loads(m):
            copy.wait()
    lax.fori_loop(0, (rows - 8) // 4, steady, 0)

    @pl.when(slab < slabs - 1)
    def _():
        for copy in halo(0):
            copy.wait_recv()

    walk(rows + 3, rows + 8, (4, last + 2), (5, last + 1), (5, last), (6, last))

    @pl.when(slab > 0)
    def _():
        for copy in halo(1):
            copy.wait_recv()

    walk(0, 10, (1, 7), (2, 6), (3, 4), (3, 5))

    shared[slab] = acc[...]
    copies = [
        pltpu.make_async_remote_copy(
            src_ref=shared.at[slab],
            dst_ref=shared.at[slab],
            send_sem=send_sum.at[k],
            recv_sem=take_sum.at[k],
            device_id=other,
            device_id_type=MESH,
        )
        for k, other in enumerate(others)
    ]
    for copy in copies:
        copy.start()

    @pl.when(slab > 0)
    def _():
        for copy in halo(0):
            copy.wait_send()

    @pl.when(slab < slabs - 1)
    def _():
        for copy in halo(1):
            copy.wait_send()

    for copy in copies:
        copy.wait()

    def gathered(n):
        total = shared[0, n]
        for m in range(1, slabs):
            total = total + shared[m, n]
        return jnp.broadcast_to(jnp.sum(total, axis=(0, 1), keepdims=True), (1, depth))

    norm, curve, square, bend = [gathered(n) for n in range(4)]
    length = norm / curve
    norm_next = length * length * square - norm
    curve_next = curve - 2.0 * length * square + length * length * bend
    ratio = norm_next / norm
    length_next = norm_next / (curve_next - ratio * norm_next / length)
    with_start = length + length_next * (1.0 + ratio)
    with_image = length_next * length

    def eighth(n, base):
        return base + lax.rem(n, 8)

    def fill(n):
        for c in pieces:
            field = wm[n, at(c), :].astype(F32)
            field = field + (with_start * res[n, at(c), :] - with_image * img[n, at(c), :])
            store(ring, eighth(n, 0), c, field)
            store(ring, eighth(n, 8), c, hd[n, at(c), :].astype(F32))

    fill(2)
    fill(3)
    count = 4
    groups = rows // count
    at_block = at_lane // (depth // count)

    def group(g):
        start = 3 + count * g
        for p in range(count):
            fill(start + p + 1)
        for c in pieces:
            fields = [near(ring, eighth(start + p, 0), c) for p in range(-1, count + 1)]
            levels = [near(ring, eighth(start + p, 8), c) for p in range(-1, count + 1)]
            steps = [
                (fields[p] - fields[p + 1]) * (levels[p] - levels[p + 1]) for p in range(count + 1)
            ]
            turns = []
            for p in range(count):
                n = start + p
                f, h, s = fields[p + 1], levels[p + 1], near(soft, n, c)
                total = near(soft, n - 1, c) * steps[p] + near(soft, n + 1, c) * steps[p + 1]
                for off in (-1, 1):
                    field = near(ring, eighth(n, 0), c, off)
                    level = near(ring, eighth(n, 8), c, off)
                    total += near(soft, n, c, off) * ((f - field) * (h - level))
                both = f * h
                product = (f - ahead(f)) * (h - ahead(h))
                total += jnp.where(is_last, both, ahead(s) * product)
                total += jnp.where(is_first, both, behind(s * product))
                place = well[0] - (first_row + n - 3) * width - c * piece
                value = jnp.where(at_row != place, s * total, 0.0)
                double = matmul(jnp.concatenate(halves(value), axis=1), turned[p])
                turns.append(double[:, :depth] + double[:, depth:])
            for t in range(count):
                joined = turns[-t % count]
                for b in range(1, count):
                    joined = jnp.where(at_block == b, turns[(b - t) % count], joined)
                mine[t % 2, g, t // 2, at(c), :] = joined
        to_mate(g).start()

    def to_mate(g):
        return pltpu.make_async_remote_copy(
            src_ref=mine.at[1 - core, g],
            dst_ref=from_mate.at[g],
            send_sem=send_mate.at[g],
            recv_sem=take_mate.at[g],
            device_id=mate,
            device_id_type=MESH,
        )

    def to_across(g):
        return pltpu.make_async_remote_copy(
            src_ref=ship.at[g],
            dst_ref=got.at[g],
            send_sem=send_across.at[g],
            recv_sem=take_across.at[g],
            device_id=across,
            device_id_type=MESH,
        )

    def relay(g):
        to_mate(g).wait_recv()
        ship[g] = encode(mine[core, g, 1 - half] + from_mate[g, 1 - half], 16)
        to_across(g).start()

    group(0)

    def step(g, _):
        group(g)
        relay(g - 1)
        return 0

    lax.fori_loop(1, groups, step, 0)
    relay(groups - 1)

    def finish(g, _):
        to_across(g).wait_recv()
        out[g] = (mine[core, g, half] + from_mate[g, half]) + decode(got[g], 16)
        to_mate(g).wait_send()
        to_across(g).wait_send()
        return 0

    lax.fori_loop(0, groups, finish, 0)


def spectral_kernel(
    summed,
    listed,
    cas_across,
    cas_depth,
    out,
    tables,
    freq,
    moments,
    filtered,
    going,
    coming,
    load_sem,
    send_end,
    take_end,
    send_back,
    take_back,
):
    groups, width, lanes = summed.shape
    count, part = going.shape[0], width // going.shape[0]
    spare = going.shape[2] - part
    rows = groups * count
    slabs = moments.shape[0]
    slab, here = lax.axis_index("space"), lax.axis_index("test")
    others = [{"space": lax.rem(slab + k, slabs)} for k in range(1, slabs)]
    peers = [lax.rem(here + k, count) for k in range(1, count)]
    fetch = pltpu.make_async_copy(listed.at[here], tables, load_sem)
    fetch.start()
    greet(others + [{"test": peer} for peer in peers])
    turn = lax.rem((count - here) * (lanes // count), lanes)

    def mix(g, _):
        top, low = halves(pltpu.roll(summed[g], turn, 1))
        mixed = matmul(cas_across[...], jnp.concatenate([top, top, low], axis=0))
        blocks = [mixed[j * part : (j + 1) * part] for j in range(count)]
        for p, plane in enumerate(swap_blocks(blocks)):
            freq[g * count + p] = plane
        return 0

    lax.fori_loop(0, groups, mix, 0)
    fetch.wait()
    pole, level, slope, decay, wrap_one, wrap_two = (tables[n] for n in range(6))

    def walk(i, carry):
        one, two, back_one, back_two = carry
        value, back = freq[i], freq[rows - 1 - i]
        return (
            value + pole * one,
            pole * (two + one),
            back + pole * back_one,
            pole * (back_two + back_one),
        )

    zero = jnp.zeros((part, lanes), jnp.float32)
    ends = lax.fori_loop(0, rows, walk, (zero, zero, zero, zero))
    for n in range(4):
        moments[slab, n] = encode(ends[n], spare)
    copies = [
        pltpu.make_async_remote_copy(
            src_ref=moments.at[slab],
            dst_ref=moments.at[slab],
            send_sem=send_end.at[k],
            recv_sem=take_end.at[k],
            device_id=other,
            device_id_type=MESH,
        )
        for k, other in enumerate(others)
    ]
    for copy in copies:
        copy.start()
    for copy in copies:
        copy.wait()

    def carried(direction, n):
        one, two = zero, zero
        for m in range(slabs, 0, -1):
            other = lax.rem(slab + 2 * slabs - direction * m, slabs)
            one, two = (
                decay * one + decode(moments[other, n], spare),
                decay * (two + rows * one) + decode(moments[other, n + 1], spare),
            )
        return wrap_one * one, wrap_one * two + wrap_two * one

    def forward(i, carry):
        one, two = carry
        two = pole * (two + one)
        one = freq[i] + pole * one
        filtered[i] = level * one + slope * two
        return one, two

    lax.fori_loop(0, rows, forward, carried(1, 0))

    def backward(i, carry):
        one, two = carry
        at = rows - 1 - i
        two = pole * (two + one)
        one = pole * one
        filtered[at] += level * one + slope * two
        return one + freq[at], two

    lax.fori_loop(0, rows, backward, carried(-1, 2))

    def to_peer(k, g):
        return pltpu.make_async_remote_copy(
            src_ref=going.at[peers[k], g],
            dst_ref=coming.at[here, g],
            send_sem=send_back.at[k, g],
            recv_sem=take_back.at[k, g],
            device_id={"test": peers[k]},
            device_id_type=MESH,
        )

    def unmix(g, _):
        blocks = swap_blocks([filtered[g * count + p] for p in range(count)])
        top, low = halves(jnp.concatenate(blocks, axis=0))
        mixed = matmul(cas_across[...], jnp.concatenate([top, top, low], axis=0))
        for u in range(count):
            going[u, g] = encode(mixed[u * part : (u + 1) * part], spare)
        for k in range(count - 1):
            to_peer(k, g).start()
        coming[here, g] = going[here, g]
        return 0

    lax.fori_loop(0, groups, unmix, 0)

    def back(g, _):
        for k in range(count - 1):
            to_peer(k, g).wait()
        planes = [decode(coming[t, g], spare) for t in range(count)]
        for p, plane in enumerate(swap_blocks(planes)):
            out[g * count + p] = dot3(plane, cas_depth[...])
        return 0

    lax.fori_loop(0, groups, back, 0)


def table(length):
    indices = np.arange(length)
    angles = (indices[:, None] * indices[None, :] % length) * (2.0 * np.pi / length)
    return (np.cos(angles) + np.sin(angles)).astype(np.float32)


def split(values):
    top = values.astype(jnp.bfloat16)
    return top, (values - top.astype(np.float32)).astype(jnp.bfloat16)


def turned_tables(length, count):
    tables = []
    for p in range(count):
        top, low = split(-0.5 * np.roll(table(length), p * (length // count), axis=1))
        tables.append(np.block([[top, low], [top, np.zeros_like(low)]]))
    return np.stack(tables)


def filter_tables(rows, along, width, depth, count):
    def kappa(length):
        return 4.0 * np.sin(np.pi * np.arange(length) / length) ** 2

    part, block = width // count, depth // count
    lanes_at = np.arange(depth)
    across_at = (lanes_at // block)[None, :] * part + np.arange(part)[:, None]
    listed = []
    for here in range(count):
        depth_at = here * block + lanes_at % block
        shift = 1.0 + range_squared * (kappa(width)[across_at] + kappa(depth)[depth_at][None, :])
        centre = 1.0 + shift / (2.0 * range_squared)
        pole = 1.0 / (centre + np.sqrt(centre * centre - 1.0))
        square = pole * pole
        gain = prior_gain / (range_squared * range_squared) * square / (width * depth)
        slope = gain / (1.0 - square) ** 2
        level = slope * (1.0 + square) / (1.0 - square)
        turn = pole**along
        wrap_one = 1.0 / (1.0 - turn)
        wrap_two = along * turn * wrap_one * wrap_one
        listed.append(np.stack([pole, level, slope, pole**rows, wrap_one, wrap_two]))
    return np.stack(listed).astype(np.float32)


def fast(log_k, heads, warm_adjoint, obs_columns, obs_residuals, well_columns):
    rows, width, depth = log_k.shape
    slabs = lax.axis_size("space")
    count = lax.axis_size("test")
    part = width // count
    groups = rows // count
    observed = obs_columns.shape[1]
    planes = rows + 6
    padded = width + 2 * GUARD
    spare = 16 - part % 16
    summed = pl.pallas_call(
        gradient_kernel,
        out_shape=shape(groups, width, depth),
        in_specs=[SM, VM, VM, ANY, ANY, ANY, VM],
        out_specs=VM,
        scratch_shapes=[pltpu.VMEM((planes, width, depth), BF)] * 3
        + [
            pltpu.VMEM((planes, padded, depth), F32),
            pltpu.VMEM((planes, width, depth), F32),
            pltpu.VMEM((planes, width, depth), F32),
            pltpu.VMEM((16, padded, depth), F32),
            pltpu.VMEM((2 * observed, depth), BF),
            pltpu.VMEM((4, 8, depth), F32),
            pltpu.VMEM((slabs, 4, 8, depth), F32),
            pltpu.VMEM((2, groups, 2, width, depth), F32),
            pltpu.VMEM((groups, 2, width, depth), F32),
            pltpu.VMEM((groups, width + 16, depth), jnp.int16),
            pltpu.VMEM((groups, width + 16, depth), jnp.int16),
            pltpu.SemaphoreType.DMA((3, 4)),
        ]
        + [pltpu.SemaphoreType.DMA((2, 3))] * 2
        + [pltpu.SemaphoreType.DMA((slabs - 1,))] * 2
        + [pltpu.SemaphoreType.DMA((groups,))] * 4,
        compiler_params=pltpu.CompilerParams(
            vmem_limit_bytes=60 * 1024 * 1024, collective_id=1, has_side_effects=True
        ),
        name="gradient",
    )(
        well_columns,
        obs_columns,
        obs_residuals[0],
        log_k,
        warm_adjoint[0],
        heads[0],
        jnp.asarray(turned_tables(depth, count)),
    )
    top, low = split(table(width))
    return pl.pallas_call(
        spectral_kernel,
        out_shape=shape(rows, part, depth),
        in_specs=[VM, ANY, VM, VM],
        out_specs=VM,
        scratch_shapes=[
            pltpu.VMEM((6, part, depth), F32),
            pltpu.VMEM((rows, part, depth), F32),
            pltpu.VMEM((slabs, 4, part + spare, depth), jnp.int16),
            pltpu.VMEM((rows, part, depth), F32),
            pltpu.VMEM((count, groups, part + spare, depth), jnp.int16),
            pltpu.VMEM((count, groups, part + spare, depth), jnp.int16),
            pltpu.SemaphoreType.DMA,
            pltpu.SemaphoreType.DMA((slabs - 1,)),
            pltpu.SemaphoreType.DMA((slabs - 1,)),
            pltpu.SemaphoreType.DMA((count - 1, groups)),
            pltpu.SemaphoreType.DMA((count - 1, groups)),
        ],
        compiler_params=pltpu.CompilerParams(
            vmem_limit_bytes=40 * 1024 * 1024, collective_id=2, has_side_effects=True
        ),
        name="spectral",
    )(
        summed,
        jnp.asarray(filter_tables(rows, rows * slabs, width, depth, count)),
        jnp.asarray(np.concatenate([top, low, top], axis=1)),
        jnp.asarray(table(depth)),
    )


def pick(log_k, heads, warm_adjoint, obs_columns, *rest):
    rows, width, depth = log_k.shape
    count = lax.axis_size("test")
    fits = depth == 128 and count == 4 and rows % 4 == 0 and rows >= 16 and width % 96 == 0
    fits = fits and obs_columns.shape[1] % 64 == 0 and rows * width <= 48 * 288
    run = fast if fits and lax.axis_size("space") > 1 else on_device
    return run(log_k, heads, warm_adjoint, obs_columns, *rest)


def solution(mesh):
    placed = (
        P(("groups", "space"), None, None),
        P("test", ("groups", "space"), None, None),
        P("test", ("groups", "space"), None, None),
        P("test", "groups"),
        P("test", "groups", None),
        P(("groups", "test")),
    )
    return jax.shard_map(
        pick,
        mesh=mesh,
        in_specs=placed,
        out_specs=P(("groups", "space"), "test", None),
        check_vma=False,
    )
```

```python
import jax
import jax.numpy as jnp
import numpy as np
from jax import lax
from jax.experimental import pallas as pl
from jax.experimental.pallas import tpu as pltpu
from jax.sharding import PartitionSpec as P

ITERS = 2


prior_gain = 5.0
range_squared = 4.0


def with_halo(cells, sides, width):
    for axis, dim in sides:
        count = lax.axis_size(axis)
        ends = count - 1
        head = lax.slice_in_dim(cells, 0, width, axis=dim)
        tail = lax.slice_in_dim(cells, cells.shape[dim] - width, cells.shape[dim], axis=dim)
        cells = jnp.concatenate(
            [
                lax.ppermute(tail, axis, [(i, (i + 1) % count) for i in range(ends)]),
                cells,
                lax.ppermute(head, axis, [((i + 1) % count, i) for i in range(ends)]),
            ],
            axis=dim,
        )
    return cells


def neighbours(padded):
    return [
        padded[2:, 1:-1, 1:-1],
        padded[:-2, 1:-1, 1:-1],
        padded[1:-1, 2:, 1:-1],
        padded[1:-1, :-2, 1:-1],
        padded[1:-1, 1:-1, 2:],
        padded[1:-1, 1:-1, :-2],
    ]


def operate(values, padded, conduct):
    summed = jnp.zeros_like(values)
    for face_k, beside in zip(conduct, neighbours(padded)):
        summed = summed + face_k * (values - beside)
    return summed


def kappa_of(indices, length):
    return 4.0 * jnp.sin(jnp.pi * indices / length) ** 2


def pad_sides(padded):
    return jnp.pad(padded, ((0, 0), (1, 1), (1, 1)))


def with_faces(values):
    return pad_sides(with_halo(values, (("space", 0),), 1))


def squares(residual):
    return lax.psum(jnp.sum(residual * residual), "space")


def hartley(length):
    indices = jnp.arange(length, dtype=jnp.int32)
    products = indices[:, None] * indices[None, :] % length
    angles = products.astype(jnp.float32) * (2.0 * jnp.pi / length)
    return jnp.cos(angles) + jnp.sin(angles)


def on_device(log_k, heads, warm_adjoint, obs_columns, obs_residuals, well_columns):
    slab_rows, width_cells, depth_cells = log_k.shape
    space_count = lax.axis_size("space")
    first_row = lax.axis_index("space") * slab_rows
    logk_pad, head_pad = (
        with_halo(log_k, (("space", 0),), 1),
        with_halo(heads[0], (("space", 0),), 1),
    )
    logk_val = log_k.astype(jnp.float32)
    conduct = [
        jnp.exp(0.5 * (logk_val + beside))
        for beside in neighbours(pad_sides(logk_pad.astype(jnp.float32)))
    ]
    columns = obs_columns[0]
    row_local = columns // width_cells - first_row
    inside = (row_local >= 0) & (row_local < slab_rows)
    row_local = jnp.where(inside, row_local, slab_rows)
    source = jnp.zeros((slab_rows, width_cells, depth_cells), jnp.float32)
    source = source.at[row_local, columns % width_cells].add(obs_residuals[0], mode="drop")
    adjoint = warm_adjoint[0].astype(jnp.float32)
    lam_padded = with_faces(adjoint)
    residual = source - operate(adjoint, lam_padded, conduct)
    direction = residual
    norm_now = squares(residual)
    for iteration in range(ITERS):
        dir_padded = with_faces(direction)
        applied = operate(direction, dir_padded, conduct)
        step_length = norm_now / lax.psum(jnp.sum(direction * applied), "space")
        adjoint = adjoint + step_length * direction
        lam_padded = lam_padded + step_length * dir_padded
        if iteration + 1 < ITERS:
            residual = residual - step_length * applied
            norm_next = squares(residual)
            direction = residual + norm_next / norm_now * direction
            norm_now = norm_next
    lam_full = pad_sides(with_halo(adjoint, (("space", 0),), 1))
    head_val = heads[0].astype(jnp.float32)
    misfit_term = jnp.zeros_like(adjoint)
    for face_k, lam_side, head_side in zip(
        conduct, neighbours(lam_full), neighbours(pad_sides(head_pad.astype(jnp.float32)))
    ):
        misfit_term = misfit_term + face_k * (adjoint - lam_side) * (head_val - head_side)
    column_ids = (first_row + jnp.arange(slab_rows, dtype=jnp.int32))[
        :, None
    ] * width_cells + jnp.arange(width_cells, dtype=jnp.int32)[None, :]
    keep_mask = (column_ids != well_columns[0]).astype(jnp.float32)
    partial_value = -0.5 * misfit_term * keep_mask[:, :, None]
    highest = lax.Precision.HIGHEST
    cas_depth = hartley(depth_cells)
    cas_across = hartley(width_cells)
    along_cells = slab_rows * space_count
    cas_along = hartley(along_cells)
    summed = lax.psum_scatter(partial_value, "test", scatter_dimension=1, tiled=True)
    depth_freq = jnp.einsum("xyz,zk->xky", summed, cas_depth, precision=highest)
    pencil = lax.all_to_all(depth_freq, "test", split_axis=1, concat_axis=2, tiled=True)
    across_freq = jnp.einsum("xzy,yk->kzx", pencil, cas_across, precision=highest)
    column_block = lax.all_to_all(across_freq, "space", split_axis=0, concat_axis=2, tiled=True)
    along_freq = jnp.einsum("yzx,xk->yzk", column_block, cas_along, precision=highest)
    across_rows = column_block.shape[0]
    depth_rows = column_block.shape[1]
    kappa_x = kappa_of(jnp.arange(along_cells).astype(jnp.float32), along_cells)
    kappa_y = kappa_of(
        (lax.axis_index("space") * across_rows + jnp.arange(across_rows)).astype(jnp.float32),
        width_cells,
    )
    kappa_z = kappa_of(
        (lax.axis_index("test") * depth_rows + jnp.arange(depth_rows)).astype(jnp.float32),
        depth_cells,
    )
    spectrum = (
        prior_gain
        / (
            1.0
            + range_squared
            * (kappa_y[:, None, None] + kappa_z[None, :, None] + kappa_x[None, None, :])
        )
        ** 2
    )
    along_back = jnp.einsum("yzk,kx->yzx", along_freq * spectrum, cas_along, precision=highest)
    slab_block = lax.all_to_all(along_back, "space", split_axis=2, concat_axis=0, tiled=True)
    across_back = jnp.einsum("yzx,yk->xzk", slab_block, cas_across, precision=highest)
    depth_block = lax.all_to_all(across_back, "test", split_axis=2, concat_axis=1, tiled=True)
    result = jnp.einsum("xky,kz->xyz", depth_block, cas_depth, precision=highest)
    scale_back = 1.0 / (along_cells * width_cells * depth_cells)
    return result * scale_back


GUARD = 8
STEP = 256.0
TOP = 32000.0
BF = jnp.bfloat16
F32 = jnp.float32
VM = pl.BlockSpec(memory_space=pltpu.VMEM)
SM = pl.BlockSpec(memory_space=pltpu.SMEM)
ANY = pl.BlockSpec(memory_space=pl.ANY)
MESH = pl.DeviceIdType.MESH


def shape(*dims, dtype=jnp.float32):
    return jax.ShapeDtypeStruct(dims, dtype)


def iota(plane, axis):
    return lax.broadcasted_iota(jnp.int32, plane, axis)


def halves(values):
    top = values.astype(BF)
    return top, (values - top.astype(F32)).astype(BF)


def matmul(a, b):
    return jnp.dot(a, b, preferred_element_type=F32)


def dot3(a, b):
    a_top, a_low = halves(a)
    b_top, b_low = halves(b)
    return matmul(a_top, b_top) + (matmul(a_top, b_low) + matmul(a_low, b_top))


def encode(values, spare):
    rows, lanes = values.shape
    peak = jnp.maximum(jnp.max(jnp.abs(values), axis=0, keepdims=True), 1e-30)
    level = jnp.ceil(jnp.log2(peak) * STEP)
    scaled = jnp.round(values * (jnp.exp2(level * (-1.0 / STEP)) * TOP))
    both = jnp.concatenate([scaled, jnp.broadcast_to(level, (spare, lanes))], axis=0)
    return both.astype(jnp.int32).astype(jnp.int16)


def decode(codes, spare):
    wide = codes.astype(jnp.int32).astype(F32)
    rows = wide.shape[0] - spare
    level = wide[rows : rows + 1]
    return wide[:rows] * (jnp.exp2(level * (1.0 / STEP)) * (1.0 / TOP))


def swap_blocks(planes):
    count = len(planes)
    lanes = planes[0].shape[1]
    block = lanes // count
    at_lane = iota(planes[0].shape, 1) // block
    swapped = []
    for to in range(count):
        joined = planes[to]
        for frm in range(count):
            if frm != to:
                shift = (block * (frm - to)) % lanes
                joined = jnp.where(at_lane == frm, pltpu.roll(planes[frm], shift, 1), joined)
        swapped.append(joined)
    return swapped


def greet(others):
    barrier = pltpu.get_barrier_semaphore()
    for other in others:
        pl.semaphore_signal(barrier, inc=1, device_id=other, device_id_type=MESH)
    pl.semaphore_wait(barrier, len(others))


def whole_kernel(
    well,
    columns,
    observed,
    logk,
    warm,
    heads,
    turned,
    listed,
    cas_across,
    cas_depth,
    out,
    lk,
    wm,
    hd,
    soft,
    res,
    img,
    ring,
    sources,
    acc,
    shared,
    mine,
    from_mate,
    ship,
    got,
    load_sem,
    halo_send,
    halo_take,
    send_sum,
    take_sum,
    send_mate,
    take_mate,
    send_across,
    take_across,
    tables,
    freq,
    moments,
    going,
    coming,
    table_sem,
    send_end,
    take_end,
    send_back,
    take_back,
):
    rows, width, depth = logk.shape
    parts = 4
    chunk = rows // parts
    piece = width // 3
    pieces = range(3)
    slabs = shared.shape[0]
    slab, here = lax.axis_index("space"), lax.axis_index("test")
    half, core = here // 2, lax.rem(here, 2)
    mate = {"test": 2 * half + 1 - core}
    across = {"test": 2 * (1 - half) + core}
    others = [{"space": lax.rem(slab + k, slabs)} for k in range(1, slabs)]
    first_row = slab * rows

    def loads(m):
        span = pl.ds(m * chunk, chunk)
        to = pl.ds(3 + m * chunk, chunk)
        return [
            pltpu.make_async_copy(frm.at[span], held.at[to], load_sem.at[n, m])
            for n, (frm, held) in enumerate(((logk, lk), (warm, wm), (heads, hd)))
        ]

    for m in range(parts):
        for copy in loads(m):
            copy.start()

    def halo(direction):
        up = direction == 1
        copies = []
        for n, (frm, held, deep) in enumerate(((logk, lk, 3), (warm, wm, 3), (heads, hd, 1))):
            at = rows - deep if up else 0
            to = 3 - deep if up else 3 + rows
            copies.append(
                pltpu.make_async_remote_copy(
                    src_ref=frm.at[pl.ds(at, deep)],
                    dst_ref=held.at[pl.ds(to, deep)],
                    send_sem=halo_send.at[direction, n],
                    recv_sem=halo_take.at[direction, n],
                    device_id={"space": slab + 1 if up else slab - 1},
                    device_id_type=MESH,
                )
            )
        return copies

    count = 4
    peers = [lax.rem(here + k, count) for k in range(1, count)]
    fetch = pltpu.make_async_copy(listed.at[here], tables, table_sem)
    fetch.start()
    greet(others + [{"test": peer} for peer in peers])

    @pl.when(slab > 0)
    def _():
        for copy in halo(0):
            copy.start()

    @pl.when(slab < slabs - 1)
    def _():
        for copy in halo(1):
            copy.start()

    blank = jnp.zeros((3, width, depth), BF)

    @pl.when(slab == 0)
    def _():
        lk[0:3] = blank
        wm[0:3] = blank
        hd[0:3] = blank

    @pl.when(slab == slabs - 1)
    def _():
        lk[rows + 3 : rows + 6] = blank
        wm[rows + 3 : rows + 6] = blank
        hd[rows + 3 : rows + 6] = blank

    top, low = halves(observed[...])
    sources[...] = jnp.concatenate([top, low], axis=0)
    acc[...] = jnp.zeros_like(acc)
    edge = jnp.zeros((GUARD, depth), F32)
    for i in range(ring.shape[0]):
        ring[i, 0:GUARD, :] = edge
        ring[i, width + GUARD : width + 2 * GUARD, :] = edge

    at_lane = iota((piece, depth), 1)
    at_row = iota((piece, depth), 0)
    is_first, is_last = at_lane == 0, at_lane == depth - 1
    spots = iota((width, 2 * columns.shape[1]), 0)

    def at(c):
        return pl.ds(c * piece, piece)

    def near(ref, i, c, off=0):
        return ref[i, pl.ds(GUARD + c * piece + off, piece), :]

    def store(ref, i, c, value):
        ref[i, pl.ds(GUARD + c * piece, piece), :] = value

    def ahead(value):
        return pltpu.roll(value, depth - 1, 1)

    def behind(value):
        return pltpu.roll(value, 1, 1)

    def ring_sum(held, ends, sides, outer):
        lanes = jnp.where(is_last, outer, ahead(held)) + jnp.where(is_first, outer, behind(held))
        return (lanes + ends) + sides

    def beside(ref, below, i, above, c, outer):
        held = near(ref, i, c)
        ends = near(ref, i, c, -1) + near(ref, i, c, 1)
        return held, ring_sum(held, ends, near(ref, below, c) + near(ref, above, c), outer)

    def around_slot(n, base, c):
        return beside(ring, base + (n - 1) % 4, base + n % 4, base + (n + 1) % 4, c, 0.0)

    def partial(value):
        return jnp.sum(value.reshape(piece // 8, 8, depth), axis=0)

    def clear(n, store_zero):
        if n < 3:
            pl.when(slab == 0)(store_zero)
        if n >= rows + 3:
            pl.when(slab == slabs - 1)(store_zero)

    blank_piece = jnp.zeros((piece, depth), F32)

    def prepare(at_row_base, views, n, static):
        soft_v, _, _, lk_v, wm_v = views
        one = jnp.ones((GUARD, depth), F32)
        soft_v[n, 0:GUARD, :] = one
        soft_v[n, width + GUARD : width + 2 * GUARD, :] = one
        for c in pieces:
            value = jnp.exp(0.5 * lk_v[n, at(c), :].astype(F32))
            store(soft_v, n, c, value)
            store(ring, n % 4, c, value * wm_v[n, at(c), :].astype(F32))

    def residual(at_row_base, views, n, static):
        soft_v, res_v = views[:2]
        spot = spots_at - (first_row + at_row_base + n - 3) * width
        hits = jnp.where(spots == spot, 1.0, 0.0).astype(BF)
        source = matmul(hits, sources[...])
        for c in pieces:
            s, around = beside(soft_v, n - 1, n, n + 1, c, 1.0)
            held, total = around_slot(n, 0, c)
            value = (s * total - held * around) + source[c * piece : (c + 1) * piece]
            res_v[n, at(c), :] = value
            store(ring, 4 + n % 4, c, s * value)
            store(ring, 12 + n % 4, c, around)

        def store_zero():
            for c in pieces:
                res_v[n, at(c), :] = blank_piece
                store(ring, 4 + n % 4, c, blank_piece)

        if static:
            clear(n, store_zero)

    def image(at_row_base, views, n, static, sums):
        soft_v, res_v, img_v = views[:3]
        for c in pieces:
            held, total = around_slot(n, 4, c)
            s, value = near(soft_v, n, c), res_v[n, at(c), :]
            applied = held * near(ring, 12 + n % 4, c) - s * total
            img_v[n, at(c), :] = applied
            store(ring, 8 + n % 4, c, s * applied)
            if sums is not None:
                sums[0].append(partial(value * value))
                sums[1].append(partial(value * applied))

        def store_zero():
            for c in pieces:
                img_v[n, at(c), :] = blank_piece
                store(ring, 8 + n % 4, c, blank_piece)

        if static:
            clear(n, store_zero)

    def twice(at_row_base, views, n, sums):
        img_v = views[2]
        for c in pieces:
            held, total = around_slot(n, 8, c)
            value = img_v[n, at(c), :]
            sums[2].append(partial(value * value))
            sums[3].append(partial(held * (value * near(ring, 12 + n % 4, c) - total)))

    def keep(sums):
        for n, terms in enumerate(sums):
            if terms:
                acc[n] += sum(terms[1:], terms[0])

    whole = (soft, res, img, lk, wm)

    def walk(first, last, r_rows, q_rows, q_own, t_rows):
        sums = [[], [], [], []]
        for k in range(first, last + 1):
            if k < rows + 6 and k <= r_rows[1] + 1:
                prepare(0, whole, k, True)
            if r_rows[0] <= k - 2 <= r_rows[1]:
                residual(0, whole, k - 2, True)
            if q_rows[0] <= k - 4 <= q_rows[1]:
                own = q_own[0] <= k - 4 <= q_own[1]
                image(0, whole, k - 4, True, sums if own else None)
            if t_rows[0] <= k - 5 <= t_rows[1]:
                twice(0, whole, k - 5, sums)
        keep(sums)

    def steady(j, _):
        base = 4 + 4 * j
        views = [ref.at[pl.ds(base, 11)] for ref in whole]
        sums = [[], [], [], []]
        for u in range(4):
            prepare(base, views, 7 + u, False)
            residual(base, views, 5 + u, False)
            image(base, views, 3 + u, False, sums)
            twice(base, views, 2 + u, sums)
        keep(sums)
        return 0

    spots_at = jnp.concatenate([columns[...], columns[...]], axis=1)
    for copy in loads(0):
        copy.wait()
    last = rows + 2
    walk(3, 10, (4, last + 2), (5, last + 1), (5, last), (6, last))
    for m in range(1, parts):
        for copy in loads(m):
            copy.wait()
    lax.fori_loop(0, (rows - 8) // 4, steady, 0)

    @pl.when(slab < slabs - 1)
    def _():
        for copy in halo(0):
            copy.wait_recv()

    walk(rows + 3, rows + 8, (4, last + 2), (5, last + 1), (5, last), (6, last))

    @pl.when(slab > 0)
    def _():
        for copy in halo(1):
            copy.wait_recv()

    walk(0, 10, (1, 7), (2, 6), (3, 4), (3, 5))

    shared[slab] = acc[...]
    copies = [
        pltpu.make_async_remote_copy(
            src_ref=shared.at[slab],
            dst_ref=shared.at[slab],
            send_sem=send_sum.at[k],
            recv_sem=take_sum.at[k],
            device_id=other,
            device_id_type=MESH,
        )
        for k, other in enumerate(others)
    ]
    for copy in copies:
        copy.start()

    @pl.when(slab > 0)
    def _():
        for copy in halo(0):
            copy.wait_send()

    @pl.when(slab < slabs - 1)
    def _():
        for copy in halo(1):
            copy.wait_send()

    for copy in copies:
        copy.wait()

    def gathered(n):
        total = shared[0, n]
        for m in range(1, slabs):
            total = total + shared[m, n]
        return jnp.broadcast_to(jnp.sum(total, axis=(0, 1), keepdims=True), (1, depth))

    norm, curve, square, bend = [gathered(n) for n in range(4)]
    length = norm / curve
    norm_next = length * length * square - norm
    curve_next = curve - 2.0 * length * square + length * length * bend
    ratio = norm_next / norm
    length_next = norm_next / (curve_next - ratio * norm_next / length)
    with_start = length + length_next * (1.0 + ratio)
    with_image = length_next * length

    def eighth(n, base):
        return base + lax.rem(n, 8)

    def fill(n):
        for c in pieces:
            field = wm[n, at(c), :].astype(F32)
            field = field + (with_start * res[n, at(c), :] - with_image * img[n, at(c), :])
            store(ring, eighth(n, 0), c, field)
            store(ring, eighth(n, 8), c, hd[n, at(c), :].astype(F32))

    fill(2)
    fill(3)
    groups = rows // count
    at_block = at_lane // (depth // count)

    def group(g):
        start = 3 + count * g
        for p in range(count):
            fill(start + p + 1)
        for c in pieces:
            fields = [near(ring, eighth(start + p, 0), c) for p in range(-1, count + 1)]
            levels = [near(ring, eighth(start + p, 8), c) for p in range(-1, count + 1)]
            steps = [
                (fields[p] - fields[p + 1]) * (levels[p] - levels[p + 1]) for p in range(count + 1)
            ]
            turns = []
            for p in range(count):
                n = start + p
                f, h, s = fields[p + 1], levels[p + 1], near(soft, n, c)
                total = near(soft, n - 1, c) * steps[p] + near(soft, n + 1, c) * steps[p + 1]
                for off in (-1, 1):
                    field = near(ring, eighth(n, 0), c, off)
                    level = near(ring, eighth(n, 8), c, off)
                    total += near(soft, n, c, off) * ((f - field) * (h - level))
                both = f * h
                product = (f - ahead(f)) * (h - ahead(h))
                total += jnp.where(is_last, both, ahead(s) * product)
                total += jnp.where(is_first, both, behind(s * product))
                place = well[0] - (first_row + n - 3) * width - c * piece
                value = jnp.where(at_row != place, s * total, 0.0)
                double = matmul(jnp.concatenate(halves(value), axis=1), turned[p])
                turns.append(double[:, :depth] + double[:, depth:])
            for t in range(count):
                joined = turns[-t % count]
                for b in range(1, count):
                    joined = jnp.where(at_block == b, turns[(b - t) % count], joined)
                mine[t % 2, g, t // 2, at(c), :] = joined

    def to_mate(g):
        return pltpu.make_async_remote_copy(
            src_ref=mine.at[1 - core, g],
            dst_ref=from_mate.at[g],
            send_sem=send_mate.at[g],
            recv_sem=take_mate.at[g],
            device_id=mate,
            device_id_type=MESH,
        )

    def to_across(g):
        return pltpu.make_async_remote_copy(
            src_ref=ship.at[g],
            dst_ref=got.at[g],
            send_sem=send_across.at[g],
            recv_sem=take_across.at[g],
            device_id=across,
            device_id_type=MESH,
        )

    def relay(g):
        to_mate(g).wait_recv()
        ship[g] = encode(mine[core, g, 1 - half] + from_mate[g, 1 - half], 16)
        to_across(g).start()

    part = width // count
    spare = going.shape[2] - part
    lanes = depth
    turn = lax.rem((count - here) * (lanes // count), lanes)
    filtered = res.at[:, pl.ds(0, part)]

    def settle(g):
        to_across(g).wait_recv()
        to_mate(g).wait_send()
        to_across(g).wait_send()

    def absorb(g):
        summed = (mine[core, g, half] + from_mate[g, half]) + decode(got[g], 16)
        top, low = halves(pltpu.roll(summed, turn, 1))
        mixed = matmul(cas_across[...], jnp.concatenate([top, top, low], axis=0))
        blocks = [mixed[j * part : (j + 1) * part] for j in range(count)]
        for p, plane in enumerate(swap_blocks(blocks)):
            freq[g * count + p] = plane

    lag = 4

    def early(g, _):
        group(g)
        to_mate(g).start()
        relay(g - 1)
        return 0

    def late(g, _):
        settle(g - lag)
        absorb(g - lag)
        group(g)
        to_mate(g).start()
        relay(g - 1)
        return 0

    group(0)
    to_mate(0).start()
    lax.fori_loop(1, lag, early, 0)
    lax.fori_loop(lag, groups, late, 0)
    relay(groups - 1)

    def finish(g, _):
        settle(g)
        absorb(g)
        return 0

    lax.fori_loop(groups - lag, groups, finish, 0)
    fetch.wait()
    pole, level, slope, decay, wrap_one, wrap_two = (tables[n] for n in range(6))

    def gather(i, carry):
        one, two, back_one, back_two = carry
        value, back = freq[i], freq[rows - 1 - i]
        return (
            value + pole * one,
            pole * (two + one),
            back + pole * back_one,
            pole * (back_two + back_one),
        )

    zero = jnp.zeros((part, lanes), jnp.float32)
    ends = lax.fori_loop(0, rows, gather, (zero, zero, zero, zero))
    for n in range(4):
        moments[slab, n] = encode(ends[n], spare)
    copies = [
        pltpu.make_async_remote_copy(
            src_ref=moments.at[slab],
            dst_ref=moments.at[slab],
            send_sem=send_end.at[k],
            recv_sem=take_end.at[k],
            device_id=other,
            device_id_type=MESH,
        )
        for k, other in enumerate(others)
    ]
    for copy in copies:
        copy.start()
    for copy in copies:
        copy.wait()

    def carried(direction, n):
        one, two = zero, zero
        for m in range(slabs, 0, -1):
            other = lax.rem(slab + 2 * slabs - direction * m, slabs)
            one, two = (
                decay * one + decode(moments[other, n], spare),
                decay * (two + rows * one) + decode(moments[other, n + 1], spare),
            )
        return wrap_one * one, wrap_one * two + wrap_two * one

    def forward(i, carry):
        one, two = carry
        two = pole * (two + one)
        one = freq[i] + pole * one
        filtered[i] = level * one + slope * two
        return one, two

    lax.fori_loop(0, rows, forward, carried(1, 0))

    def backward(i, carry):
        one, two = carry
        at = rows - 1 - i
        two = pole * (two + one)
        one = pole * one
        filtered[at] += level * one + slope * two
        return one + freq[at], two

    lax.fori_loop(0, rows, backward, carried(-1, 2))

    def to_peer(k, g):
        return pltpu.make_async_remote_copy(
            src_ref=going.at[peers[k], g],
            dst_ref=coming.at[here, g],
            send_sem=send_back.at[k, g],
            recv_sem=take_back.at[k, g],
            device_id={"test": peers[k]},
            device_id_type=MESH,
        )

    pair = 2

    def unmix(j, _):
        for g in [pair * j + n for n in range(pair)]:
            blocks = swap_blocks([filtered[g * count + p] for p in range(count)])
            top, low = halves(jnp.concatenate(blocks, axis=0))
            mixed = matmul(cas_across[...], jnp.concatenate([top, top, low], axis=0))
            for u in range(count):
                going[u, g] = encode(mixed[u * part : (u + 1) * part], spare)
        for g in [pair * j + n for n in range(pair)]:
            for k in range(count - 1):
                to_peer(k, g).start()
            coming[here, g] = going[here, g]
        return 0

    lax.fori_loop(0, groups // pair, unmix, 0)

    def back(j, _):
        for g in [pair * j + n for n in range(pair)]:
            for k in range(count - 1):
                to_peer(k, g).wait()
        for g in [pair * j + n for n in range(pair)]:
            planes = [decode(coming[t, g], spare) for t in range(count)]
            for p, plane in enumerate(swap_blocks(planes)):
                out[g * count + p] = dot3(plane, cas_depth[...])
        return 0

    lax.fori_loop(0, groups // pair, back, 0)


def table(length):
    indices = np.arange(length)
    angles = (indices[:, None] * indices[None, :] % length) * (2.0 * np.pi / length)
    return (np.cos(angles) + np.sin(angles)).astype(np.float32)


def split(values):
    top = values.astype(jnp.bfloat16)
    return top, (values - top.astype(np.float32)).astype(jnp.bfloat16)


def turned_tables(length, count):
    tables = []
    for p in range(count):
        top, low = split(-0.5 * np.roll(table(length), p * (length // count), axis=1))
        tables.append(np.block([[top, low], [top, np.zeros_like(low)]]))
    return np.stack(tables)


def filter_tables(rows, along, width, depth, count):
    def kappa(length):
        return 4.0 * np.sin(np.pi * np.arange(length) / length) ** 2

    part, block = width // count, depth // count
    lanes_at = np.arange(depth)
    across_at = (lanes_at // block)[None, :] * part + np.arange(part)[:, None]
    listed = []
    for here in range(count):
        depth_at = here * block + lanes_at % block
        shift = 1.0 + range_squared * (kappa(width)[across_at] + kappa(depth)[depth_at][None, :])
        centre = 1.0 + shift / (2.0 * range_squared)
        pole = 1.0 / (centre + np.sqrt(centre * centre - 1.0))
        square = pole * pole
        gain = prior_gain / (range_squared * range_squared) * square / (width * depth)
        slope = gain / (1.0 - square) ** 2
        level = slope * (1.0 + square) / (1.0 - square)
        turn = pole**along
        wrap_one = 1.0 / (1.0 - turn)
        wrap_two = along * turn * wrap_one * wrap_one
        listed.append(np.stack([pole, level, slope, pole**rows, wrap_one, wrap_two]))
    return np.stack(listed).astype(np.float32)


def fast(log_k, heads, warm_adjoint, obs_columns, obs_residuals, well_columns):
    rows, width, depth = log_k.shape
    slabs = lax.axis_size("space")
    count = lax.axis_size("test")
    part = width // count
    groups = rows // count
    observed = obs_columns.shape[1]
    planes = rows + 6
    padded = width + 2 * GUARD
    spare = 16 - part % 16
    top, low = split(table(width))
    return pl.pallas_call(
        whole_kernel,
        out_shape=shape(rows, part, depth),
        in_specs=[SM, VM, VM, ANY, ANY, ANY, VM, ANY, VM, VM],
        out_specs=VM,
        scratch_shapes=[pltpu.VMEM((planes, width, depth), BF)] * 3
        + [
            pltpu.VMEM((planes, padded, depth), F32),
            pltpu.VMEM((planes, width, depth), F32),
            pltpu.VMEM((planes, width, depth), F32),
            pltpu.VMEM((16, padded, depth), F32),
            pltpu.VMEM((2 * observed, depth), BF),
            pltpu.VMEM((4, 8, depth), F32),
            pltpu.VMEM((slabs, 4, 8, depth), F32),
            pltpu.VMEM((2, groups, 2, width, depth), F32),
            pltpu.VMEM((groups, 2, width, depth), F32),
            pltpu.VMEM((groups, width + 16, depth), jnp.int16),
            pltpu.VMEM((groups, width + 16, depth), jnp.int16),
            pltpu.SemaphoreType.DMA((3, 4)),
        ]
        + [pltpu.SemaphoreType.DMA((2, 3))] * 2
        + [pltpu.SemaphoreType.DMA((slabs - 1,))] * 2
        + [pltpu.SemaphoreType.DMA((groups,))] * 4
        + [
            pltpu.VMEM((6, part, depth), F32),
            pltpu.VMEM((rows, part, depth), F32),
            pltpu.VMEM((slabs, 4, part + spare, depth), jnp.int16),
            pltpu.VMEM((count, groups, part + spare, depth), jnp.int16),
            pltpu.VMEM((count, groups, part + spare, depth), jnp.int16),
            pltpu.SemaphoreType.DMA,
        ]
        + [pltpu.SemaphoreType.DMA((slabs - 1,))] * 2
        + [pltpu.SemaphoreType.DMA((count - 1, groups))] * 2,
        compiler_params=pltpu.CompilerParams(
            vmem_limit_bytes=63 * 1024 * 1024, collective_id=1, has_side_effects=True
        ),
        name="whole",
    )(
        well_columns,
        obs_columns,
        obs_residuals[0],
        log_k,
        warm_adjoint[0],
        heads[0],
        jnp.asarray(turned_tables(depth, count)),
        jnp.asarray(filter_tables(rows, rows * slabs, width, depth, count)),
        jnp.asarray(np.concatenate([top, low, top], axis=1)),
        jnp.asarray(table(depth)),
    )


def pick(log_k, heads, warm_adjoint, obs_columns, *rest):
    rows, width, depth = log_k.shape
    count = lax.axis_size("test")
    fits = depth == 128 and count == 4 and rows % 8 == 0 and rows >= 16 and width % 96 == 0
    fits = fits and obs_columns.shape[1] % 64 == 0 and rows * width <= 48 * 288
    run = fast if fits and lax.axis_size("space") > 1 else on_device
    return run(log_k, heads, warm_adjoint, obs_columns, *rest)


def solution(mesh):
    placed = (
        P(("groups", "space"), None, None),
        P("test", ("groups", "space"), None, None),
        P("test", ("groups", "space"), None, None),
        P("test", "groups"),
        P("test", "groups", None),
        P(("groups", "test")),
    )
    return jax.shard_map(
        pick,
        mesh=mesh,
        in_specs=placed,
        out_specs=P(("groups", "space"), "test", None),
        check_vma=False,
    )
```

```python
import jax
import jax.numpy as jnp
import numpy as np
from jax import lax
from jax.experimental import pallas as pl
from jax.experimental.pallas import tpu as pltpu
from jax.sharding import PartitionSpec as P

ITERS = 2


prior_gain = 5.0
range_squared = 4.0


def with_halo(cells, sides, width):
    for axis, dim in sides:
        count = lax.axis_size(axis)
        ends = count - 1
        head = lax.slice_in_dim(cells, 0, width, axis=dim)
        tail = lax.slice_in_dim(cells, cells.shape[dim] - width, cells.shape[dim], axis=dim)
        cells = jnp.concatenate(
            [
                lax.ppermute(tail, axis, [(i, (i + 1) % count) for i in range(ends)]),
                cells,
                lax.ppermute(head, axis, [((i + 1) % count, i) for i in range(ends)]),
            ],
            axis=dim,
        )
    return cells


def neighbours(padded):
    return [
        padded[2:, 1:-1, 1:-1],
        padded[:-2, 1:-1, 1:-1],
        padded[1:-1, 2:, 1:-1],
        padded[1:-1, :-2, 1:-1],
        padded[1:-1, 1:-1, 2:],
        padded[1:-1, 1:-1, :-2],
    ]


def operate(values, padded, conduct):
    summed = jnp.zeros_like(values)
    for face_k, beside in zip(conduct, neighbours(padded)):
        summed = summed + face_k * (values - beside)
    return summed


def kappa_of(indices, length):
    return 4.0 * jnp.sin(jnp.pi * indices / length) ** 2


def pad_sides(padded):
    return jnp.pad(padded, ((0, 0), (1, 1), (1, 1)))


def with_faces(values):
    return pad_sides(with_halo(values, (("space", 0),), 1))


def squares(residual):
    return lax.psum(jnp.sum(residual * residual), "space")


def hartley(length):
    indices = jnp.arange(length, dtype=jnp.int32)
    products = indices[:, None] * indices[None, :] % length
    angles = products.astype(jnp.float32) * (2.0 * jnp.pi / length)
    return jnp.cos(angles) + jnp.sin(angles)


def on_device(log_k, heads, warm_adjoint, obs_columns, obs_residuals, well_columns):
    slab_rows, width_cells, depth_cells = log_k.shape
    space_count = lax.axis_size("space")
    first_row = lax.axis_index("space") * slab_rows
    logk_pad, head_pad = (
        with_halo(log_k, (("space", 0),), 1),
        with_halo(heads[0], (("space", 0),), 1),
    )
    logk_val = log_k.astype(jnp.float32)
    conduct = [
        jnp.exp(0.5 * (logk_val + beside))
        for beside in neighbours(pad_sides(logk_pad.astype(jnp.float32)))
    ]
    columns = obs_columns[0]
    row_local = columns // width_cells - first_row
    inside = (row_local >= 0) & (row_local < slab_rows)
    row_local = jnp.where(inside, row_local, slab_rows)
    source = jnp.zeros((slab_rows, width_cells, depth_cells), jnp.float32)
    source = source.at[row_local, columns % width_cells].add(obs_residuals[0], mode="drop")
    adjoint = warm_adjoint[0].astype(jnp.float32)
    lam_padded = with_faces(adjoint)
    residual = source - operate(adjoint, lam_padded, conduct)
    direction = residual
    norm_now = squares(residual)
    for iteration in range(ITERS):
        dir_padded = with_faces(direction)
        applied = operate(direction, dir_padded, conduct)
        step_length = norm_now / lax.psum(jnp.sum(direction * applied), "space")
        adjoint = adjoint + step_length * direction
        lam_padded = lam_padded + step_length * dir_padded
        if iteration + 1 < ITERS:
            residual = residual - step_length * applied
            norm_next = squares(residual)
            direction = residual + norm_next / norm_now * direction
            norm_now = norm_next
    lam_full = pad_sides(with_halo(adjoint, (("space", 0),), 1))
    head_val = heads[0].astype(jnp.float32)
    misfit_term = jnp.zeros_like(adjoint)
    for face_k, lam_side, head_side in zip(
        conduct, neighbours(lam_full), neighbours(pad_sides(head_pad.astype(jnp.float32)))
    ):
        misfit_term = misfit_term + face_k * (adjoint - lam_side) * (head_val - head_side)
    column_ids = (first_row + jnp.arange(slab_rows, dtype=jnp.int32))[
        :, None
    ] * width_cells + jnp.arange(width_cells, dtype=jnp.int32)[None, :]
    keep_mask = (column_ids != well_columns[0]).astype(jnp.float32)
    partial_value = -0.5 * misfit_term * keep_mask[:, :, None]
    highest = lax.Precision.HIGHEST
    cas_depth = hartley(depth_cells)
    cas_across = hartley(width_cells)
    along_cells = slab_rows * space_count
    cas_along = hartley(along_cells)
    summed = lax.psum_scatter(partial_value, "test", scatter_dimension=1, tiled=True)
    depth_freq = jnp.einsum("xyz,zk->xky", summed, cas_depth, precision=highest)
    pencil = lax.all_to_all(depth_freq, "test", split_axis=1, concat_axis=2, tiled=True)
    across_freq = jnp.einsum("xzy,yk->kzx", pencil, cas_across, precision=highest)
    column_block = lax.all_to_all(across_freq, "space", split_axis=0, concat_axis=2, tiled=True)
    along_freq = jnp.einsum("yzx,xk->yzk", column_block, cas_along, precision=highest)
    across_rows = column_block.shape[0]
    depth_rows = column_block.shape[1]
    kappa_x = kappa_of(jnp.arange(along_cells).astype(jnp.float32), along_cells)
    kappa_y = kappa_of(
        (lax.axis_index("space") * across_rows + jnp.arange(across_rows)).astype(jnp.float32),
        width_cells,
    )
    kappa_z = kappa_of(
        (lax.axis_index("test") * depth_rows + jnp.arange(depth_rows)).astype(jnp.float32),
        depth_cells,
    )
    spectrum = (
        prior_gain
        / (
            1.0
            + range_squared
            * (kappa_y[:, None, None] + kappa_z[None, :, None] + kappa_x[None, None, :])
        )
        ** 2
    )
    along_back = jnp.einsum("yzk,kx->yzx", along_freq * spectrum, cas_along, precision=highest)
    slab_block = lax.all_to_all(along_back, "space", split_axis=2, concat_axis=0, tiled=True)
    across_back = jnp.einsum("yzx,yk->xzk", slab_block, cas_across, precision=highest)
    depth_block = lax.all_to_all(across_back, "test", split_axis=2, concat_axis=1, tiled=True)
    result = jnp.einsum("xky,kz->xyz", depth_block, cas_depth, precision=highest)
    scale_back = 1.0 / (along_cells * width_cells * depth_cells)
    return result * scale_back


GUARD = 8
RING = 6
STEP = 256.0
TOP = 32000.0
HALF_LOG = 0.5 / float(np.log(2.0))
BF = jnp.bfloat16
F32 = jnp.float32
VM = pl.BlockSpec(memory_space=pltpu.VMEM)
SM = pl.BlockSpec(memory_space=pltpu.SMEM)
ANY = pl.BlockSpec(memory_space=pl.ANY)
MESH = pl.DeviceIdType.MESH


def shape(*dims, dtype=jnp.float32):
    return jax.ShapeDtypeStruct(dims, dtype)


def iota(plane, axis):
    return lax.broadcasted_iota(jnp.int32, plane, axis)


def halves(values):
    top = values.astype(BF)
    return top, (values - top.astype(F32)).astype(BF)


def matmul(a, b):
    return jnp.dot(a, b, preferred_element_type=F32)


def encode(values, spare):
    rows, lanes = values.shape
    peak = jnp.maximum(jnp.max(jnp.abs(values), axis=0, keepdims=True), 1e-30)
    level = jnp.ceil(jnp.log2(peak) * STEP)
    scaled = jnp.round(values * (jnp.exp2(level * (-1.0 / STEP)) * TOP))
    both = jnp.concatenate([scaled, jnp.broadcast_to(level, (spare, lanes))], axis=0)
    return both.astype(jnp.int32).astype(jnp.int16)


def decode(codes, spare):
    wide = codes.astype(jnp.int32).astype(F32)
    rows = wide.shape[0] - spare
    level = wide[rows : rows + 1]
    return wide[:rows] * (jnp.exp2(level * (1.0 / STEP)) * (1.0 / TOP))


def swap_blocks(planes):
    planes = list(planes)
    count = len(planes)
    lanes = planes[0].shape[1]
    block = lanes // count
    at_block = iota(planes[0].shape, 1) // block
    span = 1
    while span < count:
        odd = (at_block // span) % 2 == 1
        for low in range(count):
            if (low // span) % 2 == 0:
                first, second = planes[low], planes[low + span]
                up = pltpu.roll(second, block * span, 1)
                down = pltpu.roll(first, lanes - block * span, 1)
                planes[low] = jnp.where(odd, up, first)
                planes[low + span] = jnp.where(odd, second, down)
        span *= 2
    return planes


def greet(others):
    barrier = pltpu.get_barrier_semaphore()
    for other in others:
        pl.semaphore_signal(barrier, inc=1, device_id=other, device_id_type=MESH)
    pl.semaphore_wait(barrier, len(others))


def whole_kernel(
    well,
    columns,
    observed,
    logk,
    warm,
    heads,
    turned,
    beside_lanes,
    listed,
    cas_across,
    cas_depth,
    out,
    lk,
    wm,
    level_ends,
    soft,
    res,
    img,
    ring,
    sources,
    acc,
    shared,
    mine,
    from_mate,
    ship,
    got,
    load_sem,
    halo_send,
    halo_take,
    send_sum,
    take_sum,
    send_mate,
    take_mate,
    send_across,
    take_across,
    tables,
    freq,
    moments,
    going,
    coming,
    table_sem,
    send_end,
    take_end,
    send_back,
    take_back,
):
    rows, width, depth = logk.shape
    parts = 4
    chunk = rows // parts
    piece = width // 3
    pieces = range(3)
    slabs = shared.shape[0]
    slab, here = lax.axis_index("space"), lax.axis_index("test")
    half, core = here // 2, lax.rem(here, 2)
    mate = {"test": 2 * half + 1 - core}
    across = {"test": 2 * (1 - half) + core}
    others = [{"space": lax.rem(slab + k, slabs)} for k in range(1, slabs)]
    first_row = slab * rows

    def loads(m):
        span = pl.ds(m * chunk, chunk)
        to = pl.ds(3 + m * chunk, chunk)
        return [
            pltpu.make_async_copy(frm.at[span], held.at[to], load_sem.at[n, m])
            for n, (frm, held) in enumerate(((logk, lk), (warm, wm)))
        ]

    for m in range(parts):
        for copy in loads(m):
            copy.start()

    def halo(direction):
        up = direction == 1
        copies = []
        for n, (frm, held, deep) in enumerate(((logk, lk, 3), (warm, wm, 3), (heads, level_ends, 1))):
            at = rows - deep if up else 0
            to = 3 - deep if up else 3 + rows
            if deep == 1:
                to = 0 if up else 1
            copies.append(
                pltpu.make_async_remote_copy(
                    src_ref=frm.at[pl.ds(at, deep)],
                    dst_ref=held.at[pl.ds(to, deep)],
                    send_sem=halo_send.at[direction, n],
                    recv_sem=halo_take.at[direction, n],
                    device_id={"space": slab + 1 if up else slab - 1},
                    device_id_type=MESH,
                )
            )
        return copies

    count = 4
    peers = [lax.rem(here + k, count) for k in range(1, count)]
    fetch = pltpu.make_async_copy(listed.at[here], tables, table_sem)
    fetch.start()
    greet(others + [{"test": peer} for peer in peers])

    @pl.when(slab > 0)
    def _():
        for copy in halo(0):
            copy.start()

    @pl.when(slab < slabs - 1)
    def _():
        for copy in halo(1):
            copy.start()

    blank = jnp.zeros((3, width, depth), BF)

    @pl.when(slab == 0)
    def _():
        lk[0:3] = blank
        wm[0:3] = blank
        level_ends[0] = blank[0]

    @pl.when(slab == slabs - 1)
    def _():
        lk[rows + 3 : rows + 6] = blank
        wm[rows + 3 : rows + 6] = blank
        level_ends[1] = blank[0]

    top, low = halves(observed[...])
    sources[...] = jnp.concatenate([top, low], axis=0)
    acc[...] = jnp.zeros_like(acc)
    edge = jnp.zeros((GUARD, depth), F32)
    for i in range(ring.shape[0]):
        ring[i, 0:GUARD, :] = edge
        ring[i, width + GUARD : width + 2 * GUARD, :] = edge

    at_lane = iota((piece, depth), 1)
    at_row = iota((piece, depth), 0)
    is_first, is_last = at_lane == 0, at_lane == depth - 1
    spots = iota((width, 2 * columns.shape[1]), 0)

    def at(c):
        return pl.ds(c * piece, piece)

    def near(ref, i, c, off=0):
        return ref[i, pl.ds(GUARD + c * piece + off, piece), :]

    def store(ref, i, c, value):
        ref[i, pl.ds(GUARD + c * piece, piece), :] = value

    def ahead(value):
        return pltpu.roll(value, depth - 1, 1)

    def behind(value):
        return pltpu.roll(value, 1, 1)

    def ring_sum(held, ends, sides, outer):
        lanes = jnp.where(is_last, outer, ahead(held)) + jnp.where(is_first, outer, behind(held))
        return (lanes + ends) + sides

    def beside(ref, below, i, above, c, outer):
        held = near(ref, i, c)
        ends = near(ref, i, c, -1) + near(ref, i, c, 1)
        return held, ring_sum(held, ends, near(ref, below, c) + near(ref, above, c), outer)

    def around_slot(n, base, c):
        return beside(ring, base + (n - 1) % 4, base + n % 4, base + (n + 1) % 4, c, 0.0)

    def partial(value):
        return jnp.sum(value.reshape(piece // 8, 8, depth), axis=0)

    def clear(n, store_zero):
        if n < 3:
            pl.when(slab == 0)(store_zero)
        if n >= rows + 3:
            pl.when(slab == slabs - 1)(store_zero)

    blank_piece = jnp.zeros((piece, depth), F32)

    def prepare(at_row_base, views, n, static):
        soft_v, _, _, lk_v, wm_v = views
        one = jnp.ones((GUARD, depth), F32)
        soft_v[n, 0:GUARD, :] = one
        soft_v[n, width + GUARD : width + 2 * GUARD, :] = one
        for c in pieces:
            value = jnp.exp2(HALF_LOG * lk_v[n, at(c), :].astype(F32))
            store(soft_v, n, c, value)
            store(ring, n % 4, c, value * wm_v[n, at(c), :].astype(F32))

    def residual(at_row_base, views, n, static):
        soft_v, res_v = views[:2]
        spot = spots_at - (first_row + at_row_base + n - 3) * width
        hits = jnp.where(spots == spot, 1.0, 0.0).astype(BF)
        source = matmul(hits, sources[...])
        for c in pieces:
            s, around = beside(soft_v, n - 1, n, n + 1, c, 1.0)
            held, total = around_slot(n, 0, c)
            value = (s * total - held * around) + source[c * piece : (c + 1) * piece]
            res_v[n, at(c), :] = value
            store(ring, 4 + n % 4, c, s * value)
            store(ring, 12 + n % 4, c, around)

        def store_zero():
            for c in pieces:
                res_v[n, at(c), :] = blank_piece
                store(ring, 4 + n % 4, c, blank_piece)

        if static:
            clear(n, store_zero)

    def image(at_row_base, views, n, static, sums):
        soft_v, res_v, img_v = views[:3]
        plane = ring[4 + n % 4, pl.ds(GUARD, width), :]
        lanes = matmul(jnp.concatenate(halves(plane), axis=1), beside_lanes[...])
        for c in pieces:
            held = near(ring, 4 + n % 4, c)
            ends = near(ring, 4 + n % 4, c, -1) + near(ring, 4 + n % 4, c, 1)
            sides = near(ring, 4 + (n - 1) % 4, c) + near(ring, 4 + (n + 1) % 4, c)
            total = (lanes[c * piece : (c + 1) * piece] + ends) + sides
            s, value = near(soft_v, n, c), res_v[n, at(c), :]
            applied = held * near(ring, 12 + n % 4, c) - s * total
            img_v[n, at(c), :] = applied
            store(ring, 8 + n % 4, c, s * applied)
            if sums is not None:
                sums[0].append(partial(value * value))
                sums[1].append(partial(value * applied))

        def store_zero():
            for c in pieces:
                img_v[n, at(c), :] = blank_piece
                store(ring, 8 + n % 4, c, blank_piece)

        if static:
            clear(n, store_zero)

    def twice(at_row_base, views, n, sums):
        img_v = views[2]
        for c in pieces:
            held, value = near(ring, 8 + n % 4, c), img_v[n, at(c), :]
            after = near(ring, 8 + (n + 1) % 4, c) + near(ring, 8 + n % 4, c, 1)
            after = after + jnp.where(is_last, 0.0, ahead(held))
            sums[2].append(partial(value * value))
            sums[3].append(partial(held * (value * near(ring, 12 + n % 4, c) - 2.0 * after)))

    def keep(sums):
        for n, terms in enumerate(sums):
            if terms:
                acc[n] += sum(terms[1:], terms[0])

    whole = (soft, res, img, lk, wm)

    def walk(first, last, r_rows, q_rows, q_own, t_rows):
        sums = [[], [], [], []]
        for k in range(first, last + 1):
            if k < rows + 6 and k <= r_rows[1] + 1:
                prepare(0, whole, k, True)
            if r_rows[0] <= k - 2 <= r_rows[1]:
                residual(0, whole, k - 2, True)
            if q_rows[0] <= k - 4 <= q_rows[1]:
                own = q_own[0] <= k - 4 <= q_own[1]
                image(0, whole, k - 4, True, sums if own else None)
            if t_rows[0] <= k - 5 <= t_rows[1]:
                twice(0, whole, k - 5, sums)
        keep(sums)

    def steady(j, _):
        base = 4 + 4 * j
        views = [ref.at[pl.ds(base, 11)] for ref in whole]
        sums = [[], [], [], []]
        for u in range(4):
            prepare(base, views, 7 + u, False)
            residual(base, views, 5 + u, False)
            image(base, views, 3 + u, False, sums)
            twice(base, views, 2 + u, sums)
        keep(sums)
        return 0

    spots_at = jnp.concatenate([columns[...], columns[...]], axis=1)
    for copy in loads(0):
        copy.wait()
    last = rows + 2
    walk(3, 10, (4, last + 2), (5, last + 1), (5, last), (6, last))
    for m in range(1, parts):
        for copy in loads(m):
            copy.wait()
    lax.fori_loop(0, (rows - 8) // 4, steady, 0)

    @pl.when(slab < slabs - 1)
    def _():
        for copy in halo(0):
            copy.wait_recv()

    walk(rows + 3, rows + 8, (4, last + 2), (5, last + 1), (5, last), (6, last))

    @pl.when(slab > 0)
    def _():
        for copy in halo(1):
            copy.wait_recv()

    walk(0, 10, (1, 7), (2, 6), (3, 4), (3, 5))

    levels_in = pltpu.make_async_copy(heads, lk.at[pl.ds(3, rows)], load_sem.at[0, 0])
    levels_in.start()
    lk[2] = level_ends[0]
    lk[rows + 3] = level_ends[1]
    shared[slab] = acc[...]
    copies = [
        pltpu.make_async_remote_copy(
            src_ref=shared.at[slab],
            dst_ref=shared.at[slab],
            send_sem=send_sum.at[k],
            recv_sem=take_sum.at[k],
            device_id=other,
            device_id_type=MESH,
        )
        for k, other in enumerate(others)
    ]
    for copy in copies:
        copy.start()

    @pl.when(slab > 0)
    def _():
        for copy in halo(0):
            copy.wait_send()

    @pl.when(slab < slabs - 1)
    def _():
        for copy in halo(1):
            copy.wait_send()

    for copy in copies:
        copy.wait()
    levels_in.wait()

    def gathered(n):
        total = shared[0, n]
        for m in range(1, slabs):
            total = total + shared[m, n]
        return jnp.broadcast_to(jnp.sum(total, axis=(0, 1), keepdims=True), (1, depth))

    norm, curve, square, bend = [gathered(n) for n in range(4)]
    length = norm / curve
    norm_next = length * length * square - norm
    curve_next = curve - 2.0 * length * square + length * length * bend
    ratio = norm_next / norm
    length_next = norm_next / (curve_next - ratio * norm_next / length)
    with_start = length + length_next * (1.0 + ratio)
    with_image = length_next * length

    def eighth(n, base):
        return base + lax.rem(n, 8)

    def fill(n):
        for c in pieces:
            field = wm[n, at(c), :].astype(F32)
            field = field + (with_start * res[n, at(c), :] - with_image * img[n, at(c), :])
            store(ring, eighth(n, 0), c, field)
            store(ring, eighth(n, 8), c, lk[n, at(c), :].astype(F32))

    fill(2)
    fill(3)
    groups = rows // count
    at_block = at_lane // (depth // count)

    def turn(g):
        return lax.rem(g, RING)

    def group(g):
        start = 3 + count * g
        for p in range(count):
            fill(start + p + 1)
        for c in pieces:
            fields = [near(ring, eighth(start + p, 0), c) for p in range(-1, count + 1)]
            levels = [near(ring, eighth(start + p, 8), c) for p in range(-1, count + 1)]
            steps = [
                (fields[p] - fields[p + 1]) * (levels[p] - levels[p + 1]) for p in range(count + 1)
            ]
            turns = []
            for p in range(count):
                n = start + p
                f, h, s = fields[p + 1], levels[p + 1], near(soft, n, c)
                total = near(soft, n - 1, c) * steps[p] + near(soft, n + 1, c) * steps[p + 1]
                for off in (-1, 1):
                    field = near(ring, eighth(n, 0), c, off)
                    level = near(ring, eighth(n, 8), c, off)
                    total += near(soft, n, c, off) * ((f - field) * (h - level))
                both = f * h
                product = (f - ahead(f)) * (h - ahead(h))
                total += jnp.where(is_last, both, ahead(s) * product)
                total += jnp.where(is_first, both, behind(s * product))
                place = well[0] - (first_row + n - 3) * width - c * piece
                value = jnp.where(at_row != place, s * total, 0.0)
                double = matmul(jnp.concatenate(halves(value), axis=1), turned[p])
                turns.append(double[:, :depth] + double[:, depth:])
            for t in range(count):
                joined = turns[-t % count]
                for b in range(1, count):
                    joined = jnp.where(at_block == b, turns[(b - t) % count], joined)
                mine[t % 2, turn(g), t // 2, at(c), :] = joined

    def to_mate(g):
        return pltpu.make_async_remote_copy(
            src_ref=mine.at[1 - core, turn(g)],
            dst_ref=from_mate.at[g],
            send_sem=send_mate.at[g],
            recv_sem=take_mate.at[g],
            device_id=mate,
            device_id_type=MESH,
        )

    def to_across(g):
        return pltpu.make_async_remote_copy(
            src_ref=ship.at[turn(g)],
            dst_ref=got.at[g],
            send_sem=send_across.at[g],
            recv_sem=take_across.at[g],
            device_id=across,
            device_id_type=MESH,
        )

    def relay(g):
        to_mate(g).wait_recv()
        ship[turn(g)] = encode(mine[core, turn(g), 1 - half] + from_mate[g, 1 - half], 16)
        to_across(g).start()

    part = width // count
    spare = going.shape[2] - part
    lanes = depth
    filtered = res.at[:, pl.ds(0, part)]

    def settle(g):
        to_across(g).wait_recv()
        to_mate(g).wait_send()
        to_across(g).wait_send()

    def absorb(g):
        summed = (mine[core, turn(g), half] + from_mate[g, half]) + decode(got[g], 16)
        top, low = halves(summed)
        mixed = matmul(cas_across[...], jnp.concatenate([top, top, low], axis=0))
        blocks = [mixed[j * part : (j + 1) * part] for j in range(count)]
        for p, plane in enumerate(swap_blocks(blocks)):
            freq[g * count + lax.rem(p - here + count, count)] = plane

    lag = 4

    def early(g, _):
        group(g)
        to_mate(g).start()
        relay(g - 1)
        return 0

    def late(g, _):
        settle(g - lag)
        absorb(g - lag)
        group(g)
        to_mate(g).start()
        relay(g - 1)
        return 0

    group(0)
    to_mate(0).start()
    lax.fori_loop(1, lag, early, 0)
    lax.fori_loop(lag, groups, late, 0)
    relay(groups - 1)

    def finish(g, _):
        settle(g)
        absorb(g)
        return 0

    lax.fori_loop(groups - lag, groups, finish, 0)
    fetch.wait()
    pole, level, slope, decay, wrap_one, wrap_two = (tables[n] for n in range(6))

    def gather(i, carry):
        one, two, back_one, back_two = carry
        value, back = freq[i], freq[rows - 1 - i]
        return (
            value + pole * one,
            pole * (two + one),
            back + pole * back_one,
            pole * (back_two + back_one),
        )

    zero = jnp.zeros((part, lanes), jnp.float32)
    ends = lax.fori_loop(0, rows, gather, (zero, zero, zero, zero))
    for n in range(4):
        moments[slab, n] = encode(ends[n], spare)
    copies = [
        pltpu.make_async_remote_copy(
            src_ref=moments.at[slab],
            dst_ref=moments.at[slab],
            send_sem=send_end.at[k],
            recv_sem=take_end.at[k],
            device_id=other,
            device_id_type=MESH,
        )
        for k, other in enumerate(others)
    ]
    for copy in copies:
        copy.start()
    for copy in copies:
        copy.wait()

    def carried(direction, n):
        one, two = zero, zero
        for m in range(slabs, 0, -1):
            other = lax.rem(slab + 2 * slabs - direction * m, slabs)
            one, two = (
                decay * one + decode(moments[other, n], spare),
                decay * (two + rows * one) + decode(moments[other, n + 1], spare),
            )
        return wrap_one * one, wrap_one * two + wrap_two * one

    def forward(i, carry):
        one, two = carry
        two = pole * (two + one)
        one = freq[i] + pole * one
        filtered[i] = level * one + slope * two
        return one, two

    lax.fori_loop(0, rows, forward, carried(1, 0))

    def backward(i, carry):
        one, two = carry
        at = rows - 1 - i
        two = pole * (two + one)
        one = pole * one
        filtered[at] += level * one + slope * two
        return one + freq[at], two

    lax.fori_loop(0, rows, backward, carried(-1, 2))

    def to_peer(k, g):
        return pltpu.make_async_remote_copy(
            src_ref=going.at[peers[k], g],
            dst_ref=coming.at[here, g],
            send_sem=send_back.at[k, g],
            recv_sem=take_back.at[k, g],
            device_id={"test": peers[k]},
            device_id_type=MESH,
        )

    pair = 2

    def unmix(j, _):
        both = []
        for g in [pair * j + n for n in range(pair)]:
            blocks = swap_blocks([filtered[g * count + p] for p in range(count)])
            top, low = halves(jnp.concatenate(blocks, axis=0))
            both.append(jnp.concatenate([top, top, low], axis=0))
        mixed = matmul(cas_across[...], jnp.concatenate(both, axis=1))
        for n in range(pair):
            for u in range(count):
                block = mixed[u * part : (u + 1) * part, n * lanes : (n + 1) * lanes]
                going[u, pair * j + n] = encode(block, spare)
        for g in [pair * j + n for n in range(pair)]:
            for k in range(count - 1):
                to_peer(k, g).start()
            coming[here, g] = going[here, g]
        return 0

    lax.fori_loop(0, groups // pair, unmix, 0)

    def back(j, _):
        for g in [pair * j + n for n in range(pair)]:
            for k in range(count - 1):
                to_peer(k, g).wait()
        for g in [pair * j + n for n in range(pair)]:
            planes = [decode(coming[t, g], spare) for t in range(count)]
            for p, plane in enumerate(swap_blocks(planes)):
                double = matmul(jnp.concatenate(halves(plane), axis=1), cas_depth[...])
                out[g * count + p] = double[:, :lanes] + double[:, lanes:]
        return 0

    lax.fori_loop(0, groups // pair, back, 0)


def table(length):
    indices = np.arange(length)
    angles = (indices[:, None] * indices[None, :] % length) * (2.0 * np.pi / length)
    return (np.cos(angles) + np.sin(angles)).astype(np.float32)


def split(values):
    top = values.astype(jnp.bfloat16)
    return top, (values - top.astype(np.float32)).astype(jnp.bfloat16)


def doubled_table(values):
    top, low = split(values)
    return np.block([[top, low], [top, np.zeros_like(low)]])


def turned_tables(length, count):
    tables = []
    for p in range(count):
        tables.append(doubled_table(-0.5 * np.roll(table(length), p * (length // count), axis=1)))
    return np.stack(tables)


def filter_tables(rows, along, width, depth, count):
    def kappa(length):
        return 4.0 * np.sin(np.pi * np.arange(length) / length) ** 2

    part, block = width // count, depth // count
    lanes_at = np.arange(depth)
    across_at = (lanes_at // block)[None, :] * part + np.arange(part)[:, None]
    listed = []
    for here in range(count):
        depth_at = here * block + lanes_at % block
        shift = 1.0 + range_squared * (kappa(width)[across_at] + kappa(depth)[depth_at][None, :])
        centre = 1.0 + shift / (2.0 * range_squared)
        pole = 1.0 / (centre + np.sqrt(centre * centre - 1.0))
        square = pole * pole
        gain = prior_gain / (range_squared * range_squared) * square / (width * depth)
        slope = gain / (1.0 - square) ** 2
        level = slope * (1.0 + square) / (1.0 - square)
        turn = pole**along
        wrap_one = 1.0 / (1.0 - turn)
        wrap_two = along * turn * wrap_one * wrap_one
        listed.append(np.stack([pole, level, slope, pole**rows, wrap_one, wrap_two]))
    return np.stack(listed).astype(np.float32)


def fast(log_k, heads, warm_adjoint, obs_columns, obs_residuals, well_columns):
    rows, width, depth = log_k.shape
    slabs = lax.axis_size("space")
    count = lax.axis_size("test")
    part = width // count
    groups = rows // count
    observed = obs_columns.shape[1]
    planes = rows + 6
    padded = width + 2 * GUARD
    spare = 16 - part % 16
    top, low = split(table(width))
    return pl.pallas_call(
        whole_kernel,
        out_shape=shape(rows, part, depth),
        in_specs=[SM, VM, VM, ANY, ANY, ANY, VM, VM, ANY, VM, VM],
        out_specs=VM,
        scratch_shapes=[pltpu.VMEM((planes, width, depth), BF)] * 2
        + [
            pltpu.VMEM((2, width, depth), BF),
            pltpu.VMEM((planes, padded, depth), F32),
            pltpu.VMEM((planes, width, depth), F32),
            pltpu.VMEM((planes, width, depth), F32),
            pltpu.VMEM((16, padded, depth), F32),
            pltpu.VMEM((2 * observed, depth), BF),
            pltpu.VMEM((4, 8, depth), F32),
            pltpu.VMEM((slabs, 4, 8, depth), F32),
            pltpu.VMEM((2, RING, 2, width, depth), F32),
            pltpu.VMEM((groups, 2, width, depth), F32),
            pltpu.VMEM((RING, width + 16, depth), jnp.int16),
            pltpu.VMEM((groups, width + 16, depth), jnp.int16),
            pltpu.SemaphoreType.DMA((2, 4)),
        ]
        + [pltpu.SemaphoreType.DMA((2, 3))] * 2
        + [pltpu.SemaphoreType.DMA((slabs - 1,))] * 2
        + [pltpu.SemaphoreType.DMA((groups,))] * 4
        + [
            pltpu.VMEM((6, part, depth), F32),
            pltpu.VMEM((rows, part, depth), F32),
            pltpu.VMEM((slabs, 4, part + spare, depth), jnp.int16),
            pltpu.VMEM((count, groups, part + spare, depth), jnp.int16),
            pltpu.VMEM((count, groups, part + spare, depth), jnp.int16),
            pltpu.SemaphoreType.DMA,
        ]
        + [pltpu.SemaphoreType.DMA((slabs - 1,))] * 2
        + [pltpu.SemaphoreType.DMA((count - 1, groups))] * 2,
        compiler_params=pltpu.CompilerParams(
            vmem_limit_bytes=60 * 1024 * 1024, collective_id=1, has_side_effects=True
        ),
        name="whole",
    )(
        well_columns,
        obs_columns,
        obs_residuals[0],
        log_k,
        warm_adjoint[0],
        heads[0],
        jnp.asarray(turned_tables(depth, count)),
        jnp.asarray(np.tile(np.eye(depth, k=1) + np.eye(depth, k=-1), (2, 1)), BF),
        jnp.asarray(filter_tables(rows, rows * slabs, width, depth, count)),
        jnp.asarray(np.concatenate([top, low, top], axis=1)),
        jnp.asarray(doubled_table(table(depth))),
    )


def pick(log_k, heads, warm_adjoint, obs_columns, *rest):
    rows, width, depth = log_k.shape
    count = lax.axis_size("test")
    fits = depth == 128 and count == 4 and rows % 8 == 0 and rows >= 16 and width % 96 == 0
    fits = fits and obs_columns.shape[1] % 64 == 0 and rows * width <= 48 * 288
    run = fast if fits and lax.axis_size("space") > 1 else on_device
    return run(log_k, heads, warm_adjoint, obs_columns, *rest)


def solution(mesh):
    placed = (
        P(("groups", "space"), None, None),
        P("test", ("groups", "space"), None, None),
        P("test", ("groups", "space"), None, None),
        P("test", "groups"),
        P("test", "groups", None),
        P(("groups", "test")),
    )
    return jax.shard_map(
        pick,
        mesh=mesh,
        in_specs=placed,
        out_specs=P(("groups", "space"), "test", None),
        check_vma=False,
    )
```

```python
import jax
import jax.numpy as jnp
import numpy as np
from jax import lax
from jax.experimental import pallas as pl
from jax.experimental.pallas import tpu as pltpu
from jax.sharding import PartitionSpec as P

ITERS = 2


prior_gain = 5.0
range_squared = 4.0


def with_halo(cells, sides, width):
    for axis, dim in sides:
        count = lax.axis_size(axis)
        ends = count - 1
        head = lax.slice_in_dim(cells, 0, width, axis=dim)
        tail = lax.slice_in_dim(cells, cells.shape[dim] - width, cells.shape[dim], axis=dim)
        cells = jnp.concatenate(
            [
                lax.ppermute(tail, axis, [(i, (i + 1) % count) for i in range(ends)]),
                cells,
                lax.ppermute(head, axis, [((i + 1) % count, i) for i in range(ends)]),
            ],
            axis=dim,
        )
    return cells


def neighbours(padded):
    return [
        padded[2:, 1:-1, 1:-1],
        padded[:-2, 1:-1, 1:-1],
        padded[1:-1, 2:, 1:-1],
        padded[1:-1, :-2, 1:-1],
        padded[1:-1, 1:-1, 2:],
        padded[1:-1, 1:-1, :-2],
    ]


def operate(values, padded, conduct):
    summed = jnp.zeros_like(values)
    for face_k, beside in zip(conduct, neighbours(padded)):
        summed = summed + face_k * (values - beside)
    return summed


def kappa_of(indices, length):
    return 4.0 * jnp.sin(jnp.pi * indices / length) ** 2


def pad_sides(padded):
    return jnp.pad(padded, ((0, 0), (1, 1), (1, 1)))


def with_faces(values):
    return pad_sides(with_halo(values, (("space", 0),), 1))


def squares(residual):
    return lax.psum(jnp.sum(residual * residual), "space")


def hartley(length):
    indices = jnp.arange(length, dtype=jnp.int32)
    products = indices[:, None] * indices[None, :] % length
    angles = products.astype(jnp.float32) * (2.0 * jnp.pi / length)
    return jnp.cos(angles) + jnp.sin(angles)


def on_device(log_k, heads, warm_adjoint, obs_columns, obs_residuals, well_columns):
    slab_rows, width_cells, depth_cells = log_k.shape
    space_count = lax.axis_size("space")
    first_row = lax.axis_index("space") * slab_rows
    logk_pad, head_pad = (
        with_halo(log_k, (("space", 0),), 1),
        with_halo(heads[0], (("space", 0),), 1),
    )
    logk_val = log_k.astype(jnp.float32)
    conduct = [
        jnp.exp(0.5 * (logk_val + beside))
        for beside in neighbours(pad_sides(logk_pad.astype(jnp.float32)))
    ]
    columns = obs_columns[0]
    row_local = columns // width_cells - first_row
    inside = (row_local >= 0) & (row_local < slab_rows)
    row_local = jnp.where(inside, row_local, slab_rows)
    source = jnp.zeros((slab_rows, width_cells, depth_cells), jnp.float32)
    source = source.at[row_local, columns % width_cells].add(obs_residuals[0], mode="drop")
    adjoint = warm_adjoint[0].astype(jnp.float32)
    lam_padded = with_faces(adjoint)
    residual = source - operate(adjoint, lam_padded, conduct)
    direction = residual
    norm_now = squares(residual)
    for iteration in range(ITERS):
        dir_padded = with_faces(direction)
        applied = operate(direction, dir_padded, conduct)
        step_length = norm_now / lax.psum(jnp.sum(direction * applied), "space")
        adjoint = adjoint + step_length * direction
        lam_padded = lam_padded + step_length * dir_padded
        if iteration + 1 < ITERS:
            residual = residual - step_length * applied
            norm_next = squares(residual)
            direction = residual + norm_next / norm_now * direction
            norm_now = norm_next
    lam_full = pad_sides(with_halo(adjoint, (("space", 0),), 1))
    head_val = heads[0].astype(jnp.float32)
    misfit_term = jnp.zeros_like(adjoint)
    for face_k, lam_side, head_side in zip(
        conduct, neighbours(lam_full), neighbours(pad_sides(head_pad.astype(jnp.float32)))
    ):
        misfit_term = misfit_term + face_k * (adjoint - lam_side) * (head_val - head_side)
    column_ids = (first_row + jnp.arange(slab_rows, dtype=jnp.int32))[
        :, None
    ] * width_cells + jnp.arange(width_cells, dtype=jnp.int32)[None, :]
    keep_mask = (column_ids != well_columns[0]).astype(jnp.float32)
    partial_value = -0.5 * misfit_term * keep_mask[:, :, None]
    highest = lax.Precision.HIGHEST
    cas_depth = hartley(depth_cells)
    cas_across = hartley(width_cells)
    along_cells = slab_rows * space_count
    cas_along = hartley(along_cells)
    summed = lax.psum_scatter(partial_value, "test", scatter_dimension=1, tiled=True)
    depth_freq = jnp.einsum("xyz,zk->xky", summed, cas_depth, precision=highest)
    pencil = lax.all_to_all(depth_freq, "test", split_axis=1, concat_axis=2, tiled=True)
    across_freq = jnp.einsum("xzy,yk->kzx", pencil, cas_across, precision=highest)
    column_block = lax.all_to_all(across_freq, "space", split_axis=0, concat_axis=2, tiled=True)
    along_freq = jnp.einsum("yzx,xk->yzk", column_block, cas_along, precision=highest)
    across_rows = column_block.shape[0]
    depth_rows = column_block.shape[1]
    kappa_x = kappa_of(jnp.arange(along_cells).astype(jnp.float32), along_cells)
    kappa_y = kappa_of(
        (lax.axis_index("space") * across_rows + jnp.arange(across_rows)).astype(jnp.float32),
        width_cells,
    )
    kappa_z = kappa_of(
        (lax.axis_index("test") * depth_rows + jnp.arange(depth_rows)).astype(jnp.float32),
        depth_cells,
    )
    spectrum = (
        prior_gain
        / (
            1.0
            + range_squared
            * (kappa_y[:, None, None] + kappa_z[None, :, None] + kappa_x[None, None, :])
        )
        ** 2
    )
    along_back = jnp.einsum("yzk,kx->yzx", along_freq * spectrum, cas_along, precision=highest)
    slab_block = lax.all_to_all(along_back, "space", split_axis=2, concat_axis=0, tiled=True)
    across_back = jnp.einsum("yzx,yk->xzk", slab_block, cas_across, precision=highest)
    depth_block = lax.all_to_all(across_back, "test", split_axis=2, concat_axis=1, tiled=True)
    result = jnp.einsum("xky,kz->xyz", depth_block, cas_depth, precision=highest)
    scale_back = 1.0 / (along_cells * width_cells * depth_cells)
    return result * scale_back


GUARD = 8
RING = 6
STEP = 256.0
TOP = 32000.0
HALF_LOG = 0.5 / float(np.log(2.0))
BF = jnp.bfloat16
F32 = jnp.float32
VM = pl.BlockSpec(memory_space=pltpu.VMEM)
SM = pl.BlockSpec(memory_space=pltpu.SMEM)
ANY = pl.BlockSpec(memory_space=pl.ANY)
MESH = pl.DeviceIdType.MESH


def shape(*dims, dtype=jnp.float32):
    return jax.ShapeDtypeStruct(dims, dtype)


def iota(plane, axis):
    return lax.broadcasted_iota(jnp.int32, plane, axis)


def halves(values):
    top = values.astype(BF)
    return top, (values - top.astype(F32)).astype(BF)


def matmul(a, b):
    return jnp.dot(a, b, preferred_element_type=F32)


def encode(values, spare):
    rows, lanes = values.shape
    peak = jnp.maximum(jnp.max(jnp.abs(values), axis=0, keepdims=True), 1e-30)
    level = jnp.ceil(jnp.log2(peak) * STEP)
    scaled = jnp.round(values * (jnp.exp2(level * (-1.0 / STEP)) * TOP))
    both = jnp.concatenate([scaled, jnp.broadcast_to(level, (spare, lanes))], axis=0)
    return both.astype(jnp.int32).astype(jnp.int16)


def decode(codes, spare):
    wide = codes.astype(jnp.int32).astype(F32)
    rows = wide.shape[0] - spare
    level = wide[rows : rows + 1]
    return wide[:rows] * (jnp.exp2(level * (1.0 / STEP)) * (1.0 / TOP))


def swap_blocks(planes):
    planes = list(planes)
    count = len(planes)
    lanes = planes[0].shape[1]
    block = lanes // count
    at_block = iota(planes[0].shape, 1) // block
    span = 1
    while span < count:
        odd = (at_block // span) % 2 == 1
        for low in range(count):
            if (low // span) % 2 == 0:
                first, second = planes[low], planes[low + span]
                up = pltpu.roll(second, block * span, 1)
                down = pltpu.roll(first, lanes - block * span, 1)
                planes[low] = jnp.where(odd, up, first)
                planes[low + span] = jnp.where(odd, second, down)
        span *= 2
    return planes


def greet(others):
    barrier = pltpu.get_barrier_semaphore()
    for other in others:
        pl.semaphore_signal(barrier, inc=1, device_id=other, device_id_type=MESH)
    pl.semaphore_wait(barrier, len(others))


def whole_kernel(
    well,
    columns,
    observed,
    logk,
    warm,
    heads,
    turned,
    beside_lanes,
    listed,
    cas_across,
    cas_depth,
    out,
    lk,
    wm,
    level_ends,
    soft,
    res,
    img,
    ring,
    sources,
    acc,
    shared,
    mine,
    from_mate,
    ship,
    got,
    load_sem,
    halo_send,
    halo_take,
    send_sum,
    take_sum,
    send_mate,
    take_mate,
    send_across,
    take_across,
    tables,
    freq,
    moments,
    going,
    coming,
    table_sem,
    send_end,
    take_end,
    send_back,
    take_back,
    ends,
):
    rows, width, depth = logk.shape
    parts = 4
    chunk = rows // parts
    piece = width // 3
    pieces = range(3)
    slabs = shared.shape[0]
    slab, here = lax.axis_index("space"), lax.axis_index("test")
    half, core = here // 2, lax.rem(here, 2)
    mate = {"test": 2 * half + 1 - core}
    across = {"test": 2 * (1 - half) + core}
    others = [{"space": lax.rem(slab + k, slabs)} for k in range(1, slabs)]
    first_row = slab * rows

    def loads(m):
        span = pl.ds(m * chunk, chunk)
        to = pl.ds(3 + m * chunk, chunk)
        return [
            pltpu.make_async_copy(frm.at[span], held.at[to], load_sem.at[n, m])
            for n, (frm, held) in enumerate(((logk, lk), (warm, wm)))
        ]

    for m in range(parts):
        for copy in loads(m):
            copy.start()

    def halo(direction):
        up = direction == 1
        copies = []
        for n, (frm, held, deep) in enumerate(((logk, lk, 3), (warm, wm, 3), (heads, level_ends, 1))):
            at = rows - deep if up else 0
            to = 3 - deep if up else 3 + rows
            if deep == 1:
                to = 0 if up else 1
            copies.append(
                pltpu.make_async_remote_copy(
                    src_ref=frm.at[pl.ds(at, deep)],
                    dst_ref=held.at[pl.ds(to, deep)],
                    send_sem=halo_send.at[direction, n],
                    recv_sem=halo_take.at[direction, n],
                    device_id={"space": slab + 1 if up else slab - 1},
                    device_id_type=MESH,
                )
            )
        return copies

    count = 4
    peers = [lax.rem(here + k, count) for k in range(1, count)]
    fetch = pltpu.make_async_copy(listed.at[here], tables, table_sem)
    fetch.start()
    greet(others + [{"test": peer} for peer in peers])

    @pl.when(slab > 0)
    def _():
        for copy in halo(0):
            copy.start()

    @pl.when(slab < slabs - 1)
    def _():
        for copy in halo(1):
            copy.start()

    blank = jnp.zeros((3, width, depth), BF)

    @pl.when(slab == 0)
    def _():
        lk[0:3] = blank
        wm[0:3] = blank
        level_ends[0] = blank[0]

    @pl.when(slab == slabs - 1)
    def _():
        lk[rows + 3 : rows + 6] = blank
        wm[rows + 3 : rows + 6] = blank
        level_ends[1] = blank[0]

    top, low = halves(observed[...])
    sources[...] = jnp.concatenate([top, low], axis=0)
    acc[...] = jnp.zeros_like(acc)
    edge = jnp.zeros((GUARD, depth), F32)
    for i in range(ring.shape[0]):
        ring[i, 0:GUARD, :] = edge
        ring[i, width + GUARD : width + 2 * GUARD, :] = edge

    at_lane = iota((piece, depth), 1)
    at_row = iota((piece, depth), 0)
    is_first, is_last = at_lane == 0, at_lane == depth - 1
    spots = iota((width, 2 * columns.shape[1]), 0)

    def at(c):
        return pl.ds(c * piece, piece)

    def near(ref, i, c, off=0):
        return ref[i, pl.ds(GUARD + c * piece + off, piece), :]

    def store(ref, i, c, value):
        ref[i, pl.ds(GUARD + c * piece, piece), :] = value

    def ahead(value):
        return pltpu.roll(value, depth - 1, 1)

    def behind(value):
        return pltpu.roll(value, 1, 1)

    def ring_sum(held, ends, sides, outer):
        lanes = jnp.where(is_last, outer, ahead(held)) + jnp.where(is_first, outer, behind(held))
        return (lanes + ends) + sides

    def beside(ref, below, i, above, c, outer):
        held = near(ref, i, c)
        ends = near(ref, i, c, -1) + near(ref, i, c, 1)
        return held, ring_sum(held, ends, near(ref, below, c) + near(ref, above, c), outer)

    def around_slot(n, base, c):
        return beside(ring, base + (n - 1) % 4, base + n % 4, base + (n + 1) % 4, c, 0.0)

    def partial(value):
        return jnp.sum(value.reshape(piece // 8, 8, depth), axis=0)

    def clear(n, store_zero):
        if n < 3:
            pl.when(slab == 0)(store_zero)
        if n >= rows + 3:
            pl.when(slab == slabs - 1)(store_zero)

    blank_piece = jnp.zeros((piece, depth), F32)

    def prepare(at_row_base, views, n, static):
        soft_v, _, _, lk_v, wm_v = views
        one = jnp.ones((GUARD, depth), F32)
        soft_v[n, 0:GUARD, :] = one
        soft_v[n, width + GUARD : width + 2 * GUARD, :] = one
        for c in pieces:
            value = jnp.exp2(HALF_LOG * lk_v[n, at(c), :].astype(F32))
            store(soft_v, n, c, value)
            store(ring, n % 4, c, value * wm_v[n, at(c), :].astype(F32))

    def residual(at_row_base, views, n, static):
        soft_v, res_v = views[:2]
        spot = spots_at - (first_row + at_row_base + n - 3) * width
        hits = jnp.where(spots == spot, 1.0, 0.0).astype(BF)
        source = matmul(hits, sources[...])
        for c in pieces:
            s, around = beside(soft_v, n - 1, n, n + 1, c, 1.0)
            held, total = around_slot(n, 0, c)
            value = (s * total - held * around) + source[c * piece : (c + 1) * piece]
            res_v[n, at(c), :] = value
            store(ring, 4 + n % 4, c, s * value)
            store(ring, 12 + n % 4, c, around)

        def store_zero():
            for c in pieces:
                res_v[n, at(c), :] = blank_piece
                store(ring, 4 + n % 4, c, blank_piece)

        if static:
            clear(n, store_zero)

    def image(at_row_base, views, n, static, sums):
        soft_v, res_v, img_v = views[:3]
        plane = ring[4 + n % 4, pl.ds(GUARD, width), :]
        lanes = matmul(jnp.concatenate(halves(plane), axis=1), beside_lanes[...])
        for c in pieces:
            held = near(ring, 4 + n % 4, c)
            ends = near(ring, 4 + n % 4, c, -1) + near(ring, 4 + n % 4, c, 1)
            sides = near(ring, 4 + (n - 1) % 4, c) + near(ring, 4 + (n + 1) % 4, c)
            total = (lanes[c * piece : (c + 1) * piece] + ends) + sides
            s, value = near(soft_v, n, c), res_v[n, at(c), :]
            applied = held * near(ring, 12 + n % 4, c) - s * total
            img_v[n, at(c), :] = applied
            store(ring, 8 + n % 4, c, s * applied)
            if sums is not None:
                sums[0].append(partial(value * value))
                sums[1].append(partial(value * applied))

        def store_zero():
            for c in pieces:
                img_v[n, at(c), :] = blank_piece
                store(ring, 8 + n % 4, c, blank_piece)

        if static:
            clear(n, store_zero)

    def twice(at_row_base, views, n, sums):
        img_v = views[2]
        for c in pieces:
            held, value = near(ring, 8 + n % 4, c), img_v[n, at(c), :]
            after = near(ring, 8 + (n + 1) % 4, c) + near(ring, 8 + n % 4, c, 1)
            after = after + jnp.where(is_last, 0.0, ahead(held))
            sums[2].append(partial(value * value))
            sums[3].append(partial(held * (value * near(ring, 12 + n % 4, c) - 2.0 * after)))

    def keep(sums):
        for n, terms in enumerate(sums):
            if terms:
                acc[n] += sum(terms[1:], terms[0])

    whole = (soft, res, img, lk, wm)

    def walk(first, last, r_rows, q_rows, q_own, t_rows):
        sums = [[], [], [], []]
        for k in range(first, last + 1):
            if k < rows + 6 and k <= r_rows[1] + 1:
                prepare(0, whole, k, True)
            if r_rows[0] <= k - 2 <= r_rows[1]:
                residual(0, whole, k - 2, True)
            if q_rows[0] <= k - 4 <= q_rows[1]:
                own = q_own[0] <= k - 4 <= q_own[1]
                image(0, whole, k - 4, True, sums if own else None)
            if t_rows[0] <= k - 5 <= t_rows[1]:
                twice(0, whole, k - 5, sums)
        keep(sums)

    def steady(j, _):
        base = 4 + 4 * j
        views = [ref.at[pl.ds(base, 11)] for ref in whole]
        sums = [[], [], [], []]
        for u in range(4):
            prepare(base, views, 7 + u, False)
            residual(base, views, 5 + u, False)
            image(base, views, 3 + u, False, sums)
            twice(base, views, 2 + u, sums)
        keep(sums)
        return 0

    spots_at = jnp.concatenate([columns[...], columns[...]], axis=1)
    for copy in loads(0):
        copy.wait()
    last = rows + 2
    walk(3, 10, (4, last + 2), (5, last + 1), (5, last), (6, last))
    for m in range(1, parts):
        for copy in loads(m):
            copy.wait()
    lax.fori_loop(0, (rows - 8) // 4, steady, 0)

    @pl.when(slab < slabs - 1)
    def _():
        for copy in halo(0):
            copy.wait_recv()

    walk(rows + 3, rows + 8, (4, last + 2), (5, last + 1), (5, last), (6, last))

    @pl.when(slab > 0)
    def _():
        for copy in halo(1):
            copy.wait_recv()

    walk(0, 10, (1, 7), (2, 6), (3, 4), (3, 5))

    levels_in = pltpu.make_async_copy(heads, lk.at[pl.ds(3, rows)], load_sem.at[0, 0])
    levels_in.start()
    lk[2] = level_ends[0]
    lk[rows + 3] = level_ends[1]
    rows_of = [jnp.sum(acc[n], axis=0, keepdims=True) for n in range(4)]
    shared[slab] = jnp.concatenate(rows_of + [jnp.zeros((4, depth), F32)], axis=0)
    copies = [
        pltpu.make_async_remote_copy(
            src_ref=shared.at[slab],
            dst_ref=shared.at[slab],
            send_sem=send_sum.at[k],
            recv_sem=take_sum.at[k],
            device_id=other,
            device_id_type=MESH,
        )
        for k, other in enumerate(others)
    ]
    for copy in copies:
        copy.start()

    @pl.when(slab > 0)
    def _():
        for copy in halo(0):
            copy.wait_send()

    @pl.when(slab < slabs - 1)
    def _():
        for copy in halo(1):
            copy.wait_send()

    for copy in copies:
        copy.wait()
    levels_in.wait()
    fetch.wait()

    collected = shared[0]
    for m in range(1, slabs):
        collected = collected + shared[m]

    def gathered(n):
        total = jnp.sum(collected[n : n + 1], axis=1, keepdims=True)
        return jnp.broadcast_to(total, (1, depth))

    norm, curve, square, bend = [gathered(n) for n in range(4)]
    length = norm / curve
    norm_next = length * length * square - norm
    curve_next = curve - 2.0 * length * square + length * length * bend
    ratio = norm_next / norm
    length_next = norm_next / (curve_next - ratio * norm_next / length)
    with_start = length + length_next * (1.0 + ratio)
    with_image = length_next * length

    def eighth(n, base):
        return base + lax.rem(n, 8)

    def fill(n):
        for c in pieces:
            field = wm[n, at(c), :].astype(F32)
            field = field + (with_start * res[n, at(c), :] - with_image * img[n, at(c), :])
            store(ring, eighth(n, 0), c, field)
            store(ring, eighth(n, 8), c, lk[n, at(c), :].astype(F32))

    fill(2)
    fill(3)
    groups = rows // count
    at_block = at_lane // (depth // count)

    def turn(g):
        return lax.rem(g, RING)

    def group(g):
        start = 3 + count * g
        for p in range(count):
            fill(start + p + 1)
        for c in pieces:
            fields = [near(ring, eighth(start + p, 0), c) for p in range(-1, count + 1)]
            levels = [near(ring, eighth(start + p, 8), c) for p in range(-1, count + 1)]
            steps = [
                (fields[p] - fields[p + 1]) * (levels[p] - levels[p + 1]) for p in range(count + 1)
            ]
            turns = []
            for p in range(count):
                n = start + p
                f, h, s = fields[p + 1], levels[p + 1], near(soft, n, c)
                total = near(soft, n - 1, c) * steps[p] + near(soft, n + 1, c) * steps[p + 1]
                for off in (-1, 1):
                    field = near(ring, eighth(n, 0), c, off)
                    level = near(ring, eighth(n, 8), c, off)
                    total += near(soft, n, c, off) * ((f - field) * (h - level))
                both = f * h
                product = (f - ahead(f)) * (h - ahead(h))
                total += jnp.where(is_last, both, ahead(s) * product)
                total += jnp.where(is_first, both, behind(s * product))
                place = well[0] - (first_row + n - 3) * width - c * piece
                value = jnp.where(at_row != place, s * total, 0.0)
                double = matmul(jnp.concatenate(halves(value), axis=1), turned[p])
                turns.append(double[:, :depth] + double[:, depth:])
            for t in range(count):
                joined = turns[-t % count]
                for b in range(1, count):
                    joined = jnp.where(at_block == b, turns[(b - t) % count], joined)
                mine[t % 2, turn(g), t // 2, at(c), :] = joined

    def to_mate(g):
        return pltpu.make_async_remote_copy(
            src_ref=mine.at[1 - core, turn(g)],
            dst_ref=from_mate.at[g],
            send_sem=send_mate.at[g],
            recv_sem=take_mate.at[g],
            device_id=mate,
            device_id_type=MESH,
        )

    def to_across(g):
        return pltpu.make_async_remote_copy(
            src_ref=ship.at[turn(g)],
            dst_ref=got.at[g],
            send_sem=send_across.at[g],
            recv_sem=take_across.at[g],
            device_id=across,
            device_id_type=MESH,
        )

    def relay(g):
        to_mate(g).wait_recv()
        ship[turn(g)] = encode(mine[core, turn(g), 1 - half] + from_mate[g, 1 - half], 16)
        to_across(g).start()

    part = width // count
    spare = going.shape[2] - part
    lanes = depth
    filtered = res.at[:, pl.ds(0, part)]

    def settle(g):
        to_across(g).wait_recv()
        to_mate(g).wait_send()
        to_across(g).wait_send()

    def absorb(g):
        summed = (mine[core, turn(g), half] + from_mate[g, half]) + decode(got[g], 16)
        top, low = halves(summed)
        mixed = matmul(cas_across[...], jnp.concatenate([top, top, low], axis=0))
        blocks = [mixed[j * part : (j + 1) * part] for j in range(count)]
        for p, plane in enumerate(swap_blocks(blocks)):
            freq[g * count + lax.rem(p - here + count, count)] = plane
        pole = tables[0]
        one, two, back_one, back_two, power = (ends[n] for n in range(5))
        for p in range(count):
            value = freq[g * count + p]
            one, two = value + pole * one, pole * (two + one)
            weighted = value * power
            back_one = back_one + weighted
            back_two = back_two + (g * count + p).astype(F32) * weighted
            power = power * pole
        for n, value in enumerate((one, two, back_one, back_two, power)):
            ends[n] = value

    ends[0:4] = jnp.zeros((4, part, lanes), F32)
    ends[4] = jnp.ones((part, lanes), F32)
    lag = 4

    def early(g, _):
        group(g)
        to_mate(g).start()
        relay(g - 1)
        return 0

    def late(g, _):
        settle(g - lag)
        absorb(g - lag)
        group(g)
        to_mate(g).start()
        relay(g - 1)
        return 0

    group(0)
    to_mate(0).start()
    lax.fori_loop(1, lag, early, 0)
    lax.fori_loop(lag, groups, late, 0)
    relay(groups - 1)

    def finish(g, _):
        settle(g)
        absorb(g)
        return 0

    lax.fori_loop(groups - lag, groups, finish, 0)
    pole, level, slope, decay, wrap_one, wrap_two = (tables[n] for n in range(6))
    zero = jnp.zeros((part, lanes), F32)

    def pass_on(way):
        pair = pl.ds(2 * way, 2)
        return [
            pltpu.make_async_remote_copy(
                src_ref=moments.at[slab, pair],
                dst_ref=moments.at[slab, pair],
                send_sem=send_end.at[way, k],
                recv_sem=take_end.at[way, k],
                device_id=other,
                device_id_type=MESH,
            )
            for k, other in enumerate(others)
        ]

    for way in range(2):
        for n in (2 * way, 2 * way + 1):
            moments[slab, n] = encode(ends[n], spare)
        for copy in pass_on(way):
            copy.start()
    for copy in pass_on(0):
        copy.wait()

    def carried(direction, n):
        one, two = zero, zero
        for m in range(slabs, 0, -1):
            other = lax.rem(slab + 2 * slabs - direction * m, slabs)
            one, two = (
                decay * one + decode(moments[other, n], spare),
                decay * (two + rows * one) + decode(moments[other, n + 1], spare),
            )
        return wrap_one * one, wrap_one * two + wrap_two * one

    def forward(i, carry):
        one, two = carry
        two = pole * (two + one)
        one = freq[i] + pole * one
        filtered[i] = level * one + slope * two
        return one, two

    lax.fori_loop(0, rows, forward, carried(1, 0))

    for copy in pass_on(1):
        copy.wait()

    def to_peer(k, g):
        return pltpu.make_async_remote_copy(
            src_ref=going.at[peers[k], g],
            dst_ref=coming.at[here, g],
            send_sem=send_back.at[k, g],
            recv_sem=take_back.at[k, g],
            device_id={"test": peers[k]},
            device_id_type=MESH,
        )

    pair = 2

    pairs = groups // pair

    def unmix(turned_j, carry):
        j = pairs - 1 - turned_j
        one, two = carry
        planes = [None] * (pair * count)
        for i in reversed(range(pair * count)):
            at_i = j * (pair * count) + i
            two = pole * (two + one)
            one = pole * one
            planes[i] = filtered[at_i] + (level * one + slope * two)
            one = one + freq[at_i]
        both = []
        for n in range(pair):
            blocks = swap_blocks(planes[n * count : (n + 1) * count])
            top, low = halves(jnp.concatenate(blocks, axis=0))
            both.append(jnp.concatenate([top, top, low], axis=0))
        mixed = matmul(cas_across[...], jnp.concatenate(both, axis=1))
        for n in range(pair):
            for u in range(count):
                block = mixed[u * part : (u + 1) * part, n * lanes : (n + 1) * lanes]
                going[u, pair * j + n] = encode(block, spare)
        for g in [pair * j + n for n in range(pair)]:
            for k in range(count - 1):
                to_peer(k, g).start()
            coming[here, g] = going[here, g]
        return one, two

    lax.fori_loop(0, pairs, unmix, carried(-1, 2))

    def back(turned_j, _):
        j = pairs - 1 - turned_j
        for g in [pair * j + n for n in range(pair)]:
            for k in range(count - 1):
                to_peer(k, g).wait()
        for g in [pair * j + n for n in range(pair)]:
            planes = [decode(coming[t, g], spare) for t in range(count)]
            for p, plane in enumerate(swap_blocks(planes)):
                double = matmul(jnp.concatenate(halves(plane), axis=1), cas_depth[...])
                out[g * count + p] = double[:, :lanes] + double[:, lanes:]
        return 0

    lax.fori_loop(0, pairs, back, 0)


def table(length):
    indices = np.arange(length)
    angles = (indices[:, None] * indices[None, :] % length) * (2.0 * np.pi / length)
    return (np.cos(angles) + np.sin(angles)).astype(np.float32)


def split(values):
    top = values.astype(jnp.bfloat16)
    return top, (values - top.astype(np.float32)).astype(jnp.bfloat16)


def doubled_table(values):
    top, low = split(values)
    return np.block([[top, low], [top, np.zeros_like(low)]])


def turned_tables(length, count):
    tables = []
    for p in range(count):
        tables.append(doubled_table(-0.5 * np.roll(table(length), p * (length // count), axis=1)))
    return np.stack(tables)


def filter_tables(rows, along, width, depth, count):
    def kappa(length):
        return 4.0 * np.sin(np.pi * np.arange(length) / length) ** 2

    part, block = width // count, depth // count
    lanes_at = np.arange(depth)
    across_at = (lanes_at // block)[None, :] * part + np.arange(part)[:, None]
    listed = []
    for here in range(count):
        depth_at = here * block + lanes_at % block
        shift = 1.0 + range_squared * (kappa(width)[across_at] + kappa(depth)[depth_at][None, :])
        centre = 1.0 + shift / (2.0 * range_squared)
        pole = 1.0 / (centre + np.sqrt(centre * centre - 1.0))
        square = pole * pole
        gain = prior_gain / (range_squared * range_squared) * square / (width * depth)
        slope = gain / (1.0 - square) ** 2
        level = slope * (1.0 + square) / (1.0 - square)
        turn = pole**along
        wrap_one = 1.0 / (1.0 - turn)
        wrap_two = along * turn * wrap_one * wrap_one
        listed.append(np.stack([pole, level, slope, pole**rows, wrap_one, wrap_two]))
    return np.stack(listed).astype(np.float32)


def fast(log_k, heads, warm_adjoint, obs_columns, obs_residuals, well_columns):
    rows, width, depth = log_k.shape
    slabs = lax.axis_size("space")
    count = lax.axis_size("test")
    part = width // count
    groups = rows // count
    observed = obs_columns.shape[1]
    planes = rows + 6
    padded = width + 2 * GUARD
    spare = 16 - part % 16
    top, low = split(table(width))
    return pl.pallas_call(
        whole_kernel,
        out_shape=shape(rows, part, depth),
        in_specs=[SM, VM, VM, ANY, ANY, ANY, VM, VM, ANY, VM, VM],
        out_specs=VM,
        scratch_shapes=[pltpu.VMEM((planes, width, depth), BF)] * 2
        + [
            pltpu.VMEM((2, width, depth), BF),
            pltpu.VMEM((planes, padded, depth), F32),
            pltpu.VMEM((planes, width, depth), F32),
            pltpu.VMEM((planes, width, depth), F32),
            pltpu.VMEM((16, padded, depth), F32),
            pltpu.VMEM((2 * observed, depth), BF),
            pltpu.VMEM((4, 8, depth), F32),
            pltpu.VMEM((slabs, 8, depth), F32),
            pltpu.VMEM((2, RING, 2, width, depth), F32),
            pltpu.VMEM((groups, 2, width, depth), F32),
            pltpu.VMEM((RING, width + 16, depth), jnp.int16),
            pltpu.VMEM((groups, width + 16, depth), jnp.int16),
            pltpu.SemaphoreType.DMA((2, 4)),
        ]
        + [pltpu.SemaphoreType.DMA((2, 3))] * 2
        + [pltpu.SemaphoreType.DMA((slabs - 1,))] * 2
        + [pltpu.SemaphoreType.DMA((groups,))] * 4
        + [
            pltpu.VMEM((6, part, depth), F32),
            pltpu.VMEM((rows, part, depth), F32),
            pltpu.VMEM((slabs, 4, part + spare, depth), jnp.int16),
            pltpu.VMEM((count, groups, part + spare, depth), jnp.int16),
            pltpu.VMEM((count, groups, part + spare, depth), jnp.int16),
            pltpu.SemaphoreType.DMA,
        ]
        + [pltpu.SemaphoreType.DMA((2, slabs - 1))] * 2
        + [pltpu.SemaphoreType.DMA((count - 1, groups))] * 2
        + [pltpu.VMEM((5, part, depth), F32)],
        compiler_params=pltpu.CompilerParams(
            vmem_limit_bytes=60 * 1024 * 1024, collective_id=1, has_side_effects=True
        ),
        name="whole",
    )(
        well_columns,
        obs_columns,
        obs_residuals[0],
        log_k,
        warm_adjoint[0],
        heads[0],
        jnp.asarray(turned_tables(depth, count)),
        jnp.asarray(np.tile(np.eye(depth, k=1) + np.eye(depth, k=-1), (2, 1)), BF),
        jnp.asarray(filter_tables(rows, rows * slabs, width, depth, count)),
        jnp.asarray(np.concatenate([top, low, top], axis=1)),
        jnp.asarray(doubled_table(table(depth))),
    )


def pick(log_k, heads, warm_adjoint, obs_columns, *rest):
    rows, width, depth = log_k.shape
    count = lax.axis_size("test")
    fits = depth == 128 and count == 4 and rows % 8 == 0 and rows >= 16 and width % 96 == 0
    fits = fits and obs_columns.shape[1] % 64 == 0 and rows * width <= 48 * 288
    run = fast if fits and lax.axis_size("space") > 1 else on_device
    return run(log_k, heads, warm_adjoint, obs_columns, *rest)


def solution(mesh):
    placed = (
        P(("groups", "space"), None, None),
        P("test", ("groups", "space"), None, None),
        P("test", ("groups", "space"), None, None),
        P("test", "groups"),
        P("test", "groups", None),
        P(("groups", "test")),
    )
    return jax.shard_map(
        pick,
        mesh=mesh,
        in_specs=placed,
        out_specs=P(("groups", "space"), "test", None),
        check_vma=False,
    )
```

```python
import jax
import jax.numpy as jnp
import numpy as np
from jax import lax
from jax.experimental import pallas as pl
from jax.experimental.pallas import tpu as pltpu
from jax.sharding import PartitionSpec as P

ITERS = 2


prior_gain = 5.0
range_squared = 4.0


def with_halo(cells, sides, width):
    for axis, dim in sides:
        count = lax.axis_size(axis)
        ends = count - 1
        head = lax.slice_in_dim(cells, 0, width, axis=dim)
        tail = lax.slice_in_dim(cells, cells.shape[dim] - width, cells.shape[dim], axis=dim)
        cells = jnp.concatenate(
            [
                lax.ppermute(tail, axis, [(i, (i + 1) % count) for i in range(ends)]),
                cells,
                lax.ppermute(head, axis, [((i + 1) % count, i) for i in range(ends)]),
            ],
            axis=dim,
        )
    return cells


def neighbours(padded):
    return [
        padded[2:, 1:-1, 1:-1],
        padded[:-2, 1:-1, 1:-1],
        padded[1:-1, 2:, 1:-1],
        padded[1:-1, :-2, 1:-1],
        padded[1:-1, 1:-1, 2:],
        padded[1:-1, 1:-1, :-2],
    ]


def operate(values, padded, conduct):
    summed = jnp.zeros_like(values)
    for face_k, beside in zip(conduct, neighbours(padded)):
        summed = summed + face_k * (values - beside)
    return summed


def kappa_of(indices, length):
    return 4.0 * jnp.sin(jnp.pi * indices / length) ** 2


def pad_sides(padded):
    return jnp.pad(padded, ((0, 0), (1, 1), (1, 1)))


def with_faces(values):
    return pad_sides(with_halo(values, (("space", 0),), 1))


def squares(residual):
    return lax.psum(jnp.sum(residual * residual), "space")


def hartley(length):
    indices = jnp.arange(length, dtype=jnp.int32)
    products = indices[:, None] * indices[None, :] % length
    angles = products.astype(jnp.float32) * (2.0 * jnp.pi / length)
    return jnp.cos(angles) + jnp.sin(angles)


def on_device(log_k, heads, warm_adjoint, obs_columns, obs_residuals, well_columns):
    slab_rows, width_cells, depth_cells = log_k.shape
    space_count = lax.axis_size("space")
    first_row = lax.axis_index("space") * slab_rows
    logk_pad, head_pad = (
        with_halo(log_k, (("space", 0),), 1),
        with_halo(heads[0], (("space", 0),), 1),
    )
    logk_val = log_k.astype(jnp.float32)
    conduct = [
        jnp.exp(0.5 * (logk_val + beside))
        for beside in neighbours(pad_sides(logk_pad.astype(jnp.float32)))
    ]
    columns = obs_columns[0]
    row_local = columns // width_cells - first_row
    inside = (row_local >= 0) & (row_local < slab_rows)
    row_local = jnp.where(inside, row_local, slab_rows)
    source = jnp.zeros((slab_rows, width_cells, depth_cells), jnp.float32)
    source = source.at[row_local, columns % width_cells].add(obs_residuals[0], mode="drop")
    adjoint = warm_adjoint[0].astype(jnp.float32)
    lam_padded = with_faces(adjoint)
    residual = source - operate(adjoint, lam_padded, conduct)
    direction = residual
    norm_now = squares(residual)
    for iteration in range(ITERS):
        dir_padded = with_faces(direction)
        applied = operate(direction, dir_padded, conduct)
        step_length = norm_now / lax.psum(jnp.sum(direction * applied), "space")
        adjoint = adjoint + step_length * direction
        lam_padded = lam_padded + step_length * dir_padded
        if iteration + 1 < ITERS:
            residual = residual - step_length * applied
            norm_next = squares(residual)
            direction = residual + norm_next / norm_now * direction
            norm_now = norm_next
    lam_full = pad_sides(with_halo(adjoint, (("space", 0),), 1))
    head_val = heads[0].astype(jnp.float32)
    misfit_term = jnp.zeros_like(adjoint)
    for face_k, lam_side, head_side in zip(
        conduct, neighbours(lam_full), neighbours(pad_sides(head_pad.astype(jnp.float32)))
    ):
        misfit_term = misfit_term + face_k * (adjoint - lam_side) * (head_val - head_side)
    column_ids = (first_row + jnp.arange(slab_rows, dtype=jnp.int32))[
        :, None
    ] * width_cells + jnp.arange(width_cells, dtype=jnp.int32)[None, :]
    keep_mask = (column_ids != well_columns[0]).astype(jnp.float32)
    partial_value = -0.5 * misfit_term * keep_mask[:, :, None]
    highest = lax.Precision.HIGHEST
    cas_depth = hartley(depth_cells)
    cas_across = hartley(width_cells)
    along_cells = slab_rows * space_count
    cas_along = hartley(along_cells)
    summed = lax.psum_scatter(partial_value, "test", scatter_dimension=1, tiled=True)
    depth_freq = jnp.einsum("xyz,zk->xky", summed, cas_depth, precision=highest)
    pencil = lax.all_to_all(depth_freq, "test", split_axis=1, concat_axis=2, tiled=True)
    across_freq = jnp.einsum("xzy,yk->kzx", pencil, cas_across, precision=highest)
    column_block = lax.all_to_all(across_freq, "space", split_axis=0, concat_axis=2, tiled=True)
    along_freq = jnp.einsum("yzx,xk->yzk", column_block, cas_along, precision=highest)
    across_rows = column_block.shape[0]
    depth_rows = column_block.shape[1]
    kappa_x = kappa_of(jnp.arange(along_cells).astype(jnp.float32), along_cells)
    kappa_y = kappa_of(
        (lax.axis_index("space") * across_rows + jnp.arange(across_rows)).astype(jnp.float32),
        width_cells,
    )
    kappa_z = kappa_of(
        (lax.axis_index("test") * depth_rows + jnp.arange(depth_rows)).astype(jnp.float32),
        depth_cells,
    )
    spectrum = (
        prior_gain
        / (
            1.0
            + range_squared
            * (kappa_y[:, None, None] + kappa_z[None, :, None] + kappa_x[None, None, :])
        )
        ** 2
    )
    along_back = jnp.einsum("yzk,kx->yzx", along_freq * spectrum, cas_along, precision=highest)
    slab_block = lax.all_to_all(along_back, "space", split_axis=2, concat_axis=0, tiled=True)
    across_back = jnp.einsum("yzx,yk->xzk", slab_block, cas_across, precision=highest)
    depth_block = lax.all_to_all(across_back, "test", split_axis=2, concat_axis=1, tiled=True)
    result = jnp.einsum("xky,kz->xyz", depth_block, cas_depth, precision=highest)
    scale_back = 1.0 / (along_cells * width_cells * depth_cells)
    return result * scale_back


GUARD = 8
RING = 6
STEP = 256.0
TOP = 32000.0
HALF_LOG = 0.5 / float(np.log(2.0))
BF = jnp.bfloat16
F32 = jnp.float32
VM = pl.BlockSpec(memory_space=pltpu.VMEM)
SM = pl.BlockSpec(memory_space=pltpu.SMEM)
ANY = pl.BlockSpec(memory_space=pl.ANY)
MESH = pl.DeviceIdType.MESH


def shape(*dims, dtype=jnp.float32):
    return jax.ShapeDtypeStruct(dims, dtype)


def iota(plane, axis):
    return lax.broadcasted_iota(jnp.int32, plane, axis)


def halves(values):
    top = values.astype(BF)
    return top, (values - top.astype(F32)).astype(BF)


def matmul(a, b):
    return jnp.dot(a, b, preferred_element_type=F32)


def encode(values, spare):
    rows, lanes = values.shape
    peak = jnp.maximum(jnp.max(jnp.abs(values), axis=0, keepdims=True), 1e-30)
    level = jnp.ceil(jnp.log2(peak) * STEP)
    scaled = jnp.round(values * (jnp.exp2(level * (-1.0 / STEP)) * TOP))
    both = jnp.concatenate([scaled, jnp.broadcast_to(level, (spare, lanes))], axis=0)
    return both.astype(jnp.int32).astype(jnp.int16)


def decode(codes, spare):
    wide = codes.astype(jnp.int32).astype(F32)
    rows = wide.shape[0] - spare
    level = wide[rows : rows + 1]
    return wide[:rows] * (jnp.exp2(level * (1.0 / STEP)) * (1.0 / TOP))


def swap_blocks(planes):
    planes = list(planes)
    count = len(planes)
    lanes = planes[0].shape[1]
    block = lanes // count
    at_block = iota(planes[0].shape, 1) // block
    span = 1
    while span < count:
        odd = (at_block // span) % 2 == 1
        for low in range(count):
            if (low // span) % 2 == 0:
                first, second = planes[low], planes[low + span]
                up = pltpu.roll(second, block * span, 1)
                down = pltpu.roll(first, lanes - block * span, 1)
                planes[low] = jnp.where(odd, up, first)
                planes[low + span] = jnp.where(odd, second, down)
        span *= 2
    return planes


def greet(others):
    barrier = pltpu.get_barrier_semaphore()
    for other in others:
        pl.semaphore_signal(barrier, inc=1, device_id=other, device_id_type=MESH)
    pl.semaphore_wait(barrier, len(others))


def whole_kernel(
    well,
    columns,
    observed,
    logk,
    warm,
    heads,
    turned,
    beside_lanes,
    listed,
    cas_across,
    cas_depth,
    out,
    lk,
    wm,
    level_ends,
    soft,
    res,
    img,
    ring,
    sources,
    acc,
    shared,
    mine,
    from_mate,
    ship,
    got,
    load_sem,
    halo_send,
    halo_take,
    send_sum,
    take_sum,
    send_mate,
    take_mate,
    send_across,
    take_across,
    tables,
    freq,
    moments,
    going,
    coming,
    table_sem,
    send_end,
    take_end,
    send_back,
    take_back,
    ends,
    ready,
    leave_sem,
):
    rows, width, depth = logk.shape
    parts = 4
    chunk = rows // parts
    piece = width // 6
    pieces = range(6)
    slabs = shared.shape[0]
    slab, here = lax.axis_index("space"), lax.axis_index("test")
    half, core = here // 2, lax.rem(here, 2)
    mate = {"test": 2 * half + 1 - core}
    across = {"test": 2 * (1 - half) + core}
    others = [{"space": lax.rem(slab + k, slabs)} for k in range(1, slabs)]
    first_row = slab * rows

    def loads(m):
        span = pl.ds(m * chunk, chunk)
        to = pl.ds(3 + m * chunk, chunk)
        return [
            pltpu.make_async_copy(frm.at[span], held.at[to], load_sem.at[n, m])
            for n, (frm, held) in enumerate(((logk, lk), (warm, wm)))
        ]

    for m in range(parts):
        for copy in loads(m):
            copy.start()

    def halo(direction):
        up = direction == 1
        copies = []
        for n, (frm, held, deep) in enumerate(((logk, lk, 3), (warm, wm, 3), (heads, level_ends, 1))):
            at = rows - deep if up else 0
            to = 3 - deep if up else 3 + rows
            if deep == 1:
                to = 0 if up else 1
            copies.append(
                pltpu.make_async_remote_copy(
                    src_ref=frm.at[pl.ds(at, deep)],
                    dst_ref=held.at[pl.ds(to, deep)],
                    send_sem=halo_send.at[direction, n],
                    recv_sem=halo_take.at[direction, n],
                    device_id={"space": slab + 1 if up else slab - 1},
                    device_id_type=MESH,
                )
            )
        return copies

    count = 4
    peers = [lax.rem(here + k, count) for k in range(1, count)]
    fetch = pltpu.make_async_copy(listed.at[here], tables, table_sem)
    fetch.start()
    greet(others + [{"test": peer} for peer in peers])

    @pl.when(slab > 0)
    def _():
        for copy in halo(0):
            copy.start()

    @pl.when(slab < slabs - 1)
    def _():
        for copy in halo(1):
            copy.start()

    blank = jnp.zeros((3, width, depth), BF)

    @pl.when(slab == 0)
    def _():
        lk[0:3] = blank
        wm[0:3] = blank
        level_ends[0] = blank[0]

    @pl.when(slab == slabs - 1)
    def _():
        lk[rows + 3 : rows + 6] = blank
        wm[rows + 3 : rows + 6] = blank
        level_ends[1] = blank[0]

    top, low = halves(observed[...])
    sources[...] = jnp.concatenate([top, low], axis=0)
    acc[...] = jnp.zeros_like(acc)
    edge = jnp.zeros((GUARD, depth), F32)
    for i in range(ring.shape[0]):
        ring[i, 0:GUARD, :] = edge
        ring[i, width + GUARD : width + 2 * GUARD, :] = edge

    at_lane = iota((piece, depth), 1)
    at_row = iota((piece, depth), 0)
    is_first, is_last = at_lane == 0, at_lane == depth - 1
    spots = iota((width, 2 * columns.shape[1]), 0)

    def at(c):
        return pl.ds(c * piece, piece)

    def near(ref, i, c, off=0):
        return ref[i, pl.ds(GUARD + c * piece + off, piece), :]

    def store(ref, i, c, value):
        ref[i, pl.ds(GUARD + c * piece, piece), :] = value

    def ahead(value):
        return pltpu.roll(value, depth - 1, 1)

    def behind(value):
        return pltpu.roll(value, 1, 1)

    def ring_sum(held, ends, sides, outer):
        lanes = jnp.where(is_last, outer, ahead(held)) + jnp.where(is_first, outer, behind(held))
        return (lanes + ends) + sides

    def beside(ref, below, i, above, c, outer):
        held = near(ref, i, c)
        ends = near(ref, i, c, -1) + near(ref, i, c, 1)
        return held, ring_sum(held, ends, near(ref, below, c) + near(ref, above, c), outer)

    def around_slot(n, base, c):
        return beside(ring, base + (n - 1) % 4, base + n % 4, base + (n + 1) % 4, c, 0.0)

    def partial(value):
        return jnp.sum(value.reshape(piece // 8, 8, depth), axis=0)

    def clear(n, store_zero):
        if n < 3:
            pl.when(slab == 0)(store_zero)
        if n >= rows + 3:
            pl.when(slab == slabs - 1)(store_zero)

    blank_piece = jnp.zeros((piece, depth), F32)

    def prepare(at_row_base, views, n, static):
        soft_v, _, _, lk_v, wm_v = views
        one = jnp.ones((GUARD, depth), F32)
        soft_v[n, 0:GUARD, :] = one
        soft_v[n, width + GUARD : width + 2 * GUARD, :] = one
        for c in pieces:
            value = jnp.exp2(HALF_LOG * lk_v[n, at(c), :].astype(F32))
            store(soft_v, n, c, value)
            store(ring, n % 4, c, value * wm_v[n, at(c), :].astype(F32))

    def residual(at_row_base, views, n, static):
        soft_v, res_v = views[:2]
        spot = spots_at - (first_row + at_row_base + n - 3) * width
        hits = jnp.where(spots == spot, 1.0, 0.0).astype(BF)
        source = matmul(hits, sources[...])
        for c in pieces:
            s, around = beside(soft_v, n - 1, n, n + 1, c, 1.0)
            held, total = around_slot(n, 0, c)
            value = (s * total - held * around) + source[c * piece : (c + 1) * piece]
            res_v[n, at(c), :] = value
            store(ring, 4 + n % 4, c, s * value)
            store(ring, 12 + n % 4, c, around)

        def store_zero():
            for c in pieces:
                res_v[n, at(c), :] = blank_piece
                store(ring, 4 + n % 4, c, blank_piece)

        if static:
            clear(n, store_zero)

    def image(at_row_base, views, n, static, sums):
        soft_v, res_v, img_v = views[:3]
        plane = ring[4 + n % 4, pl.ds(GUARD, width), :]
        lanes = matmul(jnp.concatenate(halves(plane), axis=1), beside_lanes[...])
        for c in pieces:
            held = near(ring, 4 + n % 4, c)
            ends = near(ring, 4 + n % 4, c, -1) + near(ring, 4 + n % 4, c, 1)
            sides = near(ring, 4 + (n - 1) % 4, c) + near(ring, 4 + (n + 1) % 4, c)
            total = (lanes[c * piece : (c + 1) * piece] + ends) + sides
            s, value = near(soft_v, n, c), res_v[n, at(c), :]
            applied = held * near(ring, 12 + n % 4, c) - s * total
            img_v[n, at(c), :] = applied
            store(ring, 8 + n % 4, c, s * applied)
            if sums is not None:
                sums[0].append(partial(value * value))
                sums[1].append(partial(value * applied))

        def store_zero():
            for c in pieces:
                img_v[n, at(c), :] = blank_piece
                store(ring, 8 + n % 4, c, blank_piece)

        if static:
            clear(n, store_zero)

    def twice(at_row_base, views, n, sums):
        img_v = views[2]
        for c in pieces:
            held, value = near(ring, 8 + n % 4, c), img_v[n, at(c), :]
            after = near(ring, 8 + (n + 1) % 4, c) + near(ring, 8 + n % 4, c, 1)
            after = after + jnp.where(is_last, 0.0, ahead(held))
            sums[2].append(partial(value * value))
            sums[3].append(partial(held * (value * near(ring, 12 + n % 4, c) - 2.0 * after)))

    def keep(sums):
        for n, terms in enumerate(sums):
            if terms:
                acc[n] += sum(terms[1:], terms[0])

    whole = (soft, res, img, lk, wm)

    def walk(first, last, r_rows, q_rows, q_own, t_rows):
        sums = [[], [], [], []]
        for k in range(first, last + 1):
            if k < rows + 6 and k <= r_rows[1] + 1:
                prepare(0, whole, k, True)
            if r_rows[0] <= k - 2 <= r_rows[1]:
                residual(0, whole, k - 2, True)
            if q_rows[0] <= k - 4 <= q_rows[1]:
                own = q_own[0] <= k - 4 <= q_own[1]
                image(0, whole, k - 4, True, sums if own else None)
            if t_rows[0] <= k - 5 <= t_rows[1]:
                twice(0, whole, k - 5, sums)
        keep(sums)

    def steady(j, _):
        base = 4 + 4 * j
        views = [ref.at[pl.ds(base, 11)] for ref in whole]
        sums = [[], [], [], []]
        for u in range(4):
            prepare(base, views, 7 + u, False)
            residual(base, views, 5 + u, False)
            image(base, views, 3 + u, False, sums)
            twice(base, views, 2 + u, sums)
        keep(sums)
        return 0

    spots_at = jnp.concatenate([columns[...], columns[...]], axis=1)
    for copy in loads(0):
        copy.wait()
    last = rows + 2
    walk(3, 10, (4, last + 2), (5, last + 1), (5, last), (6, last))
    for m in range(1, parts):
        for copy in loads(m):
            copy.wait()
    lax.fori_loop(0, (rows - 8) // 4, steady, 0)

    @pl.when(slab < slabs - 1)
    def _():
        for copy in halo(0):
            copy.wait_recv()

    walk(rows + 3, rows + 8, (4, last + 2), (5, last + 1), (5, last), (6, last))

    @pl.when(slab > 0)
    def _():
        for copy in halo(1):
            copy.wait_recv()

    def refill(base, n, values):
        for c in pieces:
            store(ring, base + n % 4, c, near(soft, n, c) * values[n, at(c), :].astype(F32))

    for n in range(3):
        prepare(0, whole, n, True)
    refill(0, 3, wm)
    residual(0, whole, 1, True)
    refill(0, 4, wm)
    residual(0, whole, 2, True)
    residual(0, whole, 3, True)
    refill(4, 4, res)
    for n in (4, 5):
        for c in pieces:
            store(ring, 12 + n % 4, c, beside(soft, n - 1, n, n + 1, c, 1.0)[1])
    sums = [[], [], [], []]
    image(0, whole, 2, True, None)
    image(0, whole, 3, True, sums)
    refill(4, 5, res)
    image(0, whole, 4, True, sums)
    refill(8, 5, img)
    refill(8, 6, img)
    for n in (3, 4, 5):
        twice(0, whole, n, sums)
    keep(sums)

    levels_in = pltpu.make_async_copy(heads, lk.at[pl.ds(3, rows)], load_sem.at[0, 0])
    levels_in.start()
    lk[2] = level_ends[0]
    lk[rows + 3] = level_ends[1]
    rows_of = [jnp.sum(acc[n], axis=0, keepdims=True) for n in range(4)]
    shared[slab] = jnp.concatenate(rows_of + [jnp.zeros((4, depth), F32)], axis=0)
    copies = [
        pltpu.make_async_remote_copy(
            src_ref=shared.at[slab],
            dst_ref=shared.at[slab],
            send_sem=send_sum.at[k],
            recv_sem=take_sum.at[k],
            device_id=other,
            device_id_type=MESH,
        )
        for k, other in enumerate(others)
    ]
    for copy in copies:
        copy.start()

    @pl.when(slab > 0)
    def _():
        for copy in halo(0):
            copy.wait_send()

    @pl.when(slab < slabs - 1)
    def _():
        for copy in halo(1):
            copy.wait_send()

    for copy in copies:
        copy.wait()
    levels_in.wait()
    fetch.wait()

    collected = shared[0]
    for m in range(1, slabs):
        collected = collected + shared[m]

    def gathered(n):
        total = jnp.sum(collected[n : n + 1], axis=1, keepdims=True)
        return jnp.broadcast_to(total, (1, depth))

    norm, curve, square, bend = [gathered(n) for n in range(4)]
    length = norm / curve
    norm_next = length * length * square - norm
    curve_next = curve - 2.0 * length * square + length * length * bend
    ratio = norm_next / norm
    length_next = norm_next / (curve_next - ratio * norm_next / length)
    with_start = length + length_next * (1.0 + ratio)
    with_image = length_next * length

    def eighth(n, base):
        return base + lax.rem(n, 8)

    def fill(n):
        for c in pieces:
            field = wm[n, at(c), :].astype(F32)
            field = field + (with_start * res[n, at(c), :] - with_image * img[n, at(c), :])
            store(ring, eighth(n, 0), c, field)
            store(ring, eighth(n, 8), c, lk[n, at(c), :].astype(F32))

    fill(2)
    fill(3)
    groups = rows // count
    at_block = at_lane // (depth // count)

    def turn(g):
        return lax.rem(g, RING)

    def group(g):
        start = 3 + count * g
        for p in range(count):
            fill(start + p + 1)
        for c in pieces:
            fields = [near(ring, eighth(start + p, 0), c) for p in range(-1, count + 1)]
            levels = [near(ring, eighth(start + p, 8), c) for p in range(-1, count + 1)]
            steps = [
                (fields[p] - fields[p + 1]) * (levels[p] - levels[p + 1]) for p in range(count + 1)
            ]
            turns = []
            for p in range(count):
                n = start + p
                f, h, s = fields[p + 1], levels[p + 1], near(soft, n, c)
                total = near(soft, n - 1, c) * steps[p] + near(soft, n + 1, c) * steps[p + 1]
                for off in (-1, 1):
                    field = near(ring, eighth(n, 0), c, off)
                    level = near(ring, eighth(n, 8), c, off)
                    total += near(soft, n, c, off) * ((f - field) * (h - level))
                both = f * h
                product = (f - ahead(f)) * (h - ahead(h))
                total += jnp.where(is_last, both, ahead(s) * product)
                total += jnp.where(is_first, both, behind(s * product))
                place = well[0] - (first_row + n - 3) * width - c * piece
                value = jnp.where(at_row != place, s * total, 0.0)
                double = matmul(jnp.concatenate(halves(value), axis=1), turned[p])
                turns.append(double[:, :depth] + double[:, depth:])
            for t in range(count):
                joined = turns[-t % count]
                for b in range(1, count):
                    joined = jnp.where(at_block == b, turns[(b - t) % count], joined)
                mine[t % 2, turn(g), t // 2, at(c), :] = joined

    def to_mate(g):
        return pltpu.make_async_remote_copy(
            src_ref=mine.at[1 - core, turn(g)],
            dst_ref=from_mate.at[g],
            send_sem=send_mate.at[g],
            recv_sem=take_mate.at[g],
            device_id=mate,
            device_id_type=MESH,
        )

    def to_across(g):
        return pltpu.make_async_remote_copy(
            src_ref=ship.at[turn(g)],
            dst_ref=got.at[g],
            send_sem=send_across.at[g],
            recv_sem=take_across.at[g],
            device_id=across,
            device_id_type=MESH,
        )

    def relay(g):
        to_mate(g).wait_recv()
        ship[turn(g)] = encode(mine[core, turn(g), 1 - half] + from_mate[g, 1 - half], 16)
        to_across(g).start()

    part = width // count
    spare = going.shape[2] - part
    lanes = depth
    filtered = res.at[:, pl.ds(0, part)]

    def settle(g):
        to_across(g).wait_recv()
        to_mate(g).wait_send()
        to_across(g).wait_send()

    def absorb(g):
        summed = (mine[core, turn(g), half] + from_mate[g, half]) + decode(got[g], 16)
        top, low = halves(summed)
        mixed = matmul(cas_across[...], jnp.concatenate([top, top, low], axis=0))
        blocks = [mixed[j * part : (j + 1) * part] for j in range(count)]
        for p, plane in enumerate(swap_blocks(blocks)):
            freq[g * count + lax.rem(p - here + count, count)] = plane
        pole = tables[0]
        one, two, back_one, back_two, power = (ends[n] for n in range(5))
        for p in range(count):
            value = freq[g * count + p]
            one, two = value + pole * one, pole * (two + one)
            weighted = value * power
            back_one = back_one + weighted
            back_two = back_two + (g * count + p).astype(F32) * weighted
            power = power * pole
        for n, value in enumerate((one, two, back_one, back_two, power)):
            ends[n] = value

    ends[0:4] = jnp.zeros((4, part, lanes), F32)
    ends[4] = jnp.ones((part, lanes), F32)
    lag = 4

    def early(g, _):
        group(g)
        to_mate(g).start()
        relay(g - 1)
        return 0

    def late(g, _):
        settle(g - lag)
        absorb(g - lag)
        group(g)
        to_mate(g).start()
        relay(g - 1)
        return 0

    group(0)
    to_mate(0).start()
    lax.fori_loop(1, lag, early, 0)
    lax.fori_loop(lag, groups, late, 0)
    relay(groups - 1)

    def finish(g, _):
        settle(g)
        absorb(g)
        return 0

    lax.fori_loop(groups - lag, groups, finish, 0)
    pole, level, slope, decay, wrap_one, wrap_two = (tables[n] for n in range(6))
    zero = jnp.zeros((part, lanes), F32)

    def pass_on(way):
        pair = pl.ds(2 * way, 2)
        return [
            pltpu.make_async_remote_copy(
                src_ref=moments.at[slab, pair],
                dst_ref=moments.at[slab, pair],
                send_sem=send_end.at[way, k],
                recv_sem=take_end.at[way, k],
                device_id=other,
                device_id_type=MESH,
            )
            for k, other in enumerate(others)
        ]

    for way in range(2):
        for n in (2 * way, 2 * way + 1):
            moments[slab, n] = encode(ends[n], spare)
        for copy in pass_on(way):
            copy.start()
    for copy in pass_on(0):
        copy.wait()

    def carried(direction, n):
        one, two = zero, zero
        for m in range(slabs, 0, -1):
            other = lax.rem(slab + 2 * slabs - direction * m, slabs)
            one, two = (
                decay * one + decode(moments[other, n], spare),
                decay * (two + rows * one) + decode(moments[other, n + 1], spare),
            )
        return wrap_one * one, wrap_one * two + wrap_two * one

    def forward(i, carry):
        one, two = carry
        two = pole * (two + one)
        one = freq[i] + pole * one
        filtered[i] = level * one + slope * two
        return one, two

    lax.fori_loop(0, rows, forward, carried(1, 0))

    for copy in pass_on(1):
        copy.wait()

    def to_peer(k, g):
        return pltpu.make_async_remote_copy(
            src_ref=going.at[peers[k], g],
            dst_ref=coming.at[here, g],
            send_sem=send_back.at[k, g],
            recv_sem=take_back.at[k, g],
            device_id={"test": peers[k]},
            device_id_type=MESH,
        )

    pair = 2

    pairs = groups // pair

    def unmix(turned_j, carry):
        j = pairs - 1 - turned_j
        one, two = carry
        planes = [None] * (pair * count)
        for i in reversed(range(pair * count)):
            at_i = j * (pair * count) + i
            two = pole * (two + one)
            one = pole * one
            planes[i] = filtered[at_i] + (level * one + slope * two)
            one = one + freq[at_i]
        both = []
        for n in range(pair):
            blocks = swap_blocks(planes[n * count : (n + 1) * count])
            top, low = halves(jnp.concatenate(blocks, axis=0))
            both.append(jnp.concatenate([top, top, low], axis=0))
        mixed = matmul(cas_across[...], jnp.concatenate(both, axis=1))
        for n in range(pair):
            for u in range(count):
                block = mixed[u * part : (u + 1) * part, n * lanes : (n + 1) * lanes]
                going[u, pair * j + n] = encode(block, spare)
        for g in [pair * j + n for n in range(pair)]:
            for k in range(count - 1):
                to_peer(k, g).start()
            coming[here, g] = going[here, g]
        return one, two

    lax.fori_loop(0, pairs, unmix, carried(-1, 2))

    def leave(j):
        span = pl.ds(j * (pair * count), pair * count)
        return pltpu.make_async_copy(ready.at[span], out.at[span], leave_sem.at[j])

    def back(turned_j, _):
        j = pairs - 1 - turned_j
        for g in [pair * j + n for n in range(pair)]:
            for k in range(count - 1):
                to_peer(k, g).wait()
        for g in [pair * j + n for n in range(pair)]:
            planes = [decode(coming[t, g], spare) for t in range(count)]
            for p, plane in enumerate(swap_blocks(planes)):
                double = matmul(jnp.concatenate(halves(plane), axis=1), cas_depth[...])
                ready[g * count + p] = double[:, :lanes] + double[:, lanes:]
        leave(j).start()
        return 0

    def left(j, _):
        leave(j).wait()
        return 0

    lax.fori_loop(0, pairs, back, 0)
    lax.fori_loop(0, pairs, left, 0)


def table(length):
    indices = np.arange(length)
    angles = (indices[:, None] * indices[None, :] % length) * (2.0 * np.pi / length)
    return (np.cos(angles) + np.sin(angles)).astype(np.float32)


def split(values):
    top = values.astype(jnp.bfloat16)
    return top, (values - top.astype(np.float32)).astype(jnp.bfloat16)


def doubled_table(values):
    top, low = split(values)
    return np.block([[top, low], [top, np.zeros_like(low)]])


def turned_tables(length, count):
    tables = []
    for p in range(count):
        tables.append(doubled_table(-0.5 * np.roll(table(length), p * (length // count), axis=1)))
    return np.stack(tables)


def filter_tables(rows, along, width, depth, count):
    def kappa(length):
        return 4.0 * np.sin(np.pi * np.arange(length) / length) ** 2

    part, block = width // count, depth // count
    lanes_at = np.arange(depth)
    across_at = (lanes_at // block)[None, :] * part + np.arange(part)[:, None]
    listed = []
    for here in range(count):
        depth_at = here * block + lanes_at % block
        shift = 1.0 + range_squared * (kappa(width)[across_at] + kappa(depth)[depth_at][None, :])
        centre = 1.0 + shift / (2.0 * range_squared)
        pole = 1.0 / (centre + np.sqrt(centre * centre - 1.0))
        square = pole * pole
        gain = prior_gain / (range_squared * range_squared) * square / (width * depth)
        slope = gain / (1.0 - square) ** 2
        level = slope * (1.0 + square) / (1.0 - square)
        turn = pole**along
        wrap_one = 1.0 / (1.0 - turn)
        wrap_two = along * turn * wrap_one * wrap_one
        listed.append(np.stack([pole, level, slope, pole**rows, wrap_one, wrap_two]))
    return np.stack(listed).astype(np.float32)


def fast(log_k, heads, warm_adjoint, obs_columns, obs_residuals, well_columns):
    rows, width, depth = log_k.shape
    slabs = lax.axis_size("space")
    count = lax.axis_size("test")
    part = width // count
    groups = rows // count
    observed = obs_columns.shape[1]
    planes = rows + 6
    padded = width + 2 * GUARD
    spare = 16 - part % 16
    top, low = split(table(width))
    return pl.pallas_call(
        whole_kernel,
        out_shape=shape(rows, part, depth),
        in_specs=[SM, VM, VM, ANY, ANY, ANY, VM, VM, ANY, VM, VM],
        out_specs=ANY,
        scratch_shapes=[pltpu.VMEM((planes, width, depth), BF)] * 2
        + [
            pltpu.VMEM((2, width, depth), BF),
            pltpu.VMEM((planes, padded, depth), F32),
            pltpu.VMEM((planes, width, depth), F32),
            pltpu.VMEM((planes, width, depth), F32),
            pltpu.VMEM((16, padded, depth), F32),
            pltpu.VMEM((2 * observed, depth), BF),
            pltpu.VMEM((4, 8, depth), F32),
            pltpu.VMEM((slabs, 8, depth), F32),
            pltpu.VMEM((2, RING, 2, width, depth), F32),
            pltpu.VMEM((groups, 2, width, depth), F32),
            pltpu.VMEM((RING, width + 16, depth), jnp.int16),
            pltpu.VMEM((groups, width + 16, depth), jnp.int16),
            pltpu.SemaphoreType.DMA((2, 4)),
        ]
        + [pltpu.SemaphoreType.DMA((2, 3))] * 2
        + [pltpu.SemaphoreType.DMA((slabs - 1,))] * 2
        + [pltpu.SemaphoreType.DMA((groups,))] * 4
        + [
            pltpu.VMEM((6, part, depth), F32),
            pltpu.VMEM((rows, part, depth), F32),
            pltpu.VMEM((slabs, 4, part + spare, depth), jnp.int16),
            pltpu.VMEM((count, groups, part + spare, depth), jnp.int16),
            pltpu.VMEM((count, groups, part + spare, depth), jnp.int16),
            pltpu.SemaphoreType.DMA,
        ]
        + [pltpu.SemaphoreType.DMA((2, slabs - 1))] * 2
        + [pltpu.SemaphoreType.DMA((count - 1, groups))] * 2
        + [
            pltpu.VMEM((5, part, depth), F32),
            pltpu.VMEM((rows, part, depth), F32),
            pltpu.SemaphoreType.DMA((groups // 2,)),
        ],
        compiler_params=pltpu.CompilerParams(
            vmem_limit_bytes=60 * 1024 * 1024, collective_id=1, has_side_effects=True
        ),
        name="whole",
    )(
        well_columns,
        obs_columns,
        obs_residuals[0],
        log_k,
        warm_adjoint[0],
        heads[0],
        jnp.asarray(turned_tables(depth, count)),
        jnp.asarray(np.tile(np.eye(depth, k=1) + np.eye(depth, k=-1), (2, 1)), BF),
        jnp.asarray(filter_tables(rows, rows * slabs, width, depth, count)),
        jnp.asarray(np.concatenate([top, low, top], axis=1)),
        jnp.asarray(doubled_table(table(depth))),
    )


def pick(log_k, heads, warm_adjoint, obs_columns, *rest):
    rows, width, depth = log_k.shape
    count = lax.axis_size("test")
    fits = depth == 128 and count == 4 and rows % 8 == 0 and rows >= 16 and width % 96 == 0
    fits = fits and obs_columns.shape[1] % 64 == 0 and rows * width <= 48 * 288
    run = fast if fits and lax.axis_size("space") > 1 else on_device
    return run(log_k, heads, warm_adjoint, obs_columns, *rest)


def solution(mesh):
    placed = (
        P(("groups", "space"), None, None),
        P("test", ("groups", "space"), None, None),
        P("test", ("groups", "space"), None, None),
        P("test", "groups"),
        P("test", "groups", None),
        P(("groups", "test")),
    )
    return jax.shard_map(
        pick,
        mesh=mesh,
        in_specs=placed,
        out_specs=P(("groups", "space"), "test", None),
        check_vma=False,
    )
```

```python
import jax
import jax.numpy as jnp
import numpy as np
from jax import lax
from jax.experimental import pallas as pl
from jax.experimental.pallas import tpu as pltpu
from jax.sharding import PartitionSpec as P

ITERS = 2


prior_gain = 5.0
range_squared = 4.0


def with_halo(cells, sides, width):
    for axis, dim in sides:
        count = lax.axis_size(axis)
        ends = count - 1
        head = lax.slice_in_dim(cells, 0, width, axis=dim)
        tail = lax.slice_in_dim(cells, cells.shape[dim] - width, cells.shape[dim], axis=dim)
        cells = jnp.concatenate(
            [
                lax.ppermute(tail, axis, [(i, (i + 1) % count) for i in range(ends)]),
                cells,
                lax.ppermute(head, axis, [((i + 1) % count, i) for i in range(ends)]),
            ],
            axis=dim,
        )
    return cells


def neighbours(padded):
    return [
        padded[2:, 1:-1, 1:-1],
        padded[:-2, 1:-1, 1:-1],
        padded[1:-1, 2:, 1:-1],
        padded[1:-1, :-2, 1:-1],
        padded[1:-1, 1:-1, 2:],
        padded[1:-1, 1:-1, :-2],
    ]


def operate(values, padded, conduct):
    summed = jnp.zeros_like(values)
    for face_k, beside in zip(conduct, neighbours(padded)):
        summed = summed + face_k * (values - beside)
    return summed


def kappa_of(indices, length):
    return 4.0 * jnp.sin(jnp.pi * indices / length) ** 2


def pad_sides(padded):
    return jnp.pad(padded, ((0, 0), (1, 1), (1, 1)))


def with_faces(values):
    return pad_sides(with_halo(values, (("space", 0),), 1))


def squares(residual):
    return lax.psum(jnp.sum(residual * residual), "space")


def hartley(length):
    indices = jnp.arange(length, dtype=jnp.int32)
    products = indices[:, None] * indices[None, :] % length
    angles = products.astype(jnp.float32) * (2.0 * jnp.pi / length)
    return jnp.cos(angles) + jnp.sin(angles)


def on_device(log_k, heads, warm_adjoint, obs_columns, obs_residuals, well_columns):
    slab_rows, width_cells, depth_cells = log_k.shape
    space_count = lax.axis_size("space")
    first_row = lax.axis_index("space") * slab_rows
    logk_pad, head_pad = (
        with_halo(log_k, (("space", 0),), 1),
        with_halo(heads[0], (("space", 0),), 1),
    )
    logk_val = log_k.astype(jnp.float32)
    conduct = [
        jnp.exp(0.5 * (logk_val + beside))
        for beside in neighbours(pad_sides(logk_pad.astype(jnp.float32)))
    ]
    columns = obs_columns[0]
    row_local = columns // width_cells - first_row
    inside = (row_local >= 0) & (row_local < slab_rows)
    row_local = jnp.where(inside, row_local, slab_rows)
    source = jnp.zeros((slab_rows, width_cells, depth_cells), jnp.float32)
    source = source.at[row_local, columns % width_cells].add(obs_residuals[0], mode="drop")
    adjoint = warm_adjoint[0].astype(jnp.float32)
    lam_padded = with_faces(adjoint)
    residual = source - operate(adjoint, lam_padded, conduct)
    direction = residual
    norm_now = squares(residual)
    for iteration in range(ITERS):
        dir_padded = with_faces(direction)
        applied = operate(direction, dir_padded, conduct)
        step_length = norm_now / lax.psum(jnp.sum(direction * applied), "space")
        adjoint = adjoint + step_length * direction
        lam_padded = lam_padded + step_length * dir_padded
        if iteration + 1 < ITERS:
            residual = residual - step_length * applied
            norm_next = squares(residual)
            direction = residual + norm_next / norm_now * direction
            norm_now = norm_next
    lam_full = pad_sides(with_halo(adjoint, (("space", 0),), 1))
    head_val = heads[0].astype(jnp.float32)
    misfit_term = jnp.zeros_like(adjoint)
    for face_k, lam_side, head_side in zip(
        conduct, neighbours(lam_full), neighbours(pad_sides(head_pad.astype(jnp.float32)))
    ):
        misfit_term = misfit_term + face_k * (adjoint - lam_side) * (head_val - head_side)
    column_ids = (first_row + jnp.arange(slab_rows, dtype=jnp.int32))[
        :, None
    ] * width_cells + jnp.arange(width_cells, dtype=jnp.int32)[None, :]
    keep_mask = (column_ids != well_columns[0]).astype(jnp.float32)
    partial_value = -0.5 * misfit_term * keep_mask[:, :, None]
    highest = lax.Precision.HIGHEST
    cas_depth = hartley(depth_cells)
    cas_across = hartley(width_cells)
    along_cells = slab_rows * space_count
    cas_along = hartley(along_cells)
    summed = lax.psum_scatter(partial_value, "test", scatter_dimension=1, tiled=True)
    depth_freq = jnp.einsum("xyz,zk->xky", summed, cas_depth, precision=highest)
    pencil = lax.all_to_all(depth_freq, "test", split_axis=1, concat_axis=2, tiled=True)
    across_freq = jnp.einsum("xzy,yk->kzx", pencil, cas_across, precision=highest)
    column_block = lax.all_to_all(across_freq, "space", split_axis=0, concat_axis=2, tiled=True)
    along_freq = jnp.einsum("yzx,xk->yzk", column_block, cas_along, precision=highest)
    across_rows = column_block.shape[0]
    depth_rows = column_block.shape[1]
    kappa_x = kappa_of(jnp.arange(along_cells).astype(jnp.float32), along_cells)
    kappa_y = kappa_of(
        (lax.axis_index("space") * across_rows + jnp.arange(across_rows)).astype(jnp.float32),
        width_cells,
    )
    kappa_z = kappa_of(
        (lax.axis_index("test") * depth_rows + jnp.arange(depth_rows)).astype(jnp.float32),
        depth_cells,
    )
    spectrum = (
        prior_gain
        / (
            1.0
            + range_squared
            * (kappa_y[:, None, None] + kappa_z[None, :, None] + kappa_x[None, None, :])
        )
        ** 2
    )
    along_back = jnp.einsum("yzk,kx->yzx", along_freq * spectrum, cas_along, precision=highest)
    slab_block = lax.all_to_all(along_back, "space", split_axis=2, concat_axis=0, tiled=True)
    across_back = jnp.einsum("yzx,yk->xzk", slab_block, cas_across, precision=highest)
    depth_block = lax.all_to_all(across_back, "test", split_axis=2, concat_axis=1, tiled=True)
    result = jnp.einsum("xky,kz->xyz", depth_block, cas_depth, precision=highest)
    scale_back = 1.0 / (along_cells * width_cells * depth_cells)
    return result * scale_back


GUARD = 8
RING = 6
STEP = 256.0
TOP = 32000.0
HALF_LOG = 0.5 / float(np.log(2.0))
BF = jnp.bfloat16
F32 = jnp.float32
VM = pl.BlockSpec(memory_space=pltpu.VMEM)
SM = pl.BlockSpec(memory_space=pltpu.SMEM)
ANY = pl.BlockSpec(memory_space=pl.ANY)
MESH = pl.DeviceIdType.MESH


def shape(*dims, dtype=jnp.float32):
    return jax.ShapeDtypeStruct(dims, dtype)


def iota(plane, axis):
    return lax.broadcasted_iota(jnp.int32, plane, axis)


def halves(values):
    top = values.astype(BF)
    return top, (values - top.astype(F32)).astype(BF)


def matmul(a, b):
    return jnp.dot(a, b, preferred_element_type=F32)


def encode(values, spare):
    rows, lanes = values.shape
    peak = jnp.maximum(jnp.max(jnp.abs(values), axis=0, keepdims=True), 1e-30)
    level = jnp.ceil(jnp.log2(peak) * STEP)
    scaled = jnp.round(values * (jnp.exp2(level * (-1.0 / STEP)) * TOP))
    both = jnp.concatenate([scaled, jnp.broadcast_to(level, (spare, lanes))], axis=0)
    return both.astype(jnp.int32).astype(jnp.int16)


def decode(codes, spare):
    wide = codes.astype(jnp.int32).astype(F32)
    rows = wide.shape[0] - spare
    level = wide[rows : rows + 1]
    return wide[:rows] * (jnp.exp2(level * (1.0 / STEP)) * (1.0 / TOP))


def swap_blocks(planes):
    planes = list(planes)
    count = len(planes)
    lanes = planes[0].shape[1]
    block = lanes // count
    at_block = iota(planes[0].shape, 1) // block
    span = 1
    while span < count:
        odd = (at_block // span) % 2 == 1
        for low in range(count):
            if (low // span) % 2 == 0:
                first, second = planes[low], planes[low + span]
                up = pltpu.roll(second, block * span, 1)
                down = pltpu.roll(first, lanes - block * span, 1)
                planes[low] = jnp.where(odd, up, first)
                planes[low + span] = jnp.where(odd, second, down)
        span *= 2
    return planes


def greet(others):
    barrier = pltpu.get_barrier_semaphore()
    for other in others:
        pl.semaphore_signal(barrier, inc=1, device_id=other, device_id_type=MESH)
    pl.semaphore_wait(barrier, len(others))


def whole_kernel(
    well,
    columns,
    observed,
    logk,
    warm,
    heads,
    turned,
    beside_lanes,
    listed,
    cas_across,
    cas_depth,
    out,
    lk,
    wm,
    level_ends,
    soft,
    res,
    img,
    ring,
    sources,
    acc,
    shared,
    mine,
    from_mate,
    ship,
    got,
    load_sem,
    halo_send,
    halo_take,
    send_sum,
    take_sum,
    send_mate,
    take_mate,
    send_across,
    take_across,
    tables,
    freq,
    moments,
    going,
    coming,
    table_sem,
    send_end,
    take_end,
    send_back,
    take_back,
    ends,
    ready,
    leave_sem,
):
    rows, width, depth = logk.shape
    parts = 4
    chunk = rows // parts
    piece = width // 6
    pieces = range(6)
    slabs = shared.shape[0]
    slab, here = lax.axis_index("space"), lax.axis_index("test")
    half, core = here // 2, lax.rem(here, 2)
    mate = {"test": 2 * half + 1 - core}
    across = {"test": 2 * (1 - half) + core}
    others = [{"space": lax.rem(slab + k, slabs)} for k in range(1, slabs)]
    first_row = slab * rows

    def loads(m):
        span = pl.ds(m * chunk, chunk)
        to = pl.ds(3 + m * chunk, chunk)
        return [
            pltpu.make_async_copy(frm.at[span], held.at[to], load_sem.at[n, m])
            for n, (frm, held) in enumerate(((logk, lk), (warm, wm)))
        ]

    for m in range(parts):
        for copy in loads(m):
            copy.start()

    def halo(direction):
        up = direction == 1
        copies = []
        for n, (frm, held, deep) in enumerate(((logk, lk, 3), (warm, wm, 3), (heads, level_ends, 1))):
            at = rows - deep if up else 0
            to = 3 - deep if up else 3 + rows
            if deep == 1:
                to = 0 if up else 1
            copies.append(
                pltpu.make_async_remote_copy(
                    src_ref=frm.at[pl.ds(at, deep)],
                    dst_ref=held.at[pl.ds(to, deep)],
                    send_sem=halo_send.at[direction, n],
                    recv_sem=halo_take.at[direction, n],
                    device_id={"space": slab + 1 if up else slab - 1},
                    device_id_type=MESH,
                )
            )
        return copies

    count = 4
    peers = [lax.rem(here + k, count) for k in range(1, count)]
    fetch = pltpu.make_async_copy(listed.at[here], tables, table_sem)
    fetch.start()
    greet(others + [{"test": peer} for peer in peers])

    @pl.when(slab > 0)
    def _():
        for copy in halo(0):
            copy.start()

    @pl.when(slab < slabs - 1)
    def _():
        for copy in halo(1):
            copy.start()

    blank = jnp.zeros((3, width, depth), BF)

    @pl.when(slab == 0)
    def _():
        lk[0:3] = blank
        wm[0:3] = blank
        level_ends[0] = blank[0]

    @pl.when(slab == slabs - 1)
    def _():
        lk[rows + 3 : rows + 6] = blank
        wm[rows + 3 : rows + 6] = blank
        level_ends[1] = blank[0]

    top, low = halves(observed[...])
    sources[...] = jnp.concatenate([top, low], axis=0)
    acc[...] = jnp.zeros_like(acc)
    edge = jnp.zeros((GUARD, depth), F32)
    for i in range(ring.shape[0]):
        ring[i, 0:GUARD, :] = edge
        ring[i, width + GUARD : width + 2 * GUARD, :] = edge

    at_lane = iota((piece, depth), 1)
    at_row = iota((piece, depth), 0)
    is_first, is_last = at_lane == 0, at_lane == depth - 1
    spots = iota((width, 2 * columns.shape[1]), 0)

    def at(c):
        return pl.ds(c * piece, piece)

    def near(ref, i, c, off=0):
        return ref[i, pl.ds(GUARD + c * piece + off, piece), :]

    def store(ref, i, c, value):
        ref[i, pl.ds(GUARD + c * piece, piece), :] = value

    def ahead(value):
        return pltpu.roll(value, depth - 1, 1)

    def behind(value):
        return pltpu.roll(value, 1, 1)

    def ring_sum(held, ends, sides, outer):
        lanes = jnp.where(is_last, outer, ahead(held)) + jnp.where(is_first, outer, behind(held))
        return (lanes + ends) + sides

    def beside(ref, below, i, above, c, outer):
        held = near(ref, i, c)
        ends = near(ref, i, c, -1) + near(ref, i, c, 1)
        return held, ring_sum(held, ends, near(ref, below, c) + near(ref, above, c), outer)

    def around_slot(n, base, c):
        return beside(ring, base + (n - 1) % 4, base + n % 4, base + (n + 1) % 4, c, 0.0)

    def partial(value):
        return jnp.sum(value.reshape(piece // 8, 8, depth), axis=0)

    def clear(n, store_zero):
        if n < 3:
            pl.when(slab == 0)(store_zero)
        if n >= rows + 3:
            pl.when(slab == slabs - 1)(store_zero)

    blank_piece = jnp.zeros((piece, depth), F32)

    def prepare(at_row_base, views, n, static):
        soft_v, _, _, lk_v, wm_v = views
        one = jnp.ones((GUARD, depth), F32)
        soft_v[n, 0:GUARD, :] = one
        soft_v[n, width + GUARD : width + 2 * GUARD, :] = one
        for c in pieces:
            value = jnp.exp2(HALF_LOG * lk_v[n, at(c), :].astype(F32))
            store(soft_v, n, c, value)
            store(ring, n % 4, c, value * wm_v[n, at(c), :].astype(F32))

    def residual(at_row_base, views, n, static):
        soft_v, res_v = views[:2]
        spot = spots_at - (first_row + at_row_base + n - 3) * width
        hits = jnp.where(spots == spot, 1.0, 0.0).astype(BF)
        source = matmul(hits, sources[...])
        for c in pieces:
            s, around = beside(soft_v, n - 1, n, n + 1, c, 1.0)
            held, total = around_slot(n, 0, c)
            value = (s * total - held * around) + source[c * piece : (c + 1) * piece]
            res_v[n, at(c), :] = value
            store(ring, 4 + n % 4, c, s * value)
            store(ring, 12 + n % 4, c, around)

        def store_zero():
            for c in pieces:
                res_v[n, at(c), :] = blank_piece
                store(ring, 4 + n % 4, c, blank_piece)

        if static:
            clear(n, store_zero)

    def image(at_row_base, views, n, static, sums):
        soft_v, res_v, img_v = views[:3]
        plane = ring[4 + n % 4, pl.ds(GUARD, width), :]
        lanes = matmul(jnp.concatenate(halves(plane), axis=1), beside_lanes[...])
        for c in pieces:
            held = near(ring, 4 + n % 4, c)
            ends = near(ring, 4 + n % 4, c, -1) + near(ring, 4 + n % 4, c, 1)
            sides = near(ring, 4 + (n - 1) % 4, c) + near(ring, 4 + (n + 1) % 4, c)
            total = (lanes[c * piece : (c + 1) * piece] + ends) + sides
            s, value = near(soft_v, n, c), res_v[n, at(c), :]
            applied = held * near(ring, 12 + n % 4, c) - s * total
            img_v[n, at(c), :] = applied
            store(ring, 8 + n % 4, c, s * applied)
            if sums is not None:
                sums[0].append(partial(value * value))
                sums[1].append(partial(value * applied))

        def store_zero():
            for c in pieces:
                img_v[n, at(c), :] = blank_piece
                store(ring, 8 + n % 4, c, blank_piece)

        if static:
            clear(n, store_zero)

    def twice(at_row_base, views, n, sums):
        img_v = views[2]
        for c in pieces:
            held, value = near(ring, 8 + n % 4, c), img_v[n, at(c), :]
            after = near(ring, 8 + (n + 1) % 4, c) + near(ring, 8 + n % 4, c, 1)
            after = after + jnp.where(is_last, 0.0, ahead(held))
            sums[2].append(partial(value * value))
            sums[3].append(partial(held * (value * near(ring, 12 + n % 4, c) - 2.0 * after)))

    def keep(sums):
        for n, terms in enumerate(sums):
            if terms:
                acc[n] += sum(terms[1:], terms[0])

    whole = (soft, res, img, lk, wm)

    def walk(first, last, r_rows, q_rows, q_own, t_rows):
        sums = [[], [], [], []]
        for k in range(first, last + 1):
            if k < rows + 6 and k <= r_rows[1] + 1:
                prepare(0, whole, k, True)
            if r_rows[0] <= k - 2 <= r_rows[1]:
                residual(0, whole, k - 2, True)
            if q_rows[0] <= k - 4 <= q_rows[1]:
                own = q_own[0] <= k - 4 <= q_own[1]
                image(0, whole, k - 4, True, sums if own else None)
            if t_rows[0] <= k - 5 <= t_rows[1]:
                twice(0, whole, k - 5, sums)
        keep(sums)

    def steady(j, _):
        base = 4 + 4 * j
        views = [ref.at[pl.ds(base, 11)] for ref in whole]
        sums = [[], [], [], []]
        for u in range(4):
            prepare(base, views, 7 + u, False)
            residual(base, views, 5 + u, False)
            image(base, views, 3 + u, False, sums)
            twice(base, views, 2 + u, sums)
        keep(sums)
        return 0

    spots_at = jnp.concatenate([columns[...], columns[...]], axis=1)
    for copy in loads(0):
        copy.wait()
    last = rows + 2
    walk(3, 10, (4, last + 2), (5, last + 1), (5, last), (6, last))
    for m in range(1, parts):
        for copy in loads(m):
            copy.wait()
    lax.fori_loop(0, (rows - 8) // 4, steady, 0)

    @pl.when(slab < slabs - 1)
    def _():
        for copy in halo(0):
            copy.wait_recv()

    walk(rows + 3, rows + 8, (4, last + 2), (5, last + 1), (5, last), (6, last))

    @pl.when(slab > 0)
    def _():
        for copy in halo(1):
            copy.wait_recv()

    def refill(base, n, values):
        for c in pieces:
            store(ring, base + n % 4, c, near(soft, n, c) * values[n, at(c), :].astype(F32))

    for n in range(3):
        prepare(0, whole, n, True)
    refill(0, 3, wm)
    residual(0, whole, 1, True)
    refill(0, 4, wm)
    residual(0, whole, 2, True)
    residual(0, whole, 3, True)
    refill(4, 4, res)
    for n in (4, 5):
        for c in pieces:
            store(ring, 12 + n % 4, c, beside(soft, n - 1, n, n + 1, c, 1.0)[1])
    sums = [[], [], [], []]
    image(0, whole, 2, True, None)
    image(0, whole, 3, True, sums)
    refill(4, 5, res)
    image(0, whole, 4, True, sums)
    refill(8, 5, img)
    refill(8, 6, img)
    for n in (3, 4, 5):
        twice(0, whole, n, sums)
    keep(sums)

    levels_in = pltpu.make_async_copy(heads, lk.at[pl.ds(3, rows)], load_sem.at[0, 0])
    levels_in.start()
    lk[2] = level_ends[0]
    lk[rows + 3] = level_ends[1]
    rows_of = [jnp.sum(acc[n], axis=0, keepdims=True) for n in range(4)]
    shared[slab] = jnp.concatenate(rows_of + [jnp.zeros((4, depth), F32)], axis=0)
    copies = [
        pltpu.make_async_remote_copy(
            src_ref=shared.at[slab],
            dst_ref=shared.at[slab],
            send_sem=send_sum.at[k],
            recv_sem=take_sum.at[k],
            device_id=other,
            device_id_type=MESH,
        )
        for k, other in enumerate(others)
    ]
    for copy in copies:
        copy.start()

    @pl.when(slab > 0)
    def _():
        for copy in halo(0):
            copy.wait_send()

    @pl.when(slab < slabs - 1)
    def _():
        for copy in halo(1):
            copy.wait_send()

    for copy in copies:
        copy.wait()
    levels_in.wait()
    fetch.wait()

    collected = shared[0]
    for m in range(1, slabs):
        collected = collected + shared[m]

    def gathered(n):
        total = jnp.sum(collected[n : n + 1], axis=1, keepdims=True)
        return jnp.broadcast_to(total, (1, depth))

    norm, curve, square, bend = [gathered(n) for n in range(4)]
    length = norm / curve
    norm_next = length * length * square - norm
    curve_next = curve - 2.0 * length * square + length * length * bend
    ratio = norm_next / norm
    length_next = norm_next / (curve_next - ratio * norm_next / length)
    with_start = length + length_next * (1.0 + ratio)
    with_image = length_next * length

    def eighth(n, base):
        return base + lax.rem(n, 8)

    def fill(n):
        for c in pieces:
            field = wm[n, at(c), :].astype(F32)
            field = field + (with_start * res[n, at(c), :] - with_image * img[n, at(c), :])
            store(ring, eighth(n, 0), c, field)
            store(ring, eighth(n, 8), c, lk[n, at(c), :].astype(F32))

    fill(2)
    fill(3)
    groups = rows // count
    at_block = at_lane // (depth // count)

    def turn(g):
        return lax.rem(g, RING)

    def group(g):
        start = 3 + count * g
        for p in range(count):
            fill(start + p + 1)
        for c in pieces:
            fields = [near(ring, eighth(start + p, 0), c) for p in range(-1, count + 1)]
            levels = [near(ring, eighth(start + p, 8), c) for p in range(-1, count + 1)]
            steps = [
                (fields[p] - fields[p + 1]) * (levels[p] - levels[p + 1]) for p in range(count + 1)
            ]
            turns = []
            for p in range(count):
                n = start + p
                f, h, s = fields[p + 1], levels[p + 1], near(soft, n, c)
                total = near(soft, n - 1, c) * steps[p] + near(soft, n + 1, c) * steps[p + 1]
                for off in (-1, 1):
                    field = near(ring, eighth(n, 0), c, off)
                    level = near(ring, eighth(n, 8), c, off)
                    total += near(soft, n, c, off) * ((f - field) * (h - level))
                both = f * h
                product = (f - ahead(f)) * (h - ahead(h))
                total += jnp.where(is_last, both, ahead(s) * product)
                total += jnp.where(is_first, both, behind(s * product))
                place = well[0] - (first_row + n - 3) * width - c * piece
                value = jnp.where(at_row != place, s * total, 0.0)
                double = matmul(jnp.concatenate(halves(value), axis=1), turned[p])
                turns.append(double[:, :depth] + double[:, depth:])
            for t in range(count):
                joined = turns[-t % count]
                for b in range(1, count):
                    joined = jnp.where(at_block == b, turns[(b - t) % count], joined)
                mine[t % 2, turn(g), t // 2, at(c), :] = joined

    def to_mate(g):
        return pltpu.make_async_remote_copy(
            src_ref=mine.at[1 - core, turn(g)],
            dst_ref=from_mate.at[g],
            send_sem=send_mate.at[g],
            recv_sem=take_mate.at[g],
            device_id=mate,
            device_id_type=MESH,
        )

    def to_across(g):
        return pltpu.make_async_remote_copy(
            src_ref=ship.at[turn(g)],
            dst_ref=got.at[g],
            send_sem=send_across.at[g],
            recv_sem=take_across.at[g],
            device_id=across,
            device_id_type=MESH,
        )

    def relay(g):
        to_mate(g).wait_recv()
        ship[turn(g)] = encode(mine[core, turn(g), 1 - half] + from_mate[g, 1 - half], 16)
        to_across(g).start()

    part = width // count
    spare = going.shape[2] - part
    lanes = depth
    filtered = res.at[:, pl.ds(0, part)]

    def settle(g):
        to_across(g).wait_recv()
        to_mate(g).wait_send()
        to_across(g).wait_send()

    def absorb(g):
        summed = (mine[core, turn(g), half] + from_mate[g, half]) + decode(got[g], 16)
        top, low = halves(summed)
        mixed = matmul(cas_across[...], jnp.concatenate([top, top, low], axis=0))
        blocks = [mixed[j * part : (j + 1) * part] for j in range(count)]
        for p, plane in enumerate(swap_blocks(blocks)):
            freq[g * count + lax.rem(p - here + count, count)] = plane
        pole = tables[0]
        one, two, back_one, back_two, power = (ends[n] for n in range(5))
        for p in range(count):
            value = freq[g * count + p]
            one, two = value + pole * one, pole * (two + one)
            weighted = value * power
            back_one = back_one + weighted
            back_two = back_two + (g * count + p).astype(F32) * weighted
            power = power * pole
        for n, value in enumerate((one, two, back_one, back_two, power)):
            ends[n] = value

    ends[0:4] = jnp.zeros((4, part, lanes), F32)
    ends[4] = jnp.ones((part, lanes), F32)
    lag = 5

    def early(g, _):
        group(g)
        to_mate(g).start()
        relay(g - 1)
        return 0

    def late(g, _):
        settle(g - lag)
        absorb(g - lag)
        group(g)
        to_mate(g).start()
        relay(g - 1)
        return 0

    group(0)
    to_mate(0).start()
    lax.fori_loop(1, lag, early, 0)
    lax.fori_loop(lag, groups, late, 0)
    relay(groups - 1)

    def finish(g, _):
        settle(g)
        absorb(g)
        return 0

    lax.fori_loop(groups - lag, groups, finish, 0)
    pole, level, slope, decay, wrap_one, wrap_two = (tables[n] for n in range(6))
    zero = jnp.zeros((part, lanes), F32)

    def pass_on(way):
        pair = pl.ds(2 * way, 2)
        return [
            pltpu.make_async_remote_copy(
                src_ref=moments.at[slab, pair],
                dst_ref=moments.at[slab, pair],
                send_sem=send_end.at[way, k],
                recv_sem=take_end.at[way, k],
                device_id=other,
                device_id_type=MESH,
            )
            for k, other in enumerate(others)
        ]

    for way in range(2):
        for n in (2 * way, 2 * way + 1):
            moments[slab, n] = encode(ends[n], spare)
        for copy in pass_on(way):
            copy.start()
    for copy in pass_on(0):
        copy.wait()

    def carried(direction, n):
        one, two = zero, zero
        for m in range(slabs, 0, -1):
            other = lax.rem(slab + 2 * slabs - direction * m, slabs)
            one, two = (
                decay * one + decode(moments[other, n], spare),
                decay * (two + rows * one) + decode(moments[other, n + 1], spare),
            )
        return wrap_one * one, wrap_one * two + wrap_two * one

    def forward(i, carry):
        one, two = carry
        two = pole * (two + one)
        one = freq[i] + pole * one
        filtered[i] = level * one + slope * two
        return one, two

    lax.fori_loop(0, rows, forward, carried(1, 0))

    for copy in pass_on(1):
        copy.wait()

    def to_peer(k, g):
        return pltpu.make_async_remote_copy(
            src_ref=going.at[peers[k], g],
            dst_ref=coming.at[here, g],
            send_sem=send_back.at[k, g],
            recv_sem=take_back.at[k, g],
            device_id={"test": peers[k]},
            device_id_type=MESH,
        )

    pair = 2

    pairs = groups // pair

    def unmix(turned_j, carry):
        j = pairs - 1 - turned_j
        one, two = carry
        planes = [None] * (pair * count)
        for i in reversed(range(pair * count)):
            at_i = j * (pair * count) + i
            two = pole * (two + one)
            one = pole * one
            planes[i] = filtered[at_i] + (level * one + slope * two)
            one = one + freq[at_i]
        both = []
        for n in range(pair):
            blocks = swap_blocks(planes[n * count : (n + 1) * count])
            top, low = halves(jnp.concatenate(blocks, axis=0))
            both.append(jnp.concatenate([top, top, low], axis=0))
        mixed = matmul(cas_across[...], jnp.concatenate(both, axis=1))
        for n in range(pair):
            for u in range(count):
                block = mixed[u * part : (u + 1) * part, n * lanes : (n + 1) * lanes]
                going[u, pair * j + n] = encode(block, spare)
        for g in [pair * j + n for n in range(pair)]:
            for k in range(count - 1):
                to_peer(k, g).start()
            coming[here, g] = going[here, g]
        return one, two

    lax.fori_loop(0, pairs, unmix, carried(-1, 2))

    def leave(j):
        span = pl.ds(j * (pair * count), pair * count)
        return pltpu.make_async_copy(ready.at[span], out.at[span], leave_sem.at[j])

    def back(turned_j, _):
        j = pairs - 1 - turned_j
        for g in [pair * j + n for n in range(pair)]:
            for k in range(count - 1):
                to_peer(k, g).wait()
        for g in [pair * j + n for n in range(pair)]:
            planes = [decode(coming[t, g], spare) for t in range(count)]
            for p, plane in enumerate(swap_blocks(planes)):
                double = matmul(jnp.concatenate(halves(plane), axis=1), cas_depth[...])
                ready[g * count + p] = double[:, :lanes] + double[:, lanes:]
        leave(j).start()
        return 0

    def left(j, _):
        leave(j).wait()
        return 0

    lax.fori_loop(0, pairs, back, 0)
    lax.fori_loop(0, pairs, left, 0)


def table(length):
    indices = np.arange(length)
    angles = (indices[:, None] * indices[None, :] % length) * (2.0 * np.pi / length)
    return (np.cos(angles) + np.sin(angles)).astype(np.float32)


def split(values):
    top = values.astype(jnp.bfloat16)
    return top, (values - top.astype(np.float32)).astype(jnp.bfloat16)


def doubled_table(values):
    top, low = split(values)
    return np.block([[top, low], [top, np.zeros_like(low)]])


def turned_tables(length, count):
    tables = []
    for p in range(count):
        tables.append(doubled_table(-0.5 * np.roll(table(length), p * (length // count), axis=1)))
    return np.stack(tables)


def filter_tables(rows, along, width, depth, count):
    def kappa(length):
        return 4.0 * np.sin(np.pi * np.arange(length) / length) ** 2

    part, block = width // count, depth // count
    lanes_at = np.arange(depth)
    across_at = (lanes_at // block)[None, :] * part + np.arange(part)[:, None]
    listed = []
    for here in range(count):
        depth_at = here * block + lanes_at % block
        shift = 1.0 + range_squared * (kappa(width)[across_at] + kappa(depth)[depth_at][None, :])
        centre = 1.0 + shift / (2.0 * range_squared)
        pole = 1.0 / (centre + np.sqrt(centre * centre - 1.0))
        square = pole * pole
        gain = prior_gain / (range_squared * range_squared) * square / (width * depth)
        slope = gain / (1.0 - square) ** 2
        level = slope * (1.0 + square) / (1.0 - square)
        turn = pole**along
        wrap_one = 1.0 / (1.0 - turn)
        wrap_two = along * turn * wrap_one * wrap_one
        listed.append(np.stack([pole, level, slope, pole**rows, wrap_one, wrap_two]))
    return np.stack(listed).astype(np.float32)


def fast(log_k, heads, warm_adjoint, obs_columns, obs_residuals, well_columns):
    rows, width, depth = log_k.shape
    slabs = lax.axis_size("space")
    count = lax.axis_size("test")
    part = width // count
    groups = rows // count
    observed = obs_columns.shape[1]
    planes = rows + 6
    padded = width + 2 * GUARD
    spare = 16 - part % 16
    top, low = split(table(width))
    return pl.pallas_call(
        whole_kernel,
        out_shape=shape(rows, part, depth),
        in_specs=[SM, VM, VM, ANY, ANY, ANY, VM, VM, ANY, VM, VM],
        out_specs=ANY,
        scratch_shapes=[pltpu.VMEM((planes, width, depth), BF)] * 2
        + [
            pltpu.VMEM((2, width, depth), BF),
            pltpu.VMEM((planes, padded, depth), F32),
            pltpu.VMEM((planes, width, depth), F32),
            pltpu.VMEM((planes, width, depth), F32),
            pltpu.VMEM((16, padded, depth), F32),
            pltpu.VMEM((2 * observed, depth), BF),
            pltpu.VMEM((4, 8, depth), F32),
            pltpu.VMEM((slabs, 8, depth), F32),
            pltpu.VMEM((2, RING, 2, width, depth), F32),
            pltpu.VMEM((groups, 2, width, depth), F32),
            pltpu.VMEM((RING, width + 16, depth), jnp.int16),
            pltpu.VMEM((groups, width + 16, depth), jnp.int16),
            pltpu.SemaphoreType.DMA((2, 4)),
        ]
        + [pltpu.SemaphoreType.DMA((2, 3))] * 2
        + [pltpu.SemaphoreType.DMA((slabs - 1,))] * 2
        + [pltpu.SemaphoreType.DMA((groups,))] * 4
        + [
            pltpu.VMEM((6, part, depth), F32),
            pltpu.VMEM((rows, part, depth), F32),
            pltpu.VMEM((slabs, 4, part + spare, depth), jnp.int16),
            pltpu.VMEM((count, groups, part + spare, depth), jnp.int16),
            pltpu.VMEM((count, groups, part + spare, depth), jnp.int16),
            pltpu.SemaphoreType.DMA,
        ]
        + [pltpu.SemaphoreType.DMA((2, slabs - 1))] * 2
        + [pltpu.SemaphoreType.DMA((count - 1, groups))] * 2
        + [
            pltpu.VMEM((5, part, depth), F32),
            pltpu.VMEM((rows, part, depth), F32),
            pltpu.SemaphoreType.DMA((groups // 2,)),
        ],
        compiler_params=pltpu.CompilerParams(
            vmem_limit_bytes=60 * 1024 * 1024, collective_id=1, has_side_effects=True
        ),
        name="whole",
    )(
        well_columns,
        obs_columns,
        obs_residuals[0],
        log_k,
        warm_adjoint[0],
        heads[0],
        jnp.asarray(turned_tables(depth, count)),
        jnp.asarray(np.tile(np.eye(depth, k=1) + np.eye(depth, k=-1), (2, 1)), BF),
        jnp.asarray(filter_tables(rows, rows * slabs, width, depth, count)),
        jnp.asarray(np.concatenate([top, low, top], axis=1)),
        jnp.asarray(doubled_table(table(depth))),
    )


def pick(log_k, heads, warm_adjoint, obs_columns, *rest):
    rows, width, depth = log_k.shape
    count = lax.axis_size("test")
    fits = depth == 128 and count == 4 and rows % 8 == 0 and rows >= 16 and width % 96 == 0
    fits = fits and obs_columns.shape[1] % 64 == 0 and rows * width <= 48 * 288
    run = fast if fits and lax.axis_size("space") > 1 else on_device
    return run(log_k, heads, warm_adjoint, obs_columns, *rest)


def solution(mesh):
    placed = (
        P(("groups", "space"), None, None),
        P("test", ("groups", "space"), None, None),
        P("test", ("groups", "space"), None, None),
        P("test", "groups"),
        P("test", "groups", None),
        P(("groups", "test")),
    )
    return jax.shard_map(
        pick,
        mesh=mesh,
        in_specs=placed,
        out_specs=P(("groups", "space"), "test", None),
        check_vma=False,
    )
```
